32 devices in a mesh: grp: 4 (over y, x), pair: 8 (over z, core).
Axes of the slice: x: 2, y: 2, z: 4, core: 2. Of those that a mesh axis runs over, the one named last changes fastest.
Arguments:
- amplitudes: bfloat16 [24, 24, 9216], P('pair'), may hold values from -6 to 6
- integrals: bfloat16 [9216, 9216], P('pair', 'grp'), may hold values from -0.0625 to 0.0625
- live_counts: int32 [2], replicated, may hold values from 48 to 96, as said below
Outputs:
- residual: bfloat16 [24, 24, 9216], P('pair', None, 'grp')
The draws below stay inside these ranges and needn't reach their ends.
Inputs may be any that keep to these rules, and one draw needn't show every extreme that they name: `live_counts`: orbital slots at or beyond a count are padding; exactly one of the two counts equals 96.
All inputs are finite; a program needn't handle non-finite values.
Results may differ from the reference program's by a relative error of at most 0.001.
Values may be sent and summed in bfloat16 or wider, within the bound.
A program may use at most 128 MiB of HBM per device.

```python
import jax
import jax.numpy as jnp

VB = 96
NOCC = 24
AB = 9216


def draw_live_counts(key, part):
    key = jax.random.fold_in(key, 7)
    first, second = jax.random.split(key)
    counts = jax.random.randint(first, (2,), VB // 2, VB)
    chosen = jax.random.randint(second, (), 0, 2)
    return jnp.where(jnp.arange(2) == chosen, VB, counts).astype(jnp.int32)


def level_of(key, shape, cuts, low, top_value):
    loudness, own = 1.0, jax.random.fold_in(key, 6)
    for axis_at, blocks in cuts:
        heights = jnp.exp(jax.random.uniform(jax.random.fold_in(own, axis_at), (blocks,), jnp.float32, low / len(cuts), top_value / len(cuts)))
        loudness = loudness * jnp.repeat(heights, shape[axis_at] // blocks).reshape([-1 if axis == axis_at else 1 for axis in range(len(shape))])
    return loudness


def scatter_about(rng, dims, spread, most, shards=(), held_as=jnp.bfloat16):
    drawn = jax.random.normal(rng, dims, jnp.float32) * spread
    if len(shards) > 0:
        drawn = level_of(rng, dims, shards, -0.22, 0.18) * drawn
    return jnp.clip(drawn, min=-most, max=most).astype(held_as)


def setup_inputs(seed: int = 0) -> dict:
    splits = jax.random.split(jax.random.key(seed), 4)
    return {
        "amplitudes": scatter_about(splits[0], (NOCC, NOCC, AB), 1.0, 6.0, ((0, 8),)),
        "integrals": scatter_about(splits[1], (AB, AB), AB ** -0.5, 0.0625, ((0, 8), (1, 4))),
        "live_counts": draw_live_counts(jax.random.fold_in(splits[3], 71), 0),
    }


def reference(amplitudes, integrals, live_counts):
    position = jnp.arange(VB * VB)
    keep_pairs = ((position // VB < live_counts[1]) & (position % VB < live_counts[1])).astype(jnp.bfloat16)
    flat_rows = (amplitudes * keep_pairs).reshape(NOCC * NOCC, VB * VB)
    ladder = jnp.dot(flat_rows, integrals, preferred_element_type=jnp.float32)
    ladder = ladder.reshape(NOCC, NOCC, VB, VB)
    summed = ladder + jnp.transpose(ladder, (1, 0, 3, 2))
    virtual = jnp.arange(VB)
    keep_out = ((virtual[:, None] < live_counts[0]) & (virtual[None, :] < live_counts[0])).astype(jnp.float32)
    return (summed * keep_out).reshape(NOCC, NOCC, VB * VB).astype(jnp.bfloat16)
```

```python
import jax
import jax.numpy as jnp
from jax import lax
from jax.sharding import PartitionSpec as P

VB = 96


def on_device(amplitudes, integrals, live_counts):
    occ_rows, occupied, virt_pairs = amplitudes.shape
    my_pairs, slab_cols = integrals.shape
    tile_size = VB
    slab_lanes = slab_cols // tile_size
    rows = occ_rows * occupied
    flat_rows = lax.all_to_all(
        amplitudes.reshape(rows, virt_pairs), "pair", split_axis=1, concat_axis=0, tiled=True
    )
    position = lax.axis_index("pair") * my_pairs + jnp.arange(my_pairs)
    keep_pairs = (
        (position // tile_size < live_counts[1]) & (position % tile_size < live_counts[1])
    ).astype(jnp.bfloat16)
    partial = jnp.dot(flat_rows * keep_pairs, integrals, preferred_element_type=jnp.float32)
    ladder = lax.psum_scatter(partial, "pair", scatter_dimension=0, tiled=True)
    blocks = ladder.reshape(occ_rows, occupied, slab_lanes, tile_size)
    mirrored = lax.all_to_all(
        lax.all_to_all(blocks, "grp", split_axis=3, concat_axis=2, tiled=True),
        "pair",
        split_axis=1,
        concat_axis=0,
        tiled=True,
    )
    summed = blocks + jnp.transpose(mirrored, (1, 0, 3, 2))
    first_virt = lax.axis_index("grp") * slab_lanes + jnp.arange(slab_lanes)
    second_virt = jnp.arange(tile_size)
    keep_out = (
        (first_virt[:, None] < live_counts[0]) & (second_virt[None, :] < live_counts[0])
    ).astype(jnp.float32)
    return (summed * keep_out).reshape(occ_rows, occupied, slab_cols).astype(jnp.bfloat16)


def solution(mesh):
    return jax.shard_map(
        on_device,
        mesh=mesh,
        in_specs=(P("pair", None, None), P("pair", "grp"), P()),
        out_specs=P("pair", None, "grp"),
        check_vma=False,
    )
```

```python
import functools

import jax
import jax.numpy as jnp
from jax import lax
from jax.experimental import pallas as pl
from jax.experimental.pallas import tpu as pltpu
from jax.sharding import PartitionSpec as P

VB = 96
STEPS = 32767.0
MESH = pl.DeviceIdType.MESH
VMEM_BYTES = 50 * 2**20


def quantize(value):
    peak = jnp.maximum(jnp.max(jnp.abs(value), axis=0, keepdims=True), 1e-33)
    whole = jnp.floor(value * (STEPS / peak) + 0.5).astype(jnp.int32)
    half = value.shape[1] // 2
    stacked = jnp.concatenate([whole[:, :half], whole[:, half:]], axis=0)
    return stacked.astype(jnp.int16), peak


def dequantize(stacked, peak):
    rows = stacked.shape[0] // 2
    wide = stacked.astype(jnp.int32).astype(jnp.float32)
    return jnp.concatenate([wide[:rows], wide[rows:]], axis=1) * (peak * (1.0 / STEPS))


def kernel(
    sizes, live_ref, amp_ref, w_hbm, out_ref,
    w_ref, t_ref, tt_ref, mask_ref, part_ref, cross_ref, send_q, send_s,
    recv_q, recv_s, total_ref, split_ref, turned_ref, mirror_ref,
    w_sem, t_send, t_fwd, t_recv, x_send, x_recv, q_send, s_send, q_recv, s_recv, m_send, m_recv,
):
    grps, pairs, occ_rows, occupied, depth, cols, vb = sizes
    chips = pairs // 2
    rows = occ_rows * occupied
    lanes = cols // vb
    devices = grps * pairs
    g, p = lax.axis_index("grp"), lax.axis_index("pair")
    z, core = p // 2, p % 2
    sibling = 2 * z + 1 - core
    me = g * pairs + p

    barrier = pltpu.get_barrier_semaphore()

    @pl.loop(1, devices)
    def _(step):
        other = lax.rem(me + step, devices)
        pl.semaphore_signal(
            barrier, inc=1, device_id=(other // pairs, lax.rem(other, pairs)), device_id_type=MESH
        )

    w_copy = pltpu.make_async_copy(w_hbm, w_ref, w_sem)
    w_copy.start()
    for c in range(depth // vb):
        alive = jnp.where(p * (depth // vb) + c < live_ref[1], live_ref[1], 0)
        lane = lax.broadcasted_iota(jnp.int32, (8, vb), 1)
        mask_ref[:, c * vb:(c + 1) * vb] = jnp.where(lane < alive, 1.0, 0.0)
    pl.semaphore_wait(barrier, devices - 1)

    def amp_cols(pair):
        return amp_ref.at[:, pl.ds(pl.multiple_of(pair * depth, 128), depth)]

    def t_copy(src, slot, send_sem, to_grp, to_pair):
        return pltpu.make_async_remote_copy(
            src_ref=src, dst_ref=t_ref.at[slot], send_sem=send_sem, recv_sem=t_recv.at[slot],
            device_id=(to_grp, to_pair), device_id_type=MESH,
        )

    near_low = z < chips // 2

    def group_of(step):
        low = jnp.where(step < chips - 1 - z, chips - 1 - step, step - (chips - 1 - z))
        high = jnp.where(step < z, step, chips - 1 - (step - z))
        return jnp.where(step == chips - 1, z, jnp.where(near_low, low, high))

    grp_src, grp_dst = lax.rem(g, 2), g // 2
    sends_t = core == grp_src
    relays_t = core == grp_dst

    def z_copy(step):
        to = 2 * group_of(step) + grp_dst
        return t_copy(amp_cols(to), p, t_send.at[step], g, to)

    own_copy = pltpu.make_async_copy(amp_cols(p), t_ref.at[p], t_recv.at[p])
    sib_copy = t_copy(amp_cols(sibling), p, t_send.at[chips - 1], g, sibling)

    @pl.when(sends_t)
    def _():
        @pl.loop(0, chips - 1)
        def _(step):
            z_copy(step).start()

    own_copy.start()
    sib_copy.start()

    def relay_copy(step, hop):
        slot = 2 * group_of(step) + grp_src
        return t_copy(t_ref.at[slot], slot, t_fwd.at[step, hop - 1], lax.rem(g + hop, grps), p)

    def relay(step):
        @pl.when(relays_t)
        def _():
            slot = 2 * group_of(step) + grp_src
            t_copy(t_ref.at[slot], slot, t_send.at[0], g, p).wait_recv()

            @pl.loop(1, grps)
            def _(hop):
                relay_copy(step, hop).start()

    def cross_copy(group):
        return pltpu.make_async_remote_copy(
            src_ref=part_ref.at[group, pl.ds(pl.multiple_of((1 - core) * rows, 8), rows)],
            dst_ref=cross_ref.at[group], send_sem=x_send.at[group], recv_sem=x_recv.at[group],
            device_id=(g, sibling), device_id_type=MESH,
        )

    def chain_copies(step, group, side):
        to = 2 * (z + 1 - 2 * side) + core
        quanta = pltpu.make_async_remote_copy(
            src_ref=send_q.at[step], dst_ref=recv_q.at[side, group],
            send_sem=q_send.at[step], recv_sem=q_recv.at[side, group],
            device_id=(g, to), device_id_type=MESH,
        )
        scales = pltpu.make_async_remote_copy(
            src_ref=send_s.at[step], dst_ref=recv_s.at[side, group],
            send_sem=s_send.at[step], recv_sem=s_recv.at[side, group],
            device_id=(g, to), device_id_type=MESH,
        )
        return quanta, scales

    def arrived(group, side):
        for copy in chain_copies(0, group, side):
            copy.wait_recv()
        total_ref[:, :cols] += dequantize(recv_q[side, group], recv_s[side, group])

    def own_sum(group):
        cross_copy(group).wait_recv()
        mine = part_ref[group, pl.ds(pl.multiple_of(core * rows, 8), rows), :]
        total_ref[:, :cols] = mine + cross_ref[group]

    relay(0)
    w_copy.wait()
    total_ref[:, cols:] = jnp.zeros((rows, total_ref.shape[1] - cols), jnp.float32)

    @pl.loop(0, chips)
    def _(step):
        group = group_of(step)

        @pl.when(step < chips - 2)
        def _():
            relay(step + 1)

        for c in range(2):
            slot = 2 * group + c
            local = step == chips - 1
            relayed = jnp.logical_and(relays_t, c == grp_src)

            @pl.when(jnp.logical_and(local, c == core))
            def _():
                own_copy.wait()

            @pl.when(jnp.logical_or(
                jnp.logical_and(local, c != core),
                jnp.logical_and(jnp.logical_not(local), jnp.logical_not(relayed)),
            ))
            def _():
                t_copy(t_ref.at[slot], slot, t_send.at[0], g, p).wait_recv()

        both = jnp.concatenate(
            [t_ref[2 * group].astype(jnp.float32), t_ref[2 * group + 1].astype(jnp.float32)], axis=0
        )
        tt_ref[...] = (both * mask_ref[:1, :]).astype(jnp.bfloat16)

        @pl.loop(0, cols // 256)
        def _(tile):
            at = pl.ds(pl.multiple_of(tile * 256, 256), 256)
            part_ref[group, :, at] = jnp.dot(
                tt_ref[...], w_ref[:, at], preferred_element_type=jnp.float32
            )

        cross_copy(group).start()

        @pl.when(step < chips - 1)
        def _():
            own_sum(group)
            side = jnp.where(group > z, 0, 1)
            first = jnp.where(side == 0, z == 0, z == chips - 1)

            @pl.when(jnp.logical_not(first))
            def _():
                arrived(group, side)

            quanta, peak = quantize(total_ref[:, :cols])
            send_q[step] = quanta
            send_s[step] = peak
            for copy in chain_copies(step, group, side):
                copy.start()

    own_sum(z)

    @pl.when(z > 0)
    def _():
        arrived(z, 0)

    @pl.when(z < chips - 1)
    def _():
        arrived(z, 1)

    for a in range(lanes):
        split_ref[pl.ds(a, rows, stride=lanes), :] = total_ref[:, a * vb:a * vb + 128]
    per_occ = occupied * lanes
    per_pair = occ_rows * lanes
    for i in range(occ_rows):
        turned = split_ref[i * per_occ:(i + 1) * per_occ, :].T
        for q in range(pairs):
            turned_ref[q, :, i * per_pair:(i + 1) * per_pair] = (
                turned[:vb, q * per_pair:(q + 1) * per_pair]
            )

    def mirror_copy(step):
        other = lax.rem(me + step, devices)
        to_grp, to_pair = other // pairs, lax.rem(other, pairs)
        return pltpu.make_async_remote_copy(
            src_ref=turned_ref.at[to_pair, pl.ds(pl.multiple_of(to_grp * lanes, 8), lanes)],
            dst_ref=mirror_ref.at[me], send_sem=m_send.at[step], recv_sem=m_recv.at[me],
            device_id=(to_grp, to_pair), device_id_type=MESH,
        )

    @pl.loop(1, devices)
    def _(step):
        mirror_copy(step).start()

    mirror_ref[me] = turned_ref[p, pl.ds(pl.multiple_of(g * lanes, 8), lanes), :]

    @pl.loop(1, devices)
    def _(step):
        other = lax.rem(me + step, devices)
        pltpu.make_async_remote_copy(
            src_ref=mirror_ref.at[other], dst_ref=mirror_ref.at[other], send_sem=m_send.at[step],
            recv_sem=m_recv.at[other], device_id=(g, sibling), device_id_type=MESH,
        ).wait_recv()

    @pl.loop(0, pairs)
    def _(q):
        for i in range(occ_rows):
            for j in range(occ_rows):
                at = pl.ds(pl.multiple_of((j * occupied + q * occ_rows + i) * lanes, 8), lanes)
                off = (i * occ_rows + j) * lanes
                for h in range(grps):
                    split_ref[at, h * lanes:(h + 1) * lanes] += (
                        mirror_ref[h * pairs + q, :, off:off + lanes]
                    )

    lane = lax.broadcasted_iota(jnp.int32, (rows, vb), 1)
    for a in range(lanes):
        alive = jnp.where(g * lanes + a < live_ref[0], live_ref[0], 0)
        total_ref[:, a * vb:(a + 1) * vb] = jnp.where(
            lane < alive, split_ref[pl.ds(a, rows, stride=lanes), :][:, :vb], 0.0
        )
    out_ref[...] = total_ref[:, :cols].astype(jnp.bfloat16)

    sib_copy.wait_send()

    @pl.when(sends_t)
    def _():
        @pl.loop(0, chips - 1)
        def _(step):
            z_copy(step).wait_send()

    @pl.when(relays_t)
    def _():
        @pl.loop(0, chips - 1)
        def _(step):
            @pl.loop(1, grps)
            def _(hop):
                relay_copy(step, hop).wait_send()

    @pl.loop(0, chips)
    def _(group):
        cross_copy(group).wait_send()

    @pl.loop(0, chips - 1)
    def _(step):
        group = group_of(step)
        for copy in chain_copies(step, group, jnp.where(group > z, 0, 1)):
            copy.wait_send()

    @pl.loop(1, devices)
    def _(step):
        mirror_copy(step).wait_send()


def fused(mesh, amplitudes, integrals, live_counts):
    occ_rows, occupied, virt_pairs = amplitudes.shape
    depth, cols = integrals.shape
    grps, pairs = mesh.shape["grp"], mesh.shape["pair"]
    rows, chips, devices = occ_rows * occupied, pairs // 2, grps * pairs
    lanes = cols // VB
    sizes = (grps, pairs, occ_rows, occupied, depth, cols, VB)
    block = -(-occ_rows * occ_rows * lanes // 128) * 128
    f32, bf16, i16 = jnp.float32, jnp.bfloat16, jnp.int16
    dma = pltpu.SemaphoreType.DMA
    out = pl.pallas_call(
        functools.partial(kernel, sizes),
        out_shape=jax.ShapeDtypeStruct((rows, cols), bf16),
        in_specs=[
            pl.BlockSpec(memory_space=pltpu.SMEM),
            pl.BlockSpec(memory_space=pltpu.VMEM),
            pl.BlockSpec(memory_space=pl.ANY),
        ],
        out_specs=pl.BlockSpec(memory_space=pltpu.VMEM),
        scratch_shapes=[
            pltpu.VMEM((depth, cols), bf16),
            pltpu.VMEM((pairs, rows, depth), bf16),
            pltpu.VMEM((2 * rows, depth), bf16),
            pltpu.VMEM((8, depth), f32),
            pltpu.VMEM((chips, 2 * rows, cols), f32),
            pltpu.VMEM((chips, rows, cols), f32),
            pltpu.VMEM((chips - 1, 2 * rows, cols // 2), i16),
            pltpu.VMEM((chips - 1, 1, cols), f32),
            pltpu.VMEM((2, chips, 2 * rows, cols // 2), i16),
            pltpu.VMEM((2, chips, 1, cols), f32),
            pltpu.VMEM((rows, cols + 128), f32),
            pltpu.VMEM((rows * lanes, 128), f32),
            pltpu.VMEM((pairs, VB, block), f32),
            pltpu.VMEM((devices, lanes, block), f32),
            dma(()), dma((chips,)), dma((chips - 1, grps - 1)), dma((pairs,)),
            dma((chips,)), dma((chips,)), dma((chips - 1,)), dma((chips - 1,)),
            dma((2, chips)), dma((2, chips)), dma((devices,)), dma((devices,)),
        ],
        compiler_params=pltpu.CompilerParams(
            collective_id=0, has_side_effects=True, vmem_limit_bytes=VMEM_BYTES
        ),
        cost_estimate=pl.CostEstimate(
            flops=4 * pairs // 2 * rows * depth * cols,
            bytes_accessed=2 * depth * cols, transcendentals=0,
        ),
    )(live_counts, amplitudes.reshape(rows, virt_pairs), integrals)
    return out.reshape(occ_rows, occupied, cols)


def gathered(mesh, amplitudes, integrals, live_counts):
    occ_rows, occupied, virt_pairs = amplitudes.shape
    my_pairs, slab_cols = integrals.shape
    tile_size = VB
    slab_lanes = slab_cols // tile_size
    rows = occ_rows * occupied
    flat_rows = lax.all_to_all(
        amplitudes.reshape(rows, virt_pairs), "pair", split_axis=1, concat_axis=0, tiled=True
    )
    position = lax.axis_index("pair") * my_pairs + jnp.arange(my_pairs)
    keep_pairs = (
        (position // tile_size < live_counts[1]) & (position % tile_size < live_counts[1])
    ).astype(jnp.bfloat16)
    partial = jnp.dot(flat_rows * keep_pairs, integrals, preferred_element_type=jnp.float32)
    ladder = lax.psum_scatter(partial, "pair", scatter_dimension=0, tiled=True)
    blocks = ladder.reshape(occ_rows, occupied, slab_lanes, tile_size)
    mirrored = lax.all_to_all(
        lax.all_to_all(blocks, "grp", split_axis=3, concat_axis=2, tiled=True),
        "pair",
        split_axis=1,
        concat_axis=0,
        tiled=True,
    )
    summed = blocks + jnp.transpose(mirrored, (1, 0, 3, 2))
    first_virt = lax.axis_index("grp") * slab_lanes + jnp.arange(slab_lanes)
    second_virt = jnp.arange(tile_size)
    keep_out = (
        (first_virt[:, None] < live_counts[0]) & (second_virt[None, :] < live_counts[0])
    ).astype(jnp.float32)
    return (summed * keep_out).reshape(occ_rows, occupied, slab_cols).astype(jnp.bfloat16)


def on_device(mesh, amplitudes, integrals, live_counts):
    occ_rows, occupied, virt_pairs = amplitudes.shape
    depth, cols = integrals.shape
    rows, pairs = occ_rows * occupied, mesh.shape["pair"]
    held = 2 * depth * cols + rows * cols * (8 * pairs + 8) + 6 * rows * virt_pairs
    fits = held < VMEM_BYTES and mesh.shape["grp"] == 4
    return (fused if fits else gathered)(mesh, amplitudes, integrals, live_counts)


def solution(mesh):
    return jax.shard_map(
        functools.partial(on_device, mesh),
        mesh=mesh,
        in_specs=(P("pair", None, None), P("pair", "grp"), P()),
        out_specs=P("pair", None, "grp"),
        check_vma=False,
    )
```

```python
import functools
import math

import jax
import jax.numpy as jnp
from jax import lax
from jax.experimental import pallas as pl
from jax.experimental.pallas import tpu as pltpu
from jax.sharding import PartitionSpec as P

VB = 96
STEPS = 32767.0
MESH = pl.DeviceIdType.MESH
VMEM_BYTES = 58 * 2**20


def quantize(value):
    peak = jnp.maximum(jnp.max(jnp.abs(value), axis=0, keepdims=True), 1e-33)
    whole = jnp.floor(value * (STEPS / peak) + 0.5).astype(jnp.int32)
    return whole.astype(jnp.int16), peak


def dequantize(quanta, peak):
    return quanta.astype(jnp.int32).astype(jnp.float32) * (peak * (1.0 / STEPS))


def kernel(
    sizes, live_ref, amp_ref, w_hbm, out_ref,
    w_ref, t_ref, tt_ref, mask_ref, part_ref, cross_ref, send_q, send_s,
    recv_q, recv_s, total_ref, split_ref, half_ref, turned_ref, mirrored_ref, mirror_ref,
    w_sem, t_send, t_fwd, t_recv, x_send, x_recv, q_send, s_send, q_recv, s_recv, m_send, m_recv,
):
    grps, pairs, occ_rows, occupied, depth, cols, vb = sizes
    chips = pairs // 2
    rows = occ_rows * occupied
    lanes = cols // vb
    half_cols, half_lanes = cols // 2, lanes // 2
    devices = grps * pairs
    g, p = lax.axis_index("grp"), lax.axis_index("pair")
    z, core = p // 2, p % 2
    sibling = 2 * z + 1 - core
    me = g * pairs + p

    barrier = pltpu.get_barrier_semaphore()

    @pl.loop(1, devices)
    def _(step):
        other = lax.rem(me + step, devices)
        pl.semaphore_signal(
            barrier, inc=1, device_id=(other // pairs, lax.rem(other, pairs)), device_id_type=MESH
        )

    w_copy = pltpu.make_async_copy(w_hbm, w_ref, w_sem)
    w_copy.start()
    for c in range(depth // vb):
        alive = jnp.where(p * (depth // vb) + c < live_ref[1], live_ref[1], 0)
        lane = lax.broadcasted_iota(jnp.int32, (8, vb), 1)
        mask_ref[:, c * vb:(c + 1) * vb] = jnp.where(lane < alive, 1.0, 0.0)
    pl.semaphore_wait(barrier, devices - 1)

    def amp_cols(pair):
        return amp_ref.at[:, pl.ds(pl.multiple_of(pair * depth, 128), depth)]

    def t_copy(src, slot, send_sem, to_grp, to_pair):
        return pltpu.make_async_remote_copy(
            src_ref=src, dst_ref=t_ref.at[slot], send_sem=send_sem, recv_sem=t_recv.at[slot],
            device_id=(to_grp, to_pair), device_id_type=MESH,
        )

    near_low = z < chips // 2

    def group_of(step):
        low = jnp.where(step < chips - 1 - z, chips - 1 - step, step - (chips - 1 - z))
        high = jnp.where(step < z, step, chips - 1 - (step - z))
        return jnp.where(step == chips - 1, z, jnp.where(near_low, low, high))

    grp_src, grp_dst = lax.rem(g, 2), g // 2
    sends_t = core == grp_src
    relays_t = core == grp_dst

    def z_copy(step):
        to = 2 * group_of(step) + grp_dst
        return t_copy(amp_cols(to), p, t_send.at[step], g, to)

    own_copy = pltpu.make_async_copy(amp_cols(p), t_ref.at[p], t_recv.at[p])
    sib_copy = t_copy(amp_cols(sibling), p, t_send.at[chips - 1], g, sibling)

    @pl.when(sends_t)
    def _():
        @pl.loop(0, chips - 1)
        def _(step):
            z_copy(step).start()

    own_copy.start()
    sib_copy.start()

    def relay_copy(step, hop):
        slot = 2 * group_of(step) + grp_src
        return t_copy(t_ref.at[slot], slot, t_fwd.at[step, hop - 1], lax.rem(g + hop, grps), p)

    def relay(step):
        @pl.when(relays_t)
        def _():
            slot = 2 * group_of(step) + grp_src
            t_copy(t_ref.at[slot], slot, t_send.at[0], g, p).wait_recv()

            @pl.loop(1, grps)
            def _(hop):
                relay_copy(step, hop).start()

    def cross_copy(group):
        return pltpu.make_async_remote_copy(
            src_ref=part_ref.at[group, pl.ds(pl.multiple_of((1 - core) * rows, 8), rows)],
            dst_ref=cross_ref.at[group], send_sem=x_send.at[group], recv_sem=x_recv.at[group],
            device_id=(g, sibling), device_id_type=MESH,
        )

    def chain_copies(half, step, group, side):
        to = 2 * (z + 1 - 2 * side) + core
        quanta = pltpu.make_async_remote_copy(
            src_ref=send_q.at[half, step], dst_ref=recv_q.at[half, side, group],
            send_sem=q_send.at[half, step], recv_sem=q_recv.at[half, side, group],
            device_id=(g, to), device_id_type=MESH,
        )
        scales = pltpu.make_async_remote_copy(
            src_ref=send_s.at[half, step], dst_ref=recv_s.at[half, side, group],
            send_sem=s_send.at[half, step], recv_sem=s_recv.at[half, side, group],
            device_id=(g, to), device_id_type=MESH,
        )
        return quanta, scales

    def arrived(half, group, side):
        for copy in chain_copies(half, 0, group, side):
            copy.wait_recv()
        total_ref[:, :half_cols] += dequantize(recv_q[half, side, group], recv_s[half, side, group])

    def own_sum(half, group):
        if half == 0:
            cross_copy(group).wait_recv()
        at = slice(half * half_cols, (half + 1) * half_cols)
        mine = part_ref[group, pl.ds(pl.multiple_of(core * rows, 8), rows), at]
        total_ref[:, :half_cols] = mine + cross_ref[group, :, at]

    def chain_step(half, step):
        group = group_of(step)
        own_sum(half, group)
        side = jnp.where(group > z, 0, 1)
        first = jnp.where(side == 0, z == 0, z == chips - 1)

        @pl.when(jnp.logical_not(first))
        def _():
            arrived(half, group, side)

        quanta, peak = quantize(total_ref[:, :half_cols])
        send_q[half, step] = quanta
        send_s[half, step] = peak
        for copy in chain_copies(half, step, group, side):
            copy.start()

    def chain_half(half):
        @pl.loop(0, chips - 1)
        def _(step):
            chain_step(half, step)

    per_occ = occupied * half_lanes
    per_pair = occ_rows * half_lanes
    log_step = math.log(2.0) / 256.0

    def mirror_copy(half, step):
        other = lax.rem(me + step, devices)
        to_grp, to_pair = other // pairs, lax.rem(other, pairs)
        return pltpu.make_async_remote_copy(
            src_ref=mirrored_ref.at[half, to_pair, to_grp], dst_ref=mirror_ref.at[half, me],
            send_sem=m_send.at[half, step], recv_sem=m_recv.at[half, me],
            device_id=(to_grp, to_pair), device_id_type=MESH,
        )

    def finish_half(half):
        own_sum(half, z)

        @pl.when(z > 0)
        def _():
            arrived(half, z, 0)

        @pl.when(z < chips - 1)
        def _():
            arrived(half, z, 1)

        for a in range(half_lanes):
            column = total_ref[:, a * vb:a * vb + 128]
            split_ref[pl.ds(half * half_lanes + a, rows, stride=lanes), :] = column
            half_ref[pl.ds(a, rows, stride=half_lanes), :] = column
        for i in range(occ_rows):
            turned = half_ref[i * per_occ:(i + 1) * per_occ, :].T
            for q in range(pairs):
                turned_ref[q, :, i * per_pair:(i + 1) * per_pair] = (
                    turned[:vb, q * per_pair:(q + 1) * per_pair]
                )

        @pl.loop(0, pairs)
        def _(q):
            block = turned_ref[q]
            peak = jnp.maximum(jnp.max(jnp.abs(block), axis=1, keepdims=True), 1e-33)
            level = jnp.floor(jnp.log(peak) * (1.0 / log_step)) + 2.0
            whole = jnp.floor(block * (STEPS * jnp.exp(level * -log_step)) + 0.5)
            lane = lax.broadcasted_iota(jnp.int32, block.shape, 1)
            whole = jnp.where(lane == 127, level, whole).astype(jnp.int32)
            for h in range(grps):
                mirrored_ref[half, q, h] = whole[h * lanes:(h + 1) * lanes].astype(jnp.int16)

        @pl.loop(1, devices)
        def _(step):
            mirror_copy(half, step).start()

        mirror_ref[half, me] = mirrored_ref[half, p, g]

    def take_half(half):
        @pl.loop(1, devices)
        def _(step):
            other = lax.rem(me + step, devices)
            pltpu.make_async_remote_copy(
                src_ref=mirror_ref.at[half, other], dst_ref=mirror_ref.at[half, other],
                send_sem=m_send.at[half, step], recv_sem=m_recv.at[half, other],
                device_id=(g, sibling), device_id_type=MESH,
            ).wait_recv()

        @pl.loop(0, pairs)
        def _(q):
            for h in range(grps):
                block = mirror_ref[half, h * pairs + q].astype(jnp.int32).astype(jnp.float32)
                block = block * (jnp.exp(block[:, 127:] * log_step) * (1.0 / STEPS))
                first = h * lanes + half * half_lanes
                for i in range(occ_rows):
                    for j in range(occ_rows):
                        at = pl.ds(
                            pl.multiple_of((j * occupied + q * occ_rows + i) * lanes, 8), lanes
                        )
                        off = (i * occ_rows + j) * half_lanes
                        split_ref[at, first:first + half_lanes] += block[:, off:off + half_lanes]

    relay(0)
    w_copy.wait()
    total_ref[:, half_cols:] = jnp.zeros((rows, total_ref.shape[1] - half_cols), jnp.float32)
    turned_ref[...] = jnp.zeros(turned_ref.shape, jnp.float32)

    @pl.loop(0, chips)
    def _(step):
        group = group_of(step)

        @pl.when(step < chips - 2)
        def _():
            relay(step + 1)

        for c in range(2):
            slot = 2 * group + c
            local = step == chips - 1
            relayed = jnp.logical_and(relays_t, c == grp_src)

            @pl.when(jnp.logical_and(local, c == core))
            def _():
                own_copy.wait()

            @pl.when(jnp.logical_or(
                jnp.logical_and(local, c != core),
                jnp.logical_and(jnp.logical_not(local), jnp.logical_not(relayed)),
            ))
            def _():
                t_copy(t_ref.at[slot], slot, t_send.at[0], g, p).wait_recv()

        both = jnp.concatenate(
            [t_ref[2 * group].astype(jnp.float32), t_ref[2 * group + 1].astype(jnp.float32)], axis=0
        )
        tt_ref[...] = (both * mask_ref[:1, :]).astype(jnp.bfloat16)

        @pl.loop(0, cols // 256)
        def _(tile):
            at = pl.ds(pl.multiple_of(tile * 256, 256), 256)
            part_ref[group, :, at] = jnp.dot(
                tt_ref[...], w_ref[:, at], preferred_element_type=jnp.float32
            )

        cross_copy(group).start()

        @pl.when(step < chips - 1)
        def _():
            chain_step(0, step)

    at_end = jnp.logical_or(z == 0, z == chips - 1)

    @pl.when(at_end)
    def _():
        chain_half(1)

    finish_half(0)

    @pl.when(jnp.logical_not(at_end))
    def _():
        chain_half(1)

    finish_half(1)
    take_half(0)
    take_half(1)

    lane = lax.broadcasted_iota(jnp.int32, (rows, vb), 1)
    for a in range(lanes):
        alive = jnp.where(g * lanes + a < live_ref[0], live_ref[0], 0)
        cross_ref[0, :, a * vb:(a + 1) * vb] = jnp.where(
            lane < alive, split_ref[pl.ds(a, rows, stride=lanes), :][:, :vb], 0.0
        )
    out_ref[...] = cross_ref[0].astype(jnp.bfloat16)

    sib_copy.wait_send()

    @pl.when(sends_t)
    def _():
        @pl.loop(0, chips - 1)
        def _(step):
            z_copy(step).wait_send()

    @pl.when(relays_t)
    def _():
        @pl.loop(0, chips - 1)
        def _(step):
            @pl.loop(1, grps)
            def _(hop):
                relay_copy(step, hop).wait_send()

    @pl.loop(0, chips)
    def _(group):
        cross_copy(group).wait_send()

    @pl.loop(0, chips - 1)
    def _(step):
        group = group_of(step)
        for half in range(2):
            for copy in chain_copies(half, step, group, jnp.where(group > z, 0, 1)):
                copy.wait_send()

    @pl.loop(1, devices)
    def _(step):
        for half in range(2):
            mirror_copy(half, step).wait_send()


def fused(mesh, amplitudes, integrals, live_counts):
    occ_rows, occupied, virt_pairs = amplitudes.shape
    depth, cols = integrals.shape
    grps, pairs = mesh.shape["grp"], mesh.shape["pair"]
    rows, chips, devices = occ_rows * occupied, pairs // 2, grps * pairs
    lanes = cols // VB
    sizes = (grps, pairs, occ_rows, occupied, depth, cols, VB)
    f32, bf16, i16 = jnp.float32, jnp.bfloat16, jnp.int16
    dma = pltpu.SemaphoreType.DMA
    out = pl.pallas_call(
        functools.partial(kernel, sizes),
        out_shape=jax.ShapeDtypeStruct((rows, cols), bf16),
        in_specs=[
            pl.BlockSpec(memory_space=pltpu.SMEM),
            pl.BlockSpec(memory_space=pl.ANY),
            pl.BlockSpec(memory_space=pl.ANY),
        ],
        out_specs=pl.BlockSpec(memory_space=pltpu.VMEM),
        scratch_shapes=[
            pltpu.VMEM((depth, cols), bf16),
            pltpu.VMEM((pairs, rows, depth), bf16),
            pltpu.VMEM((2 * rows, depth), bf16),
            pltpu.VMEM((8, depth), f32),
            pltpu.VMEM((chips, 2 * rows, cols), f32),
            pltpu.VMEM((chips, rows, cols), f32),
            pltpu.VMEM((2, chips - 1, rows, cols // 2), i16),
            pltpu.VMEM((2, chips - 1, 1, cols // 2), f32),
            pltpu.VMEM((2, 2, chips, rows, cols // 2), i16),
            pltpu.VMEM((2, 2, chips, 1, cols // 2), f32),
            pltpu.VMEM((rows, cols // 2 + 128), f32),
            pltpu.VMEM((rows * lanes, 128), f32),
            pltpu.VMEM((rows * lanes // 2, 128), f32),
            pltpu.VMEM((pairs, VB, 128), f32),
            pltpu.VMEM((2, pairs, grps, lanes, 128), i16),
            pltpu.VMEM((2, devices, lanes, 128), i16),
            dma(()), dma((chips,)), dma((chips - 1, grps - 1)), dma((pairs,)),
            dma((chips,)), dma((chips,)), dma((2, chips - 1)), dma((2, chips - 1)),
            dma((2, 2, chips)), dma((2, 2, chips)), dma((2, devices)), dma((2, devices)),
        ],
        compiler_params=pltpu.CompilerParams(
            collective_id=0, has_side_effects=True, vmem_limit_bytes=VMEM_BYTES
        ),
        cost_estimate=pl.CostEstimate(
            flops=4 * pairs // 2 * rows * depth * cols,
            bytes_accessed=2 * depth * cols, transcendentals=0,
        ),
    )(live_counts, amplitudes.reshape(rows, virt_pairs), integrals)
    return out.reshape(occ_rows, occupied, cols)


def gathered(mesh, amplitudes, integrals, live_counts):
    occ_rows, occupied, virt_pairs = amplitudes.shape
    my_pairs, slab_cols = integrals.shape
    tile_size = VB
    slab_lanes = slab_cols // tile_size
    rows = occ_rows * occupied
    flat_rows = lax.all_to_all(
        amplitudes.reshape(rows, virt_pairs), "pair", split_axis=1, concat_axis=0, tiled=True
    )
    position = lax.axis_index("pair") * my_pairs + jnp.arange(my_pairs)
    keep_pairs = (
        (position // tile_size < live_counts[1]) & (position % tile_size < live_counts[1])
    ).astype(jnp.bfloat16)
    partial = jnp.dot(flat_rows * keep_pairs, integrals, preferred_element_type=jnp.float32)
    ladder = lax.psum_scatter(partial, "pair", scatter_dimension=0, tiled=True)
    blocks = ladder.reshape(occ_rows, occupied, slab_lanes, tile_size)
    mirrored = lax.all_to_all(
        lax.all_to_all(blocks, "grp", split_axis=3, concat_axis=2, tiled=True),
        "pair",
        split_axis=1,
        concat_axis=0,
        tiled=True,
    )
    summed = blocks + jnp.transpose(mirrored, (1, 0, 3, 2))
    first_virt = lax.axis_index("grp") * slab_lanes + jnp.arange(slab_lanes)
    second_virt = jnp.arange(tile_size)
    keep_out = (
        (first_virt[:, None] < live_counts[0]) & (second_virt[None, :] < live_counts[0])
    ).astype(jnp.float32)
    return (summed * keep_out).reshape(occ_rows, occupied, slab_cols).astype(jnp.bfloat16)


def on_device(mesh, amplitudes, integrals, live_counts):
    occ_rows, occupied, virt_pairs = amplitudes.shape
    depth, cols = integrals.shape
    rows, pairs = occ_rows * occupied, mesh.shape["pair"]
    held = 2 * depth * cols + rows * cols * (8 * pairs + 8) + 6 * rows * virt_pairs
    block = occ_rows * occ_rows * cols // VB // 2
    fits = held < VMEM_BYTES and mesh.shape["grp"] == 4 and block < 128
    return (fused if fits else gathered)(mesh, amplitudes, integrals, live_counts)


def solution(mesh):
    return jax.shard_map(
        functools.partial(on_device, mesh),
        mesh=mesh,
        in_specs=(P("pair", None, None), P("pair", "grp"), P()),
        out_specs=P("pair", None, "grp"),
        check_vma=False,
    )
```

```python
import functools
import math

import jax
import jax.numpy as jnp
from jax import lax
from jax.experimental import pallas as pl
from jax.experimental.pallas import tpu as pltpu
from jax.sharding import PartitionSpec as P

VB = 96
STEPS = 32767.0
MESH = pl.DeviceIdType.MESH
VMEM_BYTES = 58 * 2**20


def quantize(value):
    peak = jnp.maximum(jnp.max(jnp.abs(value), axis=0, keepdims=True), 1e-33)
    whole = jnp.floor(value * (STEPS / peak) + 0.5).astype(jnp.int32)
    return whole.astype(jnp.int16), peak


def dequantize(quanta, peak):
    return quanta.astype(jnp.int32).astype(jnp.float32) * (peak * (1.0 / STEPS))


def kernel(
    sizes, live_ref, amp_ref, w_hbm, out_ref,
    w_ref, t_ref, tt_ref, mask_ref, part_ref, cross_ref, send_q, send_s,
    recv_q, recv_s, total_ref, final_ref, split_ref, piece_ref, mirrored_ref, mirror_ref,
    w_sem, t_send, t_fwd, t_recv, x_send, x_recv, q_send, s_send, q_recv, s_recv, m_send, m_recv,
):
    grps, pairs, occ_rows, occupied, depth, cols, vb = sizes
    chips = pairs // 2
    rows = occ_rows * occupied
    lanes = cols // vb
    chunks, slots = lanes // 8, 127 // lanes
    width = cols // chunks
    devices = grps * pairs
    g, p = lax.axis_index("grp"), lax.axis_index("pair")
    z, core = p // 2, p % 2
    sibling = 2 * z + 1 - core
    me = g * pairs + p

    barrier = pltpu.get_barrier_semaphore()

    @pl.loop(1, devices)
    def _(step):
        other = lax.rem(me + step, devices)
        pl.semaphore_signal(
            barrier, inc=1, device_id=(other // pairs, lax.rem(other, pairs)), device_id_type=MESH
        )

    w_copy = pltpu.make_async_copy(w_hbm, w_ref, w_sem)
    w_copy.start()
    for c in range(depth // vb):
        alive = jnp.where(p * (depth // vb) + c < live_ref[1], live_ref[1], 0)
        lane = lax.broadcasted_iota(jnp.int32, (8, vb), 1)
        mask_ref[:, c * vb:(c + 1) * vb] = jnp.where(lane < alive, 1.0, 0.0)
    pl.semaphore_wait(barrier, devices - 1)

    def amp_cols(pair):
        return amp_ref.at[:, pl.ds(pl.multiple_of(pair * depth, 128), depth)]

    def t_copy(src, slot, send_sem, to_grp, to_pair):
        return pltpu.make_async_remote_copy(
            src_ref=src, dst_ref=t_ref.at[slot], send_sem=send_sem, recv_sem=t_recv.at[slot],
            device_id=(to_grp, to_pair), device_id_type=MESH,
        )

    near_low = z < chips // 2

    def group_of(step):
        low = jnp.where(step < chips - 1 - z, chips - 1 - step, step - (chips - 1 - z))
        high = jnp.where(step < z, step, chips - 1 - (step - z))
        return jnp.where(step == chips - 1, z, jnp.where(near_low, low, high))

    grp_src, grp_dst = lax.rem(g, 2), g // 2
    sends_t = core == grp_src
    relays_t = core == grp_dst

    def z_copy(step):
        to = 2 * group_of(step) + grp_dst
        return t_copy(amp_cols(to), p, t_send.at[step], g, to)

    own_copy = pltpu.make_async_copy(amp_cols(p), t_ref.at[p], t_recv.at[p])
    sib_copy = t_copy(amp_cols(sibling), p, t_send.at[chips - 1], g, sibling)

    @pl.when(sends_t)
    def _():
        @pl.loop(0, chips - 1)
        def _(step):
            z_copy(step).start()

    own_copy.start()
    sib_copy.start()

    def relay_copy(step, hop):
        slot = 2 * group_of(step) + grp_src
        return t_copy(t_ref.at[slot], slot, t_fwd.at[step, hop - 1], lax.rem(g + hop, grps), p)

    def relay(step):
        @pl.when(relays_t)
        def _():
            slot = 2 * group_of(step) + grp_src
            t_copy(t_ref.at[slot], slot, t_send.at[0], g, p).wait_recv()

            @pl.loop(1, grps)
            def _(hop):
                relay_copy(step, hop).start()

    def cross_copy(chunk, group):
        return pltpu.make_async_remote_copy(
            src_ref=part_ref.at[
                chunk, group, pl.ds(pl.multiple_of((1 - core) * rows, 8), rows)
            ],
            dst_ref=cross_ref.at[chunk, group], send_sem=x_send.at[chunk, group],
            recv_sem=x_recv.at[chunk, group], device_id=(g, sibling), device_id_type=MESH,
        )

    def chain_copies(chunk, step, group, side):
        to = 2 * (z + 1 - 2 * side) + core
        quanta = pltpu.make_async_remote_copy(
            src_ref=send_q.at[chunk, step], dst_ref=recv_q.at[chunk, side, group],
            send_sem=q_send.at[chunk, step], recv_sem=q_recv.at[chunk, side, group],
            device_id=(g, to), device_id_type=MESH,
        )
        scales = pltpu.make_async_remote_copy(
            src_ref=send_s.at[chunk, step], dst_ref=recv_s.at[chunk, side, group],
            send_sem=s_send.at[chunk, step], recv_sem=s_recv.at[chunk, side, group],
            device_id=(g, to), device_id_type=MESH,
        )
        return quanta, scales

    def arrived(chunk, group, side, acc):
        for copy in chain_copies(chunk, 0, group, side):
            copy.wait_recv()
        acc[:, :width] += dequantize(recv_q[chunk, side, group], recv_s[chunk, side, group])

    def own_sum(chunk, group, acc):
        cross_copy(chunk, group).wait_recv()
        mine = part_ref[chunk, group, pl.ds(pl.multiple_of(core * rows, 8), rows), :]
        acc[:, :width] = mine + cross_ref[chunk, group]

    def chain_step(chunk, step):
        group = group_of(step)
        own_sum(chunk, group, total_ref)
        side = jnp.where(group > z, 0, 1)
        first = jnp.where(side == 0, z == 0, z == chips - 1)

        @pl.when(jnp.logical_not(first))
        def _():
            arrived(chunk, group, side, total_ref)

        quanta, peak = quantize(total_ref[...])
        send_q[chunk, step] = quanta
        send_s[chunk, step] = peak
        for copy in chain_copies(chunk, step, group, side):
            copy.start()

    def chain_chunk(chunk):
        @pl.loop(0, chips - 1)
        def _(step):
            chain_step(chunk, step)

    log_step = math.log(2.0) / 256.0
    occ_pairs = [(i, j) for i in range(occ_rows) for j in range(occ_rows)]

    def mirror_copy(chunk, step):
        other = lax.rem(me + step, devices)
        to_grp, to_pair = other // pairs, lax.rem(other, pairs)
        return pltpu.make_async_remote_copy(
            src_ref=mirrored_ref.at[chunk, to_pair, to_grp], dst_ref=mirror_ref.at[chunk, me],
            send_sem=m_send.at[chunk, step], recv_sem=m_recv.at[chunk, me],
            device_id=(to_grp, to_pair), device_id_type=MESH,
        )

    def finish_chunk(chunk):
        acc = final_ref.at[chunk]
        own_sum(chunk, z, acc)

        @pl.when(z > 0)
        def _():
            arrived(chunk, z, 0, acc)

        @pl.when(z < chips - 1)
        def _():
            arrived(chunk, z, 1, acc)

        for a in range(8):
            piece_ref[pl.ds(a, rows, stride=8), :] = final_ref[chunk, :, a * vb:a * vb + 128]

        @pl.loop(0, pairs)
        def _(q):
            lane = lax.broadcasted_iota(jnp.int32, (16, 128), 1)
            pieces = [
                piece_ref[
                    pl.ds(pl.multiple_of((i * occupied + q * occ_rows + j) * 8, 8), 8), :
                ]
                for i, j in occ_pairs
            ]
            for h in range(grps):
                ends = []
                for part in (pieces[:slots], pieces[slots:]):
                    packed = jnp.zeros((8, 128), jnp.float32)
                    for at, piece in enumerate(part):
                        shift = ((at - h) * lanes) % 128
                        moved = pltpu.roll(piece, shift, 1) if shift else piece
                        inside = jnp.logical_and(
                            lane[:8] >= at * lanes, lane[:8] < (at + 1) * lanes
                        )
                        packed = jnp.where(inside, moved, packed)
                    ends.append(packed)
                block = jnp.concatenate(ends, axis=0)
                peak = jnp.maximum(jnp.max(jnp.abs(block), axis=1, keepdims=True), 1e-33)
                level = jnp.floor(jnp.log(peak) * (1.0 / log_step)) + 2.0
                whole = jnp.floor(block * (STEPS * jnp.exp(level * -log_step)) + 0.5)
                whole = jnp.where(lane == 127, level, whole).astype(jnp.int32)
                mirrored_ref[chunk, q, h] = whole.astype(jnp.int16)

        @pl.loop(1, devices)
        def _(step):
            mirror_copy(chunk, step).start()

        mirror_ref[chunk, me] = mirrored_ref[chunk, p, g]

    def take_all():
        for chunk in range(chunks):
            @pl.loop(1, devices)
            def _(step):
                other = lax.rem(me + step, devices)
                pltpu.make_async_remote_copy(
                    src_ref=mirror_ref.at[chunk, other], dst_ref=mirror_ref.at[chunk, other],
                    send_sem=m_send.at[chunk, step], recv_sem=m_recv.at[chunk, other],
                    device_id=(g, sibling), device_id_type=MESH,
                ).wait_recv()

        @pl.loop(0, pairs)
        def _(q):
            blocks = []
            for h in range(grps):
                for chunk in range(chunks):
                    block = mirror_ref[chunk, h * pairs + q].astype(jnp.int32).astype(jnp.float32)
                    blocks.append(block * (jnp.exp(block[:, 127:] * log_step) * (1.0 / STEPS)))
            rest = [jnp.zeros((128 - vb, 128), jnp.float32)]
            for end in range(2):
                turned = jnp.concatenate([b[8 * end:8 * end + 8] for b in blocks] + rest, axis=0).T
                for at, (i, j) in enumerate(occ_pairs[end * slots:(end + 1) * slots]):
                    row = (j * occupied + q * occ_rows + i) * lanes
                    split_ref[pl.ds(pl.multiple_of(row, 8), lanes), :] = (
                        turned[at * lanes:(at + 1) * lanes]
                    )

    relay(0)
    w_copy.wait()
    for chunk in range(chunks):
        final_ref[chunk, :, width:] = jnp.zeros((rows, 128), jnp.float32)

    @pl.loop(0, chips)
    def _(step):
        group = group_of(step)

        @pl.when(step < chips - 2)
        def _():
            relay(step + 1)

        for c in range(2):
            slot = 2 * group + c
            local = step == chips - 1
            relayed = jnp.logical_and(relays_t, c == grp_src)

            @pl.when(jnp.logical_and(local, c == core))
            def _():
                own_copy.wait()

            @pl.when(jnp.logical_or(
                jnp.logical_and(local, c != core),
                jnp.logical_and(jnp.logical_not(local), jnp.logical_not(relayed)),
            ))
            def _():
                t_copy(t_ref.at[slot], slot, t_send.at[0], g, p).wait_recv()

        both = jnp.concatenate(
            [t_ref[2 * group].astype(jnp.float32), t_ref[2 * group + 1].astype(jnp.float32)], axis=0
        )
        tt_ref[...] = (both * mask_ref[:1, :]).astype(jnp.bfloat16)

        for chunk in range(chunks):
            @pl.loop(0, width // 256)
            def _(tile):
                at = pl.ds(pl.multiple_of(chunk * width + tile * 256, 256), 256)
                part_ref[chunk, group, :, pl.ds(pl.multiple_of(tile * 256, 256), 256)] = jnp.dot(
                    tt_ref[...], w_ref[:, at], preferred_element_type=jnp.float32
                )

            cross_copy(chunk, group).start()

        @pl.when(step < chips - 1)
        def _():
            chain_step(0, step)

    at_end = jnp.logical_or(z == 0, z == chips - 1)

    @pl.when(at_end)
    def _():
        for chunk in range(1, chunks):
            chain_chunk(chunk)

    for chunk in range(chunks):
        if chunk > 0:
            @pl.when(jnp.logical_not(at_end))
            def _():
                chain_chunk(chunk)
        finish_chunk(chunk)

    take_all()

    lane = lax.broadcasted_iota(jnp.int32, (rows, vb), 1)
    for chunk in range(chunks):
        for a in range(8):
            v = chunk * 8 + a
            alive = jnp.where(g * lanes + v < live_ref[0], live_ref[0], 0)
            both = (
                final_ref[chunk, :, a * vb:(a + 1) * vb]
                + split_ref[pl.ds(v, rows, stride=lanes), :][:, :vb]
            )
            total_ref[:, a * vb:(a + 1) * vb] = jnp.where(lane < alive, both, 0.0)
        out_ref[:, chunk * width:(chunk + 1) * width] = total_ref[...].astype(jnp.bfloat16)

    sib_copy.wait_send()

    @pl.when(sends_t)
    def _():
        @pl.loop(0, chips - 1)
        def _(step):
            z_copy(step).wait_send()

    @pl.when(relays_t)
    def _():
        @pl.loop(0, chips - 1)
        def _(step):
            @pl.loop(1, grps)
            def _(hop):
                relay_copy(step, hop).wait_send()

    @pl.loop(0, chips)
    def _(group):
        for chunk in range(chunks):
            cross_copy(chunk, group).wait_send()

    @pl.loop(0, chips - 1)
    def _(step):
        group = group_of(step)
        for chunk in range(chunks):
            for copy in chain_copies(chunk, step, group, jnp.where(group > z, 0, 1)):
                copy.wait_send()

    @pl.loop(1, devices)
    def _(step):
        for chunk in range(chunks):
            mirror_copy(chunk, step).wait_send()


def fused(mesh, amplitudes, integrals, live_counts):
    occ_rows, occupied, virt_pairs = amplitudes.shape
    depth, cols = integrals.shape
    grps, pairs = mesh.shape["grp"], mesh.shape["pair"]
    rows, chips, devices = occ_rows * occupied, pairs // 2, grps * pairs
    lanes = cols // VB
    chunks = lanes // 8
    width = cols // chunks
    sizes = (grps, pairs, occ_rows, occupied, depth, cols, VB)
    f32, bf16, i16 = jnp.float32, jnp.bfloat16, jnp.int16
    dma = pltpu.SemaphoreType.DMA
    out = pl.pallas_call(
        functools.partial(kernel, sizes),
        out_shape=jax.ShapeDtypeStruct((rows, cols), bf16),
        in_specs=[
            pl.BlockSpec(memory_space=pltpu.SMEM),
            pl.BlockSpec(memory_space=pl.ANY),
            pl.BlockSpec(memory_space=pl.ANY),
        ],
        out_specs=pl.BlockSpec(memory_space=pltpu.VMEM),
        scratch_shapes=[
            pltpu.VMEM((depth, cols), bf16),
            pltpu.VMEM((pairs, rows, depth), bf16),
            pltpu.VMEM((2 * rows, depth), bf16),
            pltpu.VMEM((8, depth), f32),
            pltpu.VMEM((chunks, chips, 2 * rows, width), f32),
            pltpu.VMEM((chunks, chips, rows, width), f32),
            pltpu.VMEM((chunks, chips - 1, rows, width), i16),
            pltpu.VMEM((chunks, chips - 1, 1, width), f32),
            pltpu.VMEM((chunks, 2, chips, rows, width), i16),
            pltpu.VMEM((chunks, 2, chips, 1, width), f32),
            pltpu.VMEM((rows, width), f32),
            pltpu.VMEM((chunks, rows, width + 128), f32),
            pltpu.VMEM((rows * lanes, 128), f32),
            pltpu.VMEM((rows * 8, 128), f32),
            pltpu.VMEM((chunks, pairs, grps, 16, 128), i16),
            pltpu.VMEM((chunks, devices, 16, 128), i16),
            dma(()), dma((chips,)), dma((chips - 1, grps - 1)), dma((pairs,)),
            dma((chunks, chips)), dma((chunks, chips)),
            dma((chunks, chips - 1)), dma((chunks, chips - 1)),
            dma((chunks, 2, chips)), dma((chunks, 2, chips)),
            dma((chunks, devices)), dma((chunks, devices)),
        ],
        compiler_params=pltpu.CompilerParams(
            collective_id=0, has_side_effects=True, vmem_limit_bytes=VMEM_BYTES
        ),
        cost_estimate=pl.CostEstimate(
            flops=4 * pairs // 2 * rows * depth * cols,
            bytes_accessed=2 * depth * cols, transcendentals=0,
        ),
    )(live_counts, amplitudes.reshape(rows, virt_pairs), integrals)
    return out.reshape(occ_rows, occupied, cols)


def gathered(mesh, amplitudes, integrals, live_counts):
    occ_rows, occupied, virt_pairs = amplitudes.shape
    my_pairs, slab_cols = integrals.shape
    tile_size = VB
    slab_lanes = slab_cols // tile_size
    rows = occ_rows * occupied
    flat_rows = lax.all_to_all(
        amplitudes.reshape(rows, virt_pairs), "pair", split_axis=1, concat_axis=0, tiled=True
    )
    position = lax.axis_index("pair") * my_pairs + jnp.arange(my_pairs)
    keep_pairs = (
        (position // tile_size < live_counts[1]) & (position % tile_size < live_counts[1])
    ).astype(jnp.bfloat16)
    partial = jnp.dot(flat_rows * keep_pairs, integrals, preferred_element_type=jnp.float32)
    ladder = lax.psum_scatter(partial, "pair", scatter_dimension=0, tiled=True)
    blocks = ladder.reshape(occ_rows, occupied, slab_lanes, tile_size)
    mirrored = lax.all_to_all(
        lax.all_to_all(blocks, "grp", split_axis=3, concat_axis=2, tiled=True),
        "pair",
        split_axis=1,
        concat_axis=0,
        tiled=True,
    )
    summed = blocks + jnp.transpose(mirrored, (1, 0, 3, 2))
    first_virt = lax.axis_index("grp") * slab_lanes + jnp.arange(slab_lanes)
    second_virt = jnp.arange(tile_size)
    keep_out = (
        (first_virt[:, None] < live_counts[0]) & (second_virt[None, :] < live_counts[0])
    ).astype(jnp.float32)
    return (summed * keep_out).reshape(occ_rows, occupied, slab_cols).astype(jnp.bfloat16)


def on_device(mesh, amplitudes, integrals, live_counts):
    occ_rows, occupied, virt_pairs = amplitudes.shape
    depth, cols = integrals.shape
    rows, pairs = occ_rows * occupied, mesh.shape["pair"]
    held = 2 * depth * cols + rows * cols * (8 * pairs + 8) + 6 * rows * virt_pairs
    lanes = cols // VB
    packs = lanes % 8 == 0 and occ_rows * occ_rows <= 2 * (127 // lanes)
    fits = held < VMEM_BYTES and mesh.shape["grp"] == 4 and packs
    return (fused if fits else gathered)(mesh, amplitudes, integrals, live_counts)


def solution(mesh):
    return jax.shard_map(
        functools.partial(on_device, mesh),
        mesh=mesh,
        in_specs=(P("pair", None, None), P("pair", "grp"), P()),
        out_specs=P("pair", None, "grp"),
        check_vma=False,
    )
```

```python
import functools
import math

import jax
import jax.numpy as jnp
from jax import lax
from jax.experimental import pallas as pl
from jax.experimental.pallas import tpu as pltpu
from jax.sharding import PartitionSpec as P

VB = 96
STEPS = 32767.0
MESH = pl.DeviceIdType.MESH
VMEM_BYTES = 58 * 2**20


def quantize(value):
    peak = jnp.maximum(jnp.max(jnp.abs(value), axis=0, keepdims=True), 1e-33)
    whole = jnp.floor(value * (STEPS / peak) + 0.5).astype(jnp.int32)
    return whole.astype(jnp.int16), peak


def dequantize(quanta, peak):
    return quanta.astype(jnp.int32).astype(jnp.float32) * (peak * (1.0 / STEPS))


def kernel(
    sizes, live_ref, amp_ref, w_hbm, out_ref,
    w_ref, t_ref, tt_ref, mask_ref, part_ref, cross_ref, send_q, send_s,
    recv_q, recv_s, total_ref, final_ref, split_ref, piece_ref, mirrored_ref, mirror_ref,
    w_sem, t_send, t_fwd, t_recv, x_send, x_recv, q_send, s_send, q_recv, s_recv, m_send, m_recv,
):
    grps, pairs, occ_rows, occupied, depth, cols, vb = sizes
    chips = pairs // 2
    rows = occ_rows * occupied
    lanes = cols // vb
    chunks, slots = lanes // 8, 127 // lanes
    width = cols // chunks
    devices = grps * pairs
    g, p = lax.axis_index("grp"), lax.axis_index("pair")
    z, core = p // 2, p % 2
    sibling = 2 * z + 1 - core
    me = g * pairs + p

    barrier = pltpu.get_barrier_semaphore()

    @pl.loop(1, devices)
    def _(step):
        other = lax.rem(me + step, devices)
        pl.semaphore_signal(
            barrier, inc=1, device_id=(other // pairs, lax.rem(other, pairs)), device_id_type=MESH
        )

    w_copy = pltpu.make_async_copy(w_hbm, w_ref, w_sem)
    w_copy.start()
    for c in range(depth // vb):
        alive = jnp.where(p * (depth // vb) + c < live_ref[1], live_ref[1], 0)
        lane = lax.broadcasted_iota(jnp.int32, (8, vb), 1)
        mask_ref[:, c * vb:(c + 1) * vb] = jnp.where(lane < alive, 1.0, 0.0)
    pl.semaphore_wait(barrier, devices - 1)

    def amp_cols(pair):
        return amp_ref.at[:, pl.ds(pl.multiple_of(pair * depth, 128), depth)]

    def t_copy(src, slot, send_sem, to_grp, to_pair):
        return pltpu.make_async_remote_copy(
            src_ref=src, dst_ref=t_ref.at[slot], send_sem=send_sem, recv_sem=t_recv.at[slot],
            device_id=(to_grp, to_pair), device_id_type=MESH,
        )

    near_low = z < chips // 2

    def group_of(step):
        low = jnp.where(step < chips - 1 - z, chips - 1 - step, step - (chips - 1 - z))
        high = jnp.where(step < z, step, chips - 1 - (step - z))
        return jnp.where(step == chips - 1, z, jnp.where(near_low, low, high))

    grp_src, grp_dst = lax.rem(g, 2), g // 2
    sends_t = core == grp_src
    relays_t = core == grp_dst

    def z_copy(step):
        to = 2 * group_of(step) + grp_dst
        return t_copy(amp_cols(to), p, t_send.at[step], g, to)

    own_copy = pltpu.make_async_copy(amp_cols(p), t_ref.at[p], t_recv.at[p])
    sib_copy = t_copy(amp_cols(sibling), p, t_send.at[chips - 1], g, sibling)

    @pl.when(sends_t)
    def _():
        @pl.loop(0, chips - 1)
        def _(step):
            z_copy(step).start()

    own_copy.start()
    sib_copy.start()

    def relay_copy(step, hop):
        slot = 2 * group_of(step) + grp_src
        return t_copy(t_ref.at[slot], slot, t_fwd.at[step, hop - 1], lax.rem(g + hop, grps), p)

    def relay(step):
        @pl.when(relays_t)
        def _():
            slot = 2 * group_of(step) + grp_src
            t_copy(t_ref.at[slot], slot, t_send.at[0], g, p).wait_recv()

            @pl.loop(1, grps)
            def _(hop):
                relay_copy(step, hop).start()

    def cross_copy(chunk, group):
        return pltpu.make_async_remote_copy(
            src_ref=part_ref.at[
                chunk, group, pl.ds(pl.multiple_of((1 - core) * rows, 8), rows)
            ],
            dst_ref=cross_ref.at[chunk, group], send_sem=x_send.at[chunk, group],
            recv_sem=x_recv.at[chunk, group], device_id=(g, sibling), device_id_type=MESH,
        )

    def chain_copies(chunk, step, group, side):
        to = 2 * (z + 1 - 2 * side) + core
        quanta = pltpu.make_async_remote_copy(
            src_ref=send_q.at[chunk, step], dst_ref=recv_q.at[chunk, side, group],
            send_sem=q_send.at[chunk, step], recv_sem=q_recv.at[chunk, side, group],
            device_id=(g, to), device_id_type=MESH,
        )
        scales = pltpu.make_async_remote_copy(
            src_ref=send_s.at[chunk, step], dst_ref=recv_s.at[chunk, side, group],
            send_sem=s_send.at[chunk, step], recv_sem=s_recv.at[chunk, side, group],
            device_id=(g, to), device_id_type=MESH,
        )
        return quanta, scales

    def arrived(chunk, group, side, acc):
        for copy in chain_copies(chunk, 0, group, side):
            copy.wait_recv()
        acc[:, :width] += dequantize(recv_q[chunk, side, group], recv_s[chunk, side, group])

    def own_sum(chunk, group, acc):
        cross_copy(chunk, group).wait_recv()
        mine = part_ref[chunk, group, pl.ds(pl.multiple_of(core * rows, 8), rows), :]
        acc[:, :width] = mine + cross_ref[chunk, group]

    def chain_step(chunk, step):
        group = group_of(step)
        own_sum(chunk, group, total_ref)
        side = jnp.where(group > z, 0, 1)
        first = jnp.where(side == 0, z == 0, z == chips - 1)

        @pl.when(jnp.logical_not(first))
        def _():
            arrived(chunk, group, side, total_ref)

        quanta, peak = quantize(total_ref[...])
        send_q[chunk, step] = quanta
        send_s[chunk, step] = peak
        for copy in chain_copies(chunk, step, group, side):
            copy.start()

    lag = jnp.where(jnp.logical_or(z == 0, z == chips - 1), 0, 1)
    log_step = math.log(2.0) / 256.0
    occ_pairs = [(i, j) for i in range(occ_rows) for j in range(occ_rows)]

    def mirror_copy(step):
        other = lax.rem(me + step, devices)
        to_grp, to_pair = other // pairs, lax.rem(other, pairs)
        return pltpu.make_async_remote_copy(
            src_ref=mirrored_ref.at[to_pair, to_grp], dst_ref=mirror_ref.at[me],
            send_sem=m_send.at[step], recv_sem=m_recv.at[me],
            device_id=(to_grp, to_pair), device_id_type=MESH,
        )

    def finish_chunk(chunk):
        acc = final_ref.at[chunk]
        own_sum(chunk, z, acc)

        @pl.when(z > 0)
        def _():
            arrived(chunk, z, 0, acc)

        @pl.when(z < chips - 1)
        def _():
            arrived(chunk, z, 1, acc)

        for a in range(8):
            piece_ref[pl.ds(a, rows, stride=8), :] = final_ref[chunk, :, a * vb:a * vb + 128]

        @pl.loop(0, pairs)
        def _(q):
            lane = lax.broadcasted_iota(jnp.int32, (16, 128), 1)
            pieces = [
                piece_ref[
                    pl.ds(pl.multiple_of((i * occupied + q * occ_rows + j) * 8, 8), 8), :
                ]
                for i, j in occ_pairs
            ]
            for h in range(grps):
                ends = []
                for part in (pieces[:slots], pieces[slots:]):
                    packed = jnp.zeros((8, 128), jnp.float32)
                    for at, piece in enumerate(part):
                        shift = ((at - h) * lanes) % 128
                        moved = pltpu.roll(piece, shift, 1) if shift else piece
                        inside = jnp.logical_and(
                            lane[:8] >= at * lanes, lane[:8] < (at + 1) * lanes
                        )
                        packed = jnp.where(inside, moved, packed)
                    ends.append(packed)
                block = jnp.concatenate(ends, axis=0)
                peak = jnp.maximum(jnp.max(jnp.abs(block), axis=1, keepdims=True), 1e-33)
                level = jnp.floor(jnp.log(peak) * (1.0 / log_step)) + 2.0
                whole = jnp.floor(block * (STEPS * jnp.exp(level * -log_step)) + 0.5)
                whole = jnp.where(lane == 127, level, whole).astype(jnp.int32)
                mirrored_ref[q, h, 16 * chunk:16 * chunk + 16] = whole.astype(jnp.int16)

    def take_all():
        @pl.loop(1, devices)
        def _(step):
            other = lax.rem(me + step, devices)
            pltpu.make_async_remote_copy(
                src_ref=mirror_ref.at[other], dst_ref=mirror_ref.at[other],
                send_sem=m_send.at[step], recv_sem=m_recv.at[other],
                device_id=(g, sibling), device_id_type=MESH,
            ).wait_recv()

        @pl.loop(0, pairs)
        def _(q):
            blocks = []
            for h in range(grps):
                for chunk in range(chunks):
                    block = mirror_ref[h * pairs + q, 16 * chunk:16 * chunk + 16].astype(jnp.int32).astype(jnp.float32)
                    blocks.append(block * (jnp.exp(block[:, 127:] * log_step) * (1.0 / STEPS)))
            rest = [jnp.zeros((128 - vb, 128), jnp.float32)]
            for end in range(2):
                turned = jnp.concatenate([b[8 * end:8 * end + 8] for b in blocks] + rest, axis=0).T
                for at, (i, j) in enumerate(occ_pairs[end * slots:(end + 1) * slots]):
                    row = (j * occupied + q * occ_rows + i) * lanes
                    split_ref[pl.ds(pl.multiple_of(row, 8), lanes), :] = (
                        turned[at * lanes:(at + 1) * lanes]
                    )

    relay(0)
    w_copy.wait()
    for chunk in range(chunks):
        final_ref[chunk, :, width:] = jnp.zeros((rows, 128), jnp.float32)

    @pl.loop(0, chips)
    def _(step):
        group = group_of(step)

        @pl.when(step < chips - 2)
        def _():
            relay(step + 1)

        for c in range(2):
            slot = 2 * group + c
            local = step == chips - 1
            relayed = jnp.logical_and(relays_t, c == grp_src)

            @pl.when(jnp.logical_and(local, c == core))
            def _():
                own_copy.wait()

            @pl.when(jnp.logical_or(
                jnp.logical_and(local, c != core),
                jnp.logical_and(jnp.logical_not(local), jnp.logical_not(relayed)),
            ))
            def _():
                t_copy(t_ref.at[slot], slot, t_send.at[0], g, p).wait_recv()

        both = jnp.concatenate(
            [t_ref[2 * group].astype(jnp.float32), t_ref[2 * group + 1].astype(jnp.float32)], axis=0
        )
        tt_ref[...] = (both * mask_ref[:1, :]).astype(jnp.bfloat16)

        for chunk in range(chunks):
            part_ref[chunk, group] = jnp.dot(
                tt_ref[...], w_ref[:, chunk * width:(chunk + 1) * width],
                preferred_element_type=jnp.float32,
            )
            cross_copy(chunk, group).start()

        turn = step - lag

        @pl.when(jnp.logical_and(turn >= 0, turn < chips - 1))
        def _():
            @pl.loop(0, chunks)
            def _(chunk):
                chain_step(chunk, turn)

    for chunk in range(chunks):
        finish_chunk(chunk)

    @pl.loop(1, devices)
    def _(step):
        mirror_copy(step).start()

    mirror_ref[me] = mirrored_ref[p, g]
    take_all()

    lane = lax.broadcasted_iota(jnp.int32, (rows, vb), 1)
    for chunk in range(chunks):
        for a in range(8):
            v = chunk * 8 + a
            alive = jnp.where(g * lanes + v < live_ref[0], live_ref[0], 0)
            both = (
                final_ref[chunk, :, a * vb:(a + 1) * vb]
                + split_ref[pl.ds(v, rows, stride=lanes), :][:, :vb]
            )
            total_ref[:, a * vb:(a + 1) * vb] = jnp.where(lane < alive, both, 0.0)
        out_ref[:, chunk * width:(chunk + 1) * width] = total_ref[...].astype(jnp.bfloat16)

    sib_copy.wait_send()

    @pl.when(sends_t)
    def _():
        @pl.loop(0, chips - 1)
        def _(step):
            z_copy(step).wait_send()

    @pl.when(relays_t)
    def _():
        @pl.loop(0, chips - 1)
        def _(step):
            @pl.loop(1, grps)
            def _(hop):
                relay_copy(step, hop).wait_send()

    @pl.loop(0, chips)
    def _(group):
        for chunk in range(chunks):
            cross_copy(chunk, group).wait_send()

    @pl.loop(0, chips - 1)
    def _(step):
        group = group_of(step)
        for chunk in range(chunks):
            for copy in chain_copies(chunk, step, group, jnp.where(group > z, 0, 1)):
                copy.wait_send()

    @pl.loop(1, devices)
    def _(step):
        mirror_copy(step).wait_send()


def fused(mesh, amplitudes, integrals, live_counts):
    occ_rows, occupied, virt_pairs = amplitudes.shape
    depth, cols = integrals.shape
    grps, pairs = mesh.shape["grp"], mesh.shape["pair"]
    rows, chips, devices = occ_rows * occupied, pairs // 2, grps * pairs
    lanes = cols // VB
    chunks = lanes // 8
    width = cols // chunks
    sizes = (grps, pairs, occ_rows, occupied, depth, cols, VB)
    f32, bf16, i16 = jnp.float32, jnp.bfloat16, jnp.int16
    dma = pltpu.SemaphoreType.DMA
    out = pl.pallas_call(
        functools.partial(kernel, sizes),
        out_shape=jax.ShapeDtypeStruct((rows, cols), bf16),
        in_specs=[
            pl.BlockSpec(memory_space=pltpu.SMEM),
            pl.BlockSpec(memory_space=pl.ANY),
            pl.BlockSpec(memory_space=pl.ANY),
        ],
        out_specs=pl.BlockSpec(memory_space=pltpu.VMEM),
        scratch_shapes=[
            pltpu.VMEM((depth, cols), bf16),
            pltpu.VMEM((pairs, rows, depth), bf16),
            pltpu.VMEM((2 * rows, depth), bf16),
            pltpu.VMEM((8, depth), f32),
            pltpu.VMEM((chunks, chips, 2 * rows, width), f32),
            pltpu.VMEM((chunks, chips, rows, width), f32),
            pltpu.VMEM((chunks, chips - 1, rows, width), i16),
            pltpu.VMEM((chunks, chips - 1, 1, width), f32),
            pltpu.VMEM((chunks, 2, chips, rows, width), i16),
            pltpu.VMEM((chunks, 2, chips, 1, width), f32),
            pltpu.VMEM((rows, width), f32),
            pltpu.VMEM((chunks, rows, width + 128), f32),
            pltpu.VMEM((rows * lanes, 128), f32),
            pltpu.VMEM((rows * 8, 128), f32),
            pltpu.VMEM((pairs, grps, 16 * chunks, 128), i16),
            pltpu.VMEM((devices, 16 * chunks, 128), i16),
            dma(()), dma((chips,)), dma((chips - 1, grps - 1)), dma((pairs,)),
            dma((chunks, chips)), dma((chunks, chips)),
            dma((chunks, chips - 1)), dma((chunks, chips - 1)),
            dma((chunks, 2, chips)), dma((chunks, 2, chips)),
            dma((devices,)), dma((devices,)),
        ],
        compiler_params=pltpu.CompilerParams(
            collective_id=0, has_side_effects=True, vmem_limit_bytes=VMEM_BYTES
        ),
        cost_estimate=pl.CostEstimate(
            flops=4 * pairs // 2 * rows * depth * cols,
            bytes_accessed=2 * depth * cols, transcendentals=0,
        ),
    )(live_counts, amplitudes.reshape(rows, virt_pairs), integrals)
    return out.reshape(occ_rows, occupied, cols)


def gathered(mesh, amplitudes, integrals, live_counts):
    occ_rows, occupied, virt_pairs = amplitudes.shape
    my_pairs, slab_cols = integrals.shape
    tile_size = VB
    slab_lanes = slab_cols // tile_size
    rows = occ_rows * occupied
    flat_rows = lax.all_to_all(
        amplitudes.reshape(rows, virt_pairs), "pair", split_axis=1, concat_axis=0, tiled=True
    )
    position = lax.axis_index("pair") * my_pairs + jnp.arange(my_pairs)
    keep_pairs = (
        (position // tile_size < live_counts[1]) & (position % tile_size < live_counts[1])
    ).astype(jnp.bfloat16)
    partial = jnp.dot(flat_rows * keep_pairs, integrals, preferred_element_type=jnp.float32)
    ladder = lax.psum_scatter(partial, "pair", scatter_dimension=0, tiled=True)
    blocks = ladder.reshape(occ_rows, occupied, slab_lanes, tile_size)
    mirrored = lax.all_to_all(
        lax.all_to_all(blocks, "grp", split_axis=3, concat_axis=2, tiled=True),
        "pair",
        split_axis=1,
        concat_axis=0,
        tiled=True,
    )
    summed = blocks + jnp.transpose(mirrored, (1, 0, 3, 2))
    first_virt = lax.axis_index("grp") * slab_lanes + jnp.arange(slab_lanes)
    second_virt = jnp.arange(tile_size)
    keep_out = (
        (first_virt[:, None] < live_counts[0]) & (second_virt[None, :] < live_counts[0])
    ).astype(jnp.float32)
    return (summed * keep_out).reshape(occ_rows, occupied, slab_cols).astype(jnp.bfloat16)


def on_device(mesh, amplitudes, integrals, live_counts):
    occ_rows, occupied, virt_pairs = amplitudes.shape
    depth, cols = integrals.shape
    rows, pairs = occ_rows * occupied, mesh.shape["pair"]
    held = 2 * depth * cols + rows * cols * (8 * pairs + 8) + 6 * rows * virt_pairs
    lanes = cols // VB
    packs = lanes % 8 == 0 and occ_rows * occ_rows <= 2 * (127 // lanes)
    fits = held < VMEM_BYTES and mesh.shape["grp"] == 4 and packs
    return (fused if fits else gathered)(mesh, amplitudes, integrals, live_counts)


def solution(mesh):
    return jax.shard_map(
        functools.partial(on_device, mesh),
        mesh=mesh,
        in_specs=(P("pair", None, None), P("pair", "grp"), P()),
        out_specs=P("pair", None, "grp"),
        check_vma=False,
    )
```

```python
import functools
import math

import jax
import jax.numpy as jnp
from jax import lax
from jax.experimental import pallas as pl
from jax.experimental.pallas import tpu as pltpu
from jax.sharding import PartitionSpec as P

VB = 96
STEPS = 32767.0
MESH = pl.DeviceIdType.MESH
VMEM_BYTES = 58 * 2**20


def quantize(value):
    peak = jnp.maximum(jnp.max(jnp.abs(value), axis=0, keepdims=True), 1e-33)
    whole = jnp.floor(value * (STEPS / peak) + 0.5).astype(jnp.int32)
    return whole.astype(jnp.int16), peak


def dequantize(quanta, peak):
    return quanta.astype(jnp.int32).astype(jnp.float32) * (peak * (1.0 / STEPS))


def kernel(
    sizes, live_ref, amp_ref, w_hbm, out_ref,
    w_ref, t_ref, tt_ref, mask_ref, part_ref, cross_ref, send_q, send_s,
    recv_q, recv_s, total_ref, final_ref, split_ref, piece_ref, mirrored_ref, mirror_ref,
    w_sem, t_send, t_fwd, t_recv, x_send, x_recv, q_send, s_send, q_recv, s_recv, m_send, m_recv,
):
    grps, pairs, occ_rows, occupied, depth, cols, vb = sizes
    chips = pairs // 2
    rows = occ_rows * occupied
    lanes = cols // vb
    chunks, slots = lanes // 8, 127 // lanes
    width = cols // chunks
    devices = grps * pairs
    g, p = lax.axis_index("grp"), lax.axis_index("pair")
    z, core = p // 2, p % 2
    sibling = 2 * z + 1 - core
    me = g * pairs + p

    barrier = pltpu.get_barrier_semaphore()

    to_grps = [lax.rem(g + n, grps) for n in range(grps)]
    to_pairs = [lax.rem(p + n, pairs) for n in range(pairs)]
    others = [(to_grps[n], to_pairs[m]) for m in range(pairs) for n in range(grps)][1:]
    for other in others:
        pl.semaphore_signal(barrier, inc=1, device_id=other, device_id_type=MESH)

    w_copy = pltpu.make_async_copy(w_hbm, w_ref, w_sem)
    w_copy.start()
    for c in range(depth // vb):
        alive = jnp.where(p * (depth // vb) + c < live_ref[1], live_ref[1], 0)
        lane = lax.broadcasted_iota(jnp.int32, (8, vb), 1)
        mask_ref[:, c * vb:(c + 1) * vb] = jnp.where(lane < alive, 1.0, 0.0)
    pl.semaphore_wait(barrier, devices - 1)

    pieces_t = t_ref.shape[1]
    piece_cols = depth // pieces_t

    def amp_cols(pair, piece):
        return amp_ref.at[
            :, pl.ds(pl.multiple_of(pair * depth + piece * piece_cols, 128), piece_cols)
        ]

    def t_copy(src, slot, piece, send_sem, to_grp, to_pair):
        return pltpu.make_async_remote_copy(
            src_ref=src, dst_ref=t_ref.at[slot, piece], send_sem=send_sem,
            recv_sem=t_recv.at[slot, piece],
            device_id=(to_grp, to_pair), device_id_type=MESH,
        )

    def t_wait(slot, piece):
        t_copy(t_ref.at[slot, piece], slot, piece, t_send.at[0], g, sibling).wait_recv()

    def wait_sent(ref, send_sem):
        pltpu.make_async_remote_copy(
            src_ref=ref, dst_ref=ref, send_sem=send_sem, recv_sem=t_recv.at[0, 0],
            device_id=(g, sibling), device_id_type=MESH,
        ).wait_send()

    near_low = z < chips // 2

    def group_of(step):
        low = jnp.where(step < chips - 1 - z, chips - 1 - step, step - (chips - 1 - z))
        high = jnp.where(step < z, step, chips - 1 - (step - z))
        return jnp.where(step == chips - 1, z, jnp.where(near_low, low, high))

    grp_src, grp_dst = lax.rem(g, 2), g // 2
    sends_t = core == grp_src
    relays_t = core == grp_dst

    def own_copy(piece):
        return pltpu.make_async_copy(amp_cols(p, piece), t_ref.at[p, piece], t_recv.at[p, piece])

    @pl.when(sends_t)
    def _():
        @pl.loop(0, chips - 1)
        def _(step):
            to = 2 * group_of(step) + grp_dst
            for piece in range(pieces_t):
                t_copy(amp_cols(to, piece), p, piece, t_send.at[0], g, to).start()

    for piece in range(pieces_t):
        own_copy(piece).start()
        t_copy(amp_cols(sibling, piece), p, piece, t_send.at[1], g, sibling).start()

    def relay(step):
        @pl.when(relays_t)
        def _():
            slot = 2 * group_of(step) + grp_src
            for piece in range(pieces_t):
                t_wait(slot, piece)
                for hop in range(1, grps):
                    t_copy(
                        t_ref.at[slot, piece], slot, piece, t_fwd.at[hop - 1], to_grps[hop], p
                    ).start()

    def cross_copy(chunk, group):
        return pltpu.make_async_remote_copy(
            src_ref=part_ref.at[
                chunk, group, pl.ds(pl.multiple_of((1 - core) * rows, 8), rows)
            ],
            dst_ref=cross_ref.at[chunk, group], send_sem=x_send,
            recv_sem=x_recv.at[chunk, group], device_id=(g, sibling), device_id_type=MESH,
        )

    def chain_copies(chunk, step, group, side):
        to = 2 * (z + 1 - 2 * side) + core
        quanta = pltpu.make_async_remote_copy(
            src_ref=send_q.at[chunk, step], dst_ref=recv_q.at[chunk, side, group],
            send_sem=q_send, recv_sem=q_recv.at[chunk, side, group],
            device_id=(g, to), device_id_type=MESH,
        )
        scales = pltpu.make_async_remote_copy(
            src_ref=send_s.at[chunk, step], dst_ref=recv_s.at[chunk, side, group],
            send_sem=s_send, recv_sem=s_recv.at[chunk, side, group],
            device_id=(g, to), device_id_type=MESH,
        )
        return quanta, scales

    def arrived(chunk, group, side, acc):
        for copy in chain_copies(chunk, 0, group, side):
            copy.wait_recv()
        acc[:, :width] += dequantize(recv_q[chunk, side, group], recv_s[chunk, side, group])

    def own_sum(chunk, group, acc):
        cross_copy(chunk, group).wait_recv()
        mine = part_ref[chunk, group, pl.ds(pl.multiple_of(core * rows, 8), rows), :]
        acc[:, :width] = mine + cross_ref[chunk, group]

    def chain_step(chunk, step):
        group = group_of(step)
        own_sum(chunk, group, total_ref)
        side = jnp.where(group > z, 0, 1)
        first = jnp.where(side == 0, z == 0, z == chips - 1)

        @pl.when(jnp.logical_not(first))
        def _():
            arrived(chunk, group, side, total_ref)

        quanta, peak = quantize(total_ref[...])
        send_q[chunk, step] = quanta
        send_s[chunk, step] = peak
        for copy in chain_copies(chunk, step, group, side):
            copy.start()

    lag = jnp.where(jnp.logical_or(z == 0, z == chips - 1), 0, 1)
    log_step = math.log(2.0) / 256.0
    occ_pairs = [(i, j) for i in range(occ_rows) for j in range(occ_rows)]

    def mirror_copy(chunk, other):
        to_grp, to_pair = other
        return pltpu.make_async_remote_copy(
            src_ref=mirrored_ref.at[chunk, to_pair, to_grp], dst_ref=mirror_ref.at[chunk, me],
            send_sem=m_send.at[chunk], recv_sem=m_recv.at[chunk],
            device_id=(to_grp, to_pair), device_id_type=MESH,
        )

    def mirror_all(chunk):
        every = mirror_ref.at[chunk, pl.ds(0, devices - 1)]
        return pltpu.make_async_remote_copy(
            src_ref=every, dst_ref=every, send_sem=m_send.at[chunk], recv_sem=m_recv.at[chunk],
            device_id=(g, sibling), device_id_type=MESH,
        )

    def finish_chunk(chunk):
        acc = final_ref.at[chunk]
        own_sum(chunk, z, acc)

        @pl.when(z > 0)
        def _():
            arrived(chunk, z, 0, acc)

        @pl.when(z < chips - 1)
        def _():
            arrived(chunk, z, 1, acc)

        for a in range(8):
            piece_ref[pl.ds(a, rows, stride=8), :] = final_ref[chunk, :, a * vb:a * vb + 128]

        @pl.loop(0, pairs)
        def _(q):
            lane = lax.broadcasted_iota(jnp.int32, (16, 128), 1)
            pieces = [
                piece_ref[
                    pl.ds(pl.multiple_of((i * occupied + q * occ_rows + j) * 8, 8), 8), :
                ]
                for i, j in occ_pairs
            ]
            for h in range(grps):
                ends = []
                for part in (pieces[:slots], pieces[slots:]):
                    packed = jnp.zeros((8, 128), jnp.float32)
                    for at, piece in enumerate(part):
                        shift = ((at - h) * lanes) % 128
                        moved = pltpu.roll(piece, shift, 1) if shift else piece
                        inside = jnp.logical_and(
                            lane[:8] >= at * lanes, lane[:8] < (at + 1) * lanes
                        )
                        packed = jnp.where(inside, moved, packed)
                    ends.append(packed)
                block = jnp.concatenate(ends, axis=0)
                peak = jnp.maximum(jnp.max(jnp.abs(block), axis=1, keepdims=True), 1e-33)
                level = jnp.floor(jnp.log(peak) * (1.0 / log_step)) + 2.0
                whole = jnp.floor(block * (STEPS * jnp.exp(level * -log_step)) + 0.5)
                whole = jnp.where(lane == 127, level, whole).astype(jnp.int32)
                mirrored_ref[chunk, q, h] = whole.astype(jnp.int16)

        for other in others:
            mirror_copy(chunk, other).start()
        mirror_ref[chunk, me] = mirrored_ref[chunk, p, g]

    def take_all():
        for chunk in range(chunks):
            mirror_all(chunk).wait_recv()

        @pl.loop(0, pairs)
        def _(q):
            blocks = []
            for h in range(grps):
                for chunk in range(chunks):
                    block = mirror_ref[chunk, h * pairs + q].astype(jnp.int32).astype(jnp.float32)
                    blocks.append(block * (jnp.exp(block[:, 127:] * log_step) * (1.0 / STEPS)))
            rest = [jnp.zeros((128 - vb, 128), jnp.float32)]
            for end in range(2):
                turned = jnp.concatenate([b[8 * end:8 * end + 8] for b in blocks] + rest, axis=0).T
                for at, (i, j) in enumerate(occ_pairs[end * slots:(end + 1) * slots]):
                    row = (j * occupied + q * occ_rows + i) * lanes
                    split_ref[pl.ds(pl.multiple_of(row, 8), lanes), :] = (
                        turned[at * lanes:(at + 1) * lanes]
                    )

    relay(0)
    w_copy.wait()
    for chunk in range(chunks):
        final_ref[chunk, :, width:] = jnp.zeros((rows, 128), jnp.float32)

    @pl.loop(0, chips)
    def _(step):
        group = group_of(step)

        @pl.when(step < chips - 2)
        def _():
            relay(step + 1)

        for c in range(2):
            slot = 2 * group + c
            local = step == chips - 1
            relayed = jnp.logical_and(relays_t, c == grp_src)

            @pl.when(jnp.logical_and(local, c == core))
            def _():
                for piece in range(pieces_t):
                    own_copy(piece).wait()

            @pl.when(jnp.logical_or(
                jnp.logical_and(local, c != core),
                jnp.logical_and(jnp.logical_not(local), jnp.logical_not(relayed)),
            ))
            def _():
                for piece in range(pieces_t):
                    t_wait(slot, piece)

        for piece in range(pieces_t):
            at = slice(piece * piece_cols, (piece + 1) * piece_cols)
            both = jnp.concatenate(
                [t_ref[2 * group + c, piece].astype(jnp.float32) for c in range(2)], axis=0
            )
            tt_ref[:, at] = (both * mask_ref[:1, at]).astype(jnp.bfloat16)

        for chunk in range(chunks):
            part_ref[chunk, group] = jnp.dot(
                tt_ref[...], w_ref[:, chunk * width:(chunk + 1) * width],
                preferred_element_type=jnp.float32,
            )
            cross_copy(chunk, group).start()

        turn = step - lag

        @pl.when(jnp.logical_and(turn >= 0, turn < chips - 1))
        def _():
            @pl.loop(0, chunks)
            def _(chunk):
                chain_step(chunk, turn)

    for chunk in range(chunks):
        finish_chunk(chunk)

    take_all()

    lane = lax.broadcasted_iota(jnp.int32, (rows, vb), 1)
    for chunk in range(chunks):
        for a in range(8):
            v = chunk * 8 + a
            alive = jnp.where(g * lanes + v < live_ref[0], live_ref[0], 0)
            both = (
                final_ref[chunk, :, a * vb:(a + 1) * vb]
                + split_ref[pl.ds(v, rows, stride=lanes), :][:, :vb]
            )
            total_ref[:, a * vb:(a + 1) * vb] = jnp.where(lane < alive, both, 0.0)
        out_ref[:, chunk * width:(chunk + 1) * width] = total_ref[...].astype(jnp.bfloat16)

    @pl.when(sends_t)
    def _():
        wait_sent(t_ref.at[pl.ds(0, chips - 1)], t_send.at[0])

    wait_sent(t_ref.at[0], t_send.at[1])

    @pl.when(relays_t)
    def _():
        for hop in range(1, grps):
            wait_sent(t_ref.at[pl.ds(0, chips - 1)], t_fwd.at[hop - 1])

    wait_sent(cross_ref, x_send)
    wait_sent(send_q, q_send)
    wait_sent(send_s, s_send)
    for chunk in range(chunks):
        mirror_all(chunk).wait_send()


def fused(mesh, amplitudes, integrals, live_counts):
    occ_rows, occupied, virt_pairs = amplitudes.shape
    depth, cols = integrals.shape
    grps, pairs = mesh.shape["grp"], mesh.shape["pair"]
    rows, chips, devices = occ_rows * occupied, pairs // 2, grps * pairs
    lanes = cols // VB
    chunks = lanes // 8
    width = cols // chunks
    pieces = 3 if depth % 384 == 0 else 1
    sizes = (grps, pairs, occ_rows, occupied, depth, cols, VB)
    f32, bf16, i16 = jnp.float32, jnp.bfloat16, jnp.int16
    dma = pltpu.SemaphoreType.DMA
    out = pl.pallas_call(
        functools.partial(kernel, sizes),
        out_shape=jax.ShapeDtypeStruct((rows, cols), bf16),
        in_specs=[
            pl.BlockSpec(memory_space=pltpu.SMEM),
            pl.BlockSpec(memory_space=pl.ANY),
            pl.BlockSpec(memory_space=pl.ANY),
        ],
        out_specs=pl.BlockSpec(memory_space=pltpu.VMEM),
        scratch_shapes=[
            pltpu.VMEM((depth, cols), bf16),
            pltpu.VMEM((pairs, pieces, rows, depth // pieces), bf16),
            pltpu.VMEM((2 * rows, depth), bf16),
            pltpu.VMEM((8, depth), f32),
            pltpu.VMEM((chunks, chips, 2 * rows, width), f32),
            pltpu.VMEM((chunks, chips, rows, width), f32),
            pltpu.VMEM((chunks, chips - 1, rows, width), i16),
            pltpu.VMEM((chunks, chips - 1, 1, width), f32),
            pltpu.VMEM((chunks, 2, chips, rows, width), i16),
            pltpu.VMEM((chunks, 2, chips, 1, width), f32),
            pltpu.VMEM((rows, width), f32),
            pltpu.VMEM((chunks, rows, width + 128), f32),
            pltpu.VMEM((rows * lanes, 128), f32),
            pltpu.VMEM((rows * 8, 128), f32),
            pltpu.VMEM((chunks, pairs, grps, 16, 128), i16),
            pltpu.VMEM((chunks, devices, 16, 128), i16),
            dma(()), dma((2,)), dma((grps - 1,)), dma((pairs, pieces)),
            dma(()), dma((chunks, chips)), dma(()), dma(()),
            dma((chunks, 2, chips)), dma((chunks, 2, chips)), dma((chunks,)), dma((chunks,)),
        ],
        compiler_params=pltpu.CompilerParams(
            collective_id=0, has_side_effects=True, vmem_limit_bytes=VMEM_BYTES
        ),
        cost_estimate=pl.CostEstimate(
            flops=4 * pairs // 2 * rows * depth * cols,
            bytes_accessed=2 * depth * cols, transcendentals=0,
        ),
    )(live_counts, amplitudes.reshape(rows, virt_pairs), integrals)
    return out.reshape(occ_rows, occupied, cols)


def gathered(mesh, amplitudes, integrals, live_counts):
    occ_rows, occupied, virt_pairs = amplitudes.shape
    my_pairs, slab_cols = integrals.shape
    tile_size = VB
    slab_lanes = slab_cols // tile_size
    rows = occ_rows * occupied
    flat_rows = lax.all_to_all(
        amplitudes.reshape(rows, virt_pairs), "pair", split_axis=1, concat_axis=0, tiled=True
    )
    position = lax.axis_index("pair") * my_pairs + jnp.arange(my_pairs)
    keep_pairs = (
        (position // tile_size < live_counts[1]) & (position % tile_size < live_counts[1])
    ).astype(jnp.bfloat16)
    partial = jnp.dot(flat_rows * keep_pairs, integrals, preferred_element_type=jnp.float32)
    ladder = lax.psum_scatter(partial, "pair", scatter_dimension=0, tiled=True)
    blocks = ladder.reshape(occ_rows, occupied, slab_lanes, tile_size)
    mirrored = lax.all_to_all(
        lax.all_to_all(blocks, "grp", split_axis=3, concat_axis=2, tiled=True),
        "pair",
        split_axis=1,
        concat_axis=0,
        tiled=True,
    )
    summed = blocks + jnp.transpose(mirrored, (1, 0, 3, 2))
    first_virt = lax.axis_index("grp") * slab_lanes + jnp.arange(slab_lanes)
    second_virt = jnp.arange(tile_size)
    keep_out = (
        (first_virt[:, None] < live_counts[0]) & (second_virt[None, :] < live_counts[0])
    ).astype(jnp.float32)
    return (summed * keep_out).reshape(occ_rows, occupied, slab_cols).astype(jnp.bfloat16)


def on_device(mesh, amplitudes, integrals, live_counts):
    occ_rows, occupied, virt_pairs = amplitudes.shape
    depth, cols = integrals.shape
    rows, pairs = occ_rows * occupied, mesh.shape["pair"]
    held = 2 * depth * cols + rows * cols * (8 * pairs + 8) + 6 * rows * virt_pairs
    lanes = cols // VB
    packs = lanes % 8 == 0 and occ_rows * occ_rows <= 2 * (127 // lanes)
    fits = held < VMEM_BYTES and mesh.shape["grp"] == 4 and packs
    return (fused if fits else gathered)(mesh, amplitudes, integrals, live_counts)


def solution(mesh):
    return jax.shard_map(
        functools.partial(on_device, mesh),
        mesh=mesh,
        in_specs=(P("pair", None, None), P("pair", "grp"), P()),
        out_specs=P("pair", None, "grp"),
        check_vma=False,
    )
```

```python
import functools
import math

import jax
import jax.numpy as jnp
from jax import lax
from jax.experimental import pallas as pl
from jax.experimental.pallas import tpu as pltpu
from jax.sharding import PartitionSpec as P

VB = 96
STEPS = 32767.0
MESH = pl.DeviceIdType.MESH
VMEM_BYTES = 58 * 2**20


def quantize(value):
    peak = jnp.maximum(jnp.max(jnp.abs(value), axis=0, keepdims=True), 1e-33)
    whole = jnp.floor(value * (STEPS / peak) + 0.5).astype(jnp.int32)
    return whole.astype(jnp.int16), peak


def dequantize(quanta, peak):
    return quanta.astype(jnp.int32).astype(jnp.float32) * (peak * (1.0 / STEPS))


def kernel(
    sizes, live_ref, amp_ref, w_hbm, out_ref,
    w_ref, t_ref, tt_ref, mask_ref, part_ref, cross_ref, send_q, send_s,
    recv_q, recv_s, total_ref, final_ref, split_ref, piece_ref, mirrored_ref, mirror_ref,
    w_sem, t_send, t_fwd, t_recv, x_send, x_recv, q_send, s_send, q_recv, s_recv, m_send, m_recv,
):
    grps, pairs, occ_rows, occupied, depth, cols, vb = sizes
    chips = pairs // 2
    rows = occ_rows * occupied
    lanes = cols // vb
    chunks, slots = lanes // 8, 127 // lanes
    width = cols // chunks
    devices = grps * pairs
    g, p = lax.axis_index("grp"), lax.axis_index("pair")
    z, core = p // 2, p % 2
    sibling = 2 * z + 1 - core
    me = g * pairs + p

    barrier = pltpu.get_barrier_semaphore()

    to_grps = [lax.rem(g + n, grps) for n in range(grps)]
    to_pairs = [lax.rem(p + n, pairs) for n in range(pairs)]
    others = [(to_grps[n], to_pairs[m]) for m in range(pairs) for n in range(grps)][1:]
    for other in others:
        pl.semaphore_signal(barrier, inc=1, device_id=other, device_id_type=MESH)

    w_copy = pltpu.make_async_copy(w_hbm, w_ref, w_sem)
    w_copy.start()
    for c in range(depth // vb):
        alive = jnp.where(p * (depth // vb) + c < live_ref[1], live_ref[1], 0)
        lane = lax.broadcasted_iota(jnp.int32, (8, vb), 1)
        mask_ref[:, c * vb:(c + 1) * vb] = jnp.where(lane < alive, 1.0, 0.0)
    pl.semaphore_wait(barrier, devices - 1)

    pieces_t = t_ref.shape[1]
    piece_cols = depth // pieces_t

    def amp_cols(pair, piece):
        return amp_ref.at[
            :, pl.ds(pl.multiple_of(pair * depth + piece * piece_cols, 128), piece_cols)
        ]

    def t_copy(src, slot, piece, send_sem, to_grp, to_pair):
        return pltpu.make_async_remote_copy(
            src_ref=src, dst_ref=t_ref.at[slot, piece], send_sem=send_sem,
            recv_sem=t_recv.at[slot, piece],
            device_id=(to_grp, to_pair), device_id_type=MESH,
        )

    def t_wait(slot, piece):
        t_copy(t_ref.at[slot, piece], slot, piece, t_send.at[0], g, sibling).wait_recv()

    def wait_sent(ref, send_sem):
        pltpu.make_async_remote_copy(
            src_ref=ref, dst_ref=ref, send_sem=send_sem, recv_sem=t_recv.at[0, 0],
            device_id=(g, sibling), device_id_type=MESH,
        ).wait_send()

    near_low = z < chips // 2

    def group_of(step):
        low = jnp.where(step < chips - 1 - z, chips - 1 - step, step - (chips - 1 - z))
        high = jnp.where(step < z, step, chips - 1 - (step - z))
        return jnp.where(step == chips - 1, z, jnp.where(near_low, low, high))

    grp_src, grp_dst = lax.rem(g, 2), g // 2
    sends_t = core == grp_src
    relays_t = core == grp_dst

    def own_copy(piece):
        return pltpu.make_async_copy(amp_cols(p, piece), t_ref.at[p, piece], t_recv.at[p, piece])

    @pl.when(sends_t)
    def _():
        @pl.loop(0, chips - 1)
        def _(step):
            to = 2 * group_of(step) + grp_dst
            for piece in range(pieces_t):
                t_copy(amp_cols(to, piece), p, piece, t_send.at[0], g, to).start()

    for piece in range(pieces_t):
        own_copy(piece).start()
        t_copy(amp_cols(sibling, piece), p, piece, t_send.at[1], g, sibling).start()

    def relay(step):
        @pl.when(relays_t)
        def _():
            slot = 2 * group_of(step) + grp_src
            for piece in range(pieces_t):
                t_wait(slot, piece)
                for hop in range(1, grps):
                    t_copy(
                        t_ref.at[slot, piece], slot, piece, t_fwd.at[hop - 1], to_grps[hop], p
                    ).start()

    def cross_copy(chunk, group):
        return pltpu.make_async_remote_copy(
            src_ref=part_ref.at[
                chunk, group, pl.ds(pl.multiple_of((1 - core) * rows, 8), rows)
            ],
            dst_ref=cross_ref.at[chunk, group], send_sem=x_send,
            recv_sem=x_recv.at[chunk, group], device_id=(g, sibling), device_id_type=MESH,
        )

    def chain_copies(chunk, step, group, side):
        to = 2 * (z + 1 - 2 * side) + core
        quanta = pltpu.make_async_remote_copy(
            src_ref=send_q.at[chunk, step], dst_ref=recv_q.at[chunk, side, group],
            send_sem=q_send, recv_sem=q_recv.at[chunk, side, group],
            device_id=(g, to), device_id_type=MESH,
        )
        scales = pltpu.make_async_remote_copy(
            src_ref=send_s.at[chunk, step], dst_ref=recv_s.at[chunk, side, group],
            send_sem=s_send, recv_sem=s_recv.at[chunk, side, group],
            device_id=(g, to), device_id_type=MESH,
        )
        return quanta, scales

    def arrived(chunk, group, side, acc):
        for copy in chain_copies(chunk, 0, group, side):
            copy.wait_recv()
        acc[:, :width] += dequantize(recv_q[chunk, side, group], recv_s[chunk, side, group])

    def own_sum(chunk, group, acc):
        cross_copy(chunk, group).wait_recv()
        mine = part_ref[chunk, group, pl.ds(pl.multiple_of(core * rows, 8), rows), :]
        acc[:, :width] = mine + cross_ref[chunk, group]

    def chain_step(chunk, step):
        group = group_of(step)
        own_sum(chunk, group, total_ref)
        side = jnp.where(group > z, 0, 1)
        first = jnp.where(side == 0, z == 0, z == chips - 1)

        @pl.when(jnp.logical_not(first))
        def _():
            arrived(chunk, group, side, total_ref)

        quanta, peak = quantize(total_ref[...])
        send_q[chunk, step] = quanta
        send_s[chunk, step] = peak
        for copy in chain_copies(chunk, step, group, side):
            copy.start()

    lag = jnp.where(jnp.logical_or(z == 0, z == chips - 1), 0, 1)
    log_step = math.log(2.0) / 256.0
    occ_pairs = [(i, j) for i in range(occ_rows) for j in range(occ_rows)]

    def mirror_copy(other):
        to_grp, to_pair = other
        return pltpu.make_async_remote_copy(
            src_ref=mirrored_ref.at[to_pair, to_grp], dst_ref=mirror_ref.at[me],
            send_sem=m_send, recv_sem=m_recv,
            device_id=(to_grp, to_pair), device_id_type=MESH,
        )

    def mirror_all():
        every = mirror_ref.at[pl.ds(0, devices - 1)]
        return pltpu.make_async_remote_copy(
            src_ref=every, dst_ref=every, send_sem=m_send, recv_sem=m_recv,
            device_id=(g, sibling), device_id_type=MESH,
        )

    def finish_chunk(chunk):
        acc = final_ref.at[chunk]
        own_sum(chunk, z, acc)

        @pl.when(z > 0)
        def _():
            arrived(chunk, z, 0, acc)

        @pl.when(z < chips - 1)
        def _():
            arrived(chunk, z, 1, acc)

        for a in range(8):
            piece_ref[pl.ds(a, rows, stride=8), :] = final_ref[chunk, :, a * vb:a * vb + 128]

        @pl.loop(0, pairs, unroll=4)
        def _(q):
            lane = lax.broadcasted_iota(jnp.int32, (16, 128), 1)
            pieces = [
                piece_ref[
                    pl.ds(pl.multiple_of((i * occupied + q * occ_rows + j) * 8, 8), 8), :
                ]
                for i, j in occ_pairs
            ]
            for h in range(grps):
                ends = []
                for part in (pieces[:slots], pieces[slots:]):
                    packed = jnp.zeros((8, 128), jnp.float32)
                    for at, piece in enumerate(part):
                        shift = ((at - h) * lanes) % 128
                        moved = pltpu.roll(piece, shift, 1) if shift else piece
                        inside = jnp.logical_and(
                            lane[:8] >= at * lanes, lane[:8] < (at + 1) * lanes
                        )
                        packed = jnp.where(inside, moved, packed)
                    ends.append(packed)
                block = jnp.concatenate(ends, axis=0)
                peak = jnp.maximum(jnp.max(jnp.abs(block), axis=1, keepdims=True), 1e-33)
                level = jnp.floor(jnp.log(peak) * (1.0 / log_step)) + 2.0
                whole = jnp.floor(block * (STEPS * jnp.exp(level * -log_step)) + 0.5)
                whole = jnp.where(lane == 127, level, whole).astype(jnp.int32)
                mirrored_ref[q, h, 16 * chunk:16 * chunk + 16] = whole.astype(jnp.int16)

    def take_all():
        mirror_all().wait_recv()

        @pl.loop(0, pairs, unroll=4)
        def _(q):
            blocks = []
            for h in range(grps):
                for chunk in range(chunks):
                    block = mirror_ref[h * pairs + q, 16 * chunk:16 * chunk + 16].astype(jnp.int32).astype(jnp.float32)
                    blocks.append(block * (jnp.exp(block[:, 127:] * log_step) * (1.0 / STEPS)))
            rest = [jnp.zeros((128 - vb, 128), jnp.float32)]
            for end in range(2):
                turned = jnp.concatenate([b[8 * end:8 * end + 8] for b in blocks] + rest, axis=0).T
                for at, (i, j) in enumerate(occ_pairs[end * slots:(end + 1) * slots]):
                    row = (j * occupied + q * occ_rows + i) * lanes
                    split_ref[pl.ds(pl.multiple_of(row, 8), lanes), :] = (
                        turned[at * lanes:(at + 1) * lanes]
                    )

    relay(0)
    w_copy.wait()
    for chunk in range(chunks):
        final_ref[chunk, :, width:] = jnp.zeros((rows, 128), jnp.float32)

    @pl.loop(0, chips)
    def _(step):
        group = group_of(step)

        @pl.when(step < chips - 2)
        def _():
            relay(step + 1)

        for c in range(2):
            slot = 2 * group + c
            local = step == chips - 1
            relayed = jnp.logical_and(relays_t, c == grp_src)

            @pl.when(jnp.logical_and(local, c == core))
            def _():
                for piece in range(pieces_t):
                    own_copy(piece).wait()

            @pl.when(jnp.logical_or(
                jnp.logical_and(local, c != core),
                jnp.logical_and(jnp.logical_not(local), jnp.logical_not(relayed)),
            ))
            def _():
                for piece in range(pieces_t):
                    t_wait(slot, piece)

        turn = step - lag
        turning = jnp.logical_and(turn >= 0, turn < chips - 1)
        for piece in range(pieces_t):
            at = slice(piece * piece_cols, (piece + 1) * piece_cols)
            both = jnp.concatenate(
                [t_ref[2 * group + c, piece].astype(jnp.float32) for c in range(2)], axis=0
            )
            tt_ref[:, at] = (both * mask_ref[:1, at]).astype(jnp.bfloat16)

        for chunk in range(chunks):
            part_ref[chunk, group] = jnp.dot(
                tt_ref[...], w_ref[:, chunk * width:(chunk + 1) * width],
                preferred_element_type=jnp.float32,
            )
            cross_copy(chunk, group).start()
            if chunk > 0:
                @pl.when(turning)
                def _():
                    chain_step(chunk - 1, turn)

        @pl.when(turning)
        def _():
            chain_step(chunks - 1, turn)

    for chunk in range(chunks):
        finish_chunk(chunk)

    for other in others:
        mirror_copy(other).start()
    mirror_ref[me] = mirrored_ref[p, g]
    take_all()

    lane = lax.broadcasted_iota(jnp.int32, (rows, vb), 1)
    for chunk in range(chunks):
        for a in range(8):
            v = chunk * 8 + a
            alive = jnp.where(g * lanes + v < live_ref[0], live_ref[0], 0)
            both = (
                final_ref[chunk, :, a * vb:(a + 1) * vb]
                + split_ref[pl.ds(v, rows, stride=lanes), :][:, :vb]
            )
            total_ref[:, a * vb:(a + 1) * vb] = jnp.where(lane < alive, both, 0.0)
        out_ref[:, chunk * width:(chunk + 1) * width] = total_ref[...].astype(jnp.bfloat16)

    @pl.when(sends_t)
    def _():
        wait_sent(t_ref.at[pl.ds(0, chips - 1)], t_send.at[0])

    wait_sent(t_ref.at[0], t_send.at[1])

    @pl.when(relays_t)
    def _():
        for hop in range(1, grps):
            wait_sent(t_ref.at[pl.ds(0, chips - 1)], t_fwd.at[hop - 1])

    wait_sent(cross_ref, x_send)
    wait_sent(send_q, q_send)
    wait_sent(send_s, s_send)
    mirror_all().wait_send()


def fused(mesh, amplitudes, integrals, live_counts):
    occ_rows, occupied, virt_pairs = amplitudes.shape
    depth, cols = integrals.shape
    grps, pairs = mesh.shape["grp"], mesh.shape["pair"]
    rows, chips, devices = occ_rows * occupied, pairs // 2, grps * pairs
    lanes = cols // VB
    chunks = lanes // 8
    width = cols // chunks
    pieces = 3 if depth % 384 == 0 else 1
    sizes = (grps, pairs, occ_rows, occupied, depth, cols, VB)
    f32, bf16, i16 = jnp.float32, jnp.bfloat16, jnp.int16
    dma = pltpu.SemaphoreType.DMA
    out = pl.pallas_call(
        functools.partial(kernel, sizes),
        out_shape=jax.ShapeDtypeStruct((rows, cols), bf16),
        in_specs=[
            pl.BlockSpec(memory_space=pltpu.SMEM),
            pl.BlockSpec(memory_space=pl.ANY),
            pl.BlockSpec(memory_space=pl.ANY),
        ],
        out_specs=pl.BlockSpec(memory_space=pltpu.VMEM),
        scratch_shapes=[
            pltpu.VMEM((depth, cols), bf16),
            pltpu.VMEM((pairs, pieces, rows, depth // pieces), bf16),
            pltpu.VMEM((2 * rows, depth), bf16),
            pltpu.VMEM((8, depth), f32),
            pltpu.VMEM((chunks, chips, 2 * rows, width), f32),
            pltpu.VMEM((chunks, chips, rows, width), f32),
            pltpu.VMEM((chunks, chips - 1, rows, width), i16),
            pltpu.VMEM((chunks, chips - 1, 1, width), f32),
            pltpu.VMEM((chunks, 2, chips, rows, width), i16),
            pltpu.VMEM((chunks, 2, chips, 1, width), f32),
            pltpu.VMEM((rows, width), f32),
            pltpu.VMEM((chunks, rows, width + 128), f32),
            pltpu.VMEM((rows * lanes, 128), f32),
            pltpu.VMEM((rows * 8, 128), f32),
            pltpu.VMEM((pairs, grps, 16 * chunks, 128), i16),
            pltpu.VMEM((devices, 16 * chunks, 128), i16),
            dma(()), dma((2,)), dma((grps - 1,)), dma((pairs, pieces)),
            dma(()), dma((chunks, chips)), dma(()), dma(()),
            dma((chunks, 2, chips)), dma((chunks, 2, chips)), dma(()), dma(()),
        ],
        compiler_params=pltpu.CompilerParams(
            collective_id=0, has_side_effects=True, vmem_limit_bytes=VMEM_BYTES
        ),
        cost_estimate=pl.CostEstimate(
            flops=4 * pairs // 2 * rows * depth * cols,
            bytes_accessed=2 * depth * cols, transcendentals=0,
        ),
    )(live_counts, amplitudes.reshape(rows, virt_pairs), integrals)
    return out.reshape(occ_rows, occupied, cols)


def gathered(mesh, amplitudes, integrals, live_counts):
    occ_rows, occupied, virt_pairs = amplitudes.shape
    my_pairs, slab_cols = integrals.shape
    tile_size = VB
    slab_lanes = slab_cols // tile_size
    rows = occ_rows * occupied
    flat_rows = lax.all_to_all(
        amplitudes.reshape(rows, virt_pairs), "pair", split_axis=1, concat_axis=0, tiled=True
    )
    position = lax.axis_index("pair") * my_pairs + jnp.arange(my_pairs)
    keep_pairs = (
        (position // tile_size < live_counts[1]) & (position % tile_size < live_counts[1])
    ).astype(jnp.bfloat16)
    partial = jnp.dot(flat_rows * keep_pairs, integrals, preferred_element_type=jnp.float32)
    ladder = lax.psum_scatter(partial, "pair", scatter_dimension=0, tiled=True)
    blocks = ladder.reshape(occ_rows, occupied, slab_lanes, tile_size)
    mirrored = lax.all_to_all(
        lax.all_to_all(blocks, "grp", split_axis=3, concat_axis=2, tiled=True),
        "pair",
        split_axis=1,
        concat_axis=0,
        tiled=True,
    )
    summed = blocks + jnp.transpose(mirrored, (1, 0, 3, 2))
    first_virt = lax.axis_index("grp") * slab_lanes + jnp.arange(slab_lanes)
    second_virt = jnp.arange(tile_size)
    keep_out = (
        (first_virt[:, None] < live_counts[0]) & (second_virt[None, :] < live_counts[0])
    ).astype(jnp.float32)
    return (summed * keep_out).reshape(occ_rows, occupied, slab_cols).astype(jnp.bfloat16)


def on_device(mesh, amplitudes, integrals, live_counts):
    occ_rows, occupied, virt_pairs = amplitudes.shape
    depth, cols = integrals.shape
    rows, pairs = occ_rows * occupied, mesh.shape["pair"]
    held = 2 * depth * cols + rows * cols * (8 * pairs + 8) + 6 * rows * virt_pairs
    lanes = cols // VB
    packs = lanes % 8 == 0 and occ_rows * occ_rows <= 2 * (127 // lanes)
    fits = held < VMEM_BYTES and mesh.shape["grp"] == 4 and packs
    return (fused if fits else gathered)(mesh, amplitudes, integrals, live_counts)


def solution(mesh):
    return jax.shard_map(
        functools.partial(on_device, mesh),
        mesh=mesh,
        in_specs=(P("pair", None, None), P("pair", "grp"), P()),
        out_specs=P("pair", None, "grp"),
        check_vma=False,
    )
```

```python
import functools
import math

import jax
import jax.numpy as jnp
from jax import lax
from jax.experimental import pallas as pl
from jax.experimental.pallas import tpu as pltpu
from jax.sharding import PartitionSpec as P

VB = 96
STEPS = 32767.0
MESH = pl.DeviceIdType.MESH
VMEM_BYTES = 40 * 2**20


def quantize(value):
    peak = jnp.maximum(jnp.max(jnp.abs(value), axis=0, keepdims=True), 1e-33)
    whole = jnp.floor(value * (STEPS / peak) + 0.5).astype(jnp.int32)
    return whole.astype(jnp.int16), peak


def dequantize(quanta, peak):
    return quanta.astype(jnp.int32).astype(jnp.float32) * (peak * (1.0 / STEPS))


def kernel(
    sizes, live_ref, amp_ref, w_hbm, out_ref,
    w_ref, t_ref, tt_ref, mask_ref, part_ref, cross_ref, send_q, send_s,
    recv_q, recv_s, total_ref, final_ref, split_ref, piece_ref, mirrored_ref, mirror_ref,
    w_sem, t_send, t_fwd, t_recv, x_send, x_recv, q_send, s_send, q_recv, s_recv, m_send, m_recv,
):
    grps, pairs, occ_rows, occupied, depth, cols, vb = sizes
    chips = pairs // 2
    rows = occ_rows * occupied
    lanes = cols // vb
    chunks, slots = lanes // 8, 127 // lanes
    width = cols // chunks
    devices = grps * pairs
    g, p = lax.axis_index("grp"), lax.axis_index("pair")
    z, core = p // 2, p % 2
    sibling = 2 * z + 1 - core
    me = g * pairs + p

    barrier = pltpu.get_barrier_semaphore()

    to_grps = [lax.rem(g + n, grps) for n in range(grps)]
    to_pairs = [lax.rem(p + n, pairs) for n in range(pairs)]
    others = [(to_grps[n], to_pairs[m]) for m in range(pairs) for n in range(grps)][1:]
    for other in others:
        pl.semaphore_signal(barrier, inc=1, device_id=other, device_id_type=MESH)

    w_copy = pltpu.make_async_copy(w_hbm, w_ref, w_sem)
    w_copy.start()
    for c in range(depth // vb):
        alive = jnp.where(p * (depth // vb) + c < live_ref[1], live_ref[1], 0)
        lane = lax.broadcasted_iota(jnp.int32, (8, vb), 1)
        mask_ref[:, c * vb:(c + 1) * vb] = jnp.where(lane < alive, 1.0, 0.0)
    pl.semaphore_wait(barrier, devices - 1)

    pieces_t = t_ref.shape[1]
    piece_cols = depth // pieces_t

    def amp_cols(pair, piece):
        return amp_ref.at[
            :, pl.ds(pl.multiple_of(pair * depth + piece * piece_cols, 128), piece_cols)
        ]

    def t_copy(src, slot, piece, send_sem, to_grp, to_pair):
        return pltpu.make_async_remote_copy(
            src_ref=src, dst_ref=t_ref.at[slot, piece], send_sem=send_sem,
            recv_sem=t_recv.at[slot, piece],
            device_id=(to_grp, to_pair), device_id_type=MESH,
        )

    def t_wait(slot, piece):
        t_copy(t_ref.at[slot, piece], slot, piece, t_send.at[0], g, sibling).wait_recv()

    def wait_sent(ref, send_sem):
        pltpu.make_async_remote_copy(
            src_ref=ref, dst_ref=ref, send_sem=send_sem, recv_sem=t_recv.at[0, 0],
            device_id=(g, sibling), device_id_type=MESH,
        ).wait_send()

    near_low = z < chips // 2

    def group_of(step):
        low = jnp.where(step < chips - 1 - z, chips - 1 - step, step - (chips - 1 - z))
        high = jnp.where(step < z, step, chips - 1 - (step - z))
        return jnp.where(step == chips - 1, z, jnp.where(near_low, low, high))

    grp_src, grp_dst = lax.rem(g, 2), g // 2
    sends_t = core == grp_src
    relays_t = core == grp_dst

    def own_copy(piece):
        return pltpu.make_async_copy(amp_cols(p, piece), t_ref.at[p, piece], t_recv.at[p, piece])

    @pl.when(sends_t)
    def _():
        @pl.loop(0, chips - 1)
        def _(step):
            to = 2 * group_of(step) + grp_dst
            for piece in range(pieces_t):
                t_copy(amp_cols(to, piece), p, piece, t_send.at[0], g, to).start()

    for piece in range(pieces_t):
        own_copy(piece).start()
        t_copy(amp_cols(sibling, piece), p, piece, t_send.at[1], g, sibling).start()

    def relay(step):
        @pl.when(relays_t)
        def _():
            slot = 2 * group_of(step) + grp_src
            for piece in range(pieces_t):
                t_wait(slot, piece)
                for hop in range(1, grps):
                    t_copy(
                        t_ref.at[slot, piece], slot, piece, t_fwd.at[hop - 1], to_grps[hop], p
                    ).start()

    def cross_copy(chunk, group):
        return pltpu.make_async_remote_copy(
            src_ref=part_ref.at[
                chunk, group, pl.ds(pl.multiple_of((1 - core) * rows, 8), rows)
            ],
            dst_ref=cross_ref.at[chunk, group], send_sem=x_send,
            recv_sem=x_recv.at[chunk, group], device_id=(g, sibling), device_id_type=MESH,
        )

    def chain_copies(chunk, step, group, side):
        to = 2 * (z + 1 - 2 * side) + core
        quanta = pltpu.make_async_remote_copy(
            src_ref=send_q.at[chunk, step], dst_ref=recv_q.at[chunk, side, group],
            send_sem=q_send, recv_sem=q_recv.at[chunk, side, group],
            device_id=(g, to), device_id_type=MESH,
        )
        scales = pltpu.make_async_remote_copy(
            src_ref=send_s.at[chunk, step], dst_ref=recv_s.at[chunk, side, group],
            send_sem=s_send, recv_sem=s_recv.at[chunk, side, group],
            device_id=(g, to), device_id_type=MESH,
        )
        return quanta, scales

    def arrived(chunk, group, side, acc):
        for copy in chain_copies(chunk, 0, group, side):
            copy.wait_recv()
        acc[:, :width] += dequantize(recv_q[chunk, side, group], recv_s[chunk, side, group])

    def own_sum(chunk, group, acc):
        cross_copy(chunk, group).wait_recv()
        mine = part_ref[chunk, group, pl.ds(pl.multiple_of(core * rows, 8), rows), :]
        acc[:, :width] = mine + cross_ref[chunk, group]

    def chain_step(chunk, step):
        group = group_of(step)
        own_sum(chunk, group, total_ref)
        side = jnp.where(group > z, 0, 1)
        first = jnp.where(side == 0, z == 0, z == chips - 1)

        @pl.when(jnp.logical_not(first))
        def _():
            arrived(chunk, group, side, total_ref)

        quanta, peak = quantize(total_ref[...])
        send_q[chunk, step] = quanta
        send_s[chunk, step] = peak
        for copy in chain_copies(chunk, step, group, side):
            copy.start()

    lag = jnp.where(jnp.logical_or(z == 0, z == chips - 1), 0, 1)
    log_step = math.log(2.0) / 256.0
    occ_pairs = [(i, j) for i in range(occ_rows) for j in range(occ_rows)]

    def mirror_copy(other):
        to_grp, to_pair = other
        return pltpu.make_async_remote_copy(
            src_ref=mirrored_ref.at[to_pair, to_grp], dst_ref=mirror_ref.at[me],
            send_sem=m_send, recv_sem=m_recv,
            device_id=(to_grp, to_pair), device_id_type=MESH,
        )

    def mirror_all():
        every = mirror_ref.at[pl.ds(0, devices - 1)]
        return pltpu.make_async_remote_copy(
            src_ref=every, dst_ref=every, send_sem=m_send, recv_sem=m_recv,
            device_id=(g, sibling), device_id_type=MESH,
        )

    def finish_chunk(chunk):
        acc = final_ref.at[chunk]
        own_sum(chunk, z, acc)

        @pl.when(z > 0)
        def _():
            arrived(chunk, z, 0, acc)

        @pl.when(z < chips - 1)
        def _():
            arrived(chunk, z, 1, acc)

        for a in range(8):
            piece_ref[pl.ds(a, rows, stride=8), :] = final_ref[chunk, :, a * vb:a * vb + 128]

        @pl.loop(0, pairs, unroll=4)
        def _(q):
            lane = lax.broadcasted_iota(jnp.int32, (16, 128), 1)
            pieces = [
                piece_ref[
                    pl.ds(pl.multiple_of((i * occupied + q * occ_rows + j) * 8, 8), 8), :
                ]
                for i, j in occ_pairs
            ]
            for h in range(grps):
                ends = []
                for part in (pieces[:slots], pieces[slots:]):
                    packed = jnp.zeros((8, 128), jnp.float32)
                    for at, piece in enumerate(part):
                        shift = ((at - h) * lanes) % 128
                        moved = pltpu.roll(piece, shift, 1) if shift else piece
                        inside = jnp.logical_and(
                            lane[:8] >= at * lanes, lane[:8] < (at + 1) * lanes
                        )
                        packed = jnp.where(inside, moved, packed)
                    ends.append(packed)
                block = jnp.concatenate(ends, axis=0)
                peak = jnp.maximum(jnp.max(jnp.abs(block), axis=1, keepdims=True), 1e-33)
                level = jnp.floor(jnp.log(peak) * (1.0 / log_step)) + 2.0
                whole = jnp.floor(block * (STEPS * jnp.exp(level * -log_step)) + 0.5)
                whole = jnp.where(lane == 127, level, whole).astype(jnp.int32)
                mirrored_ref[q, h, 16 * chunk:16 * chunk + 16] = whole.astype(jnp.int16)

    def take_all():
        mirror_all().wait_recv()

        @pl.loop(0, pairs, unroll=4)
        def _(q):
            blocks = []
            for h in range(grps):
                for chunk in range(chunks):
                    block = mirror_ref[h * pairs + q, 16 * chunk:16 * chunk + 16].astype(jnp.int32).astype(jnp.float32)
                    blocks.append(block * (jnp.exp(block[:, 127:] * log_step) * (1.0 / STEPS)))
            rest = [jnp.zeros((128 - vb, 128), jnp.float32)]
            for end in range(2):
                turned = jnp.concatenate([b[8 * end:8 * end + 8] for b in blocks] + rest, axis=0).T
                for at, (i, j) in enumerate(occ_pairs[end * slots:(end + 1) * slots]):
                    row = (j * occupied + q * occ_rows + i) * lanes
                    split_ref[pl.ds(pl.multiple_of(row, 8), lanes), :] = (
                        turned[at * lanes:(at + 1) * lanes]
                    )

    def mask_group(group):
        for piece in range(pieces_t):
            at = slice(piece * piece_cols, (piece + 1) * piece_cols)
            both = jnp.concatenate(
                [t_ref[2 * group + c, piece].astype(jnp.float32) for c in range(2)], axis=0
            )
            tt_ref[:, at] = (both * mask_ref[:1, at]).astype(jnp.bfloat16)

    def multiply(chunk, group):
        part_ref[chunk, group] = jnp.dot(
            tt_ref[...], w_ref[:, chunk * width:(chunk + 1) * width],
            preferred_element_type=jnp.float32,
        )
        cross_copy(chunk, group).start()

    for chunk in range(chunks):
        final_ref[chunk, :, width:] = jnp.zeros((rows, 128), jnp.float32)
    w_copy.wait()
    for piece in range(pieces_t):
        own_copy(piece).wait()
        t_wait(sibling, piece)
    mask_group(z)
    multiply(0, z)
    relay(0)
    for chunk in range(1, chunks):
        multiply(chunk, z)

    @pl.loop(0, chips - 1)
    def _(step):
        group = group_of(step)

        @pl.when(step < chips - 2)
        def _():
            relay(step + 1)

        for c in range(2):
            @pl.when(jnp.logical_not(jnp.logical_and(relays_t, c == grp_src)))
            def _():
                for piece in range(pieces_t):
                    t_wait(2 * group + c, piece)

        turn = step - lag
        mask_group(group)
        for chunk in range(chunks):
            multiply(chunk, group)
            if chunk > 0:
                @pl.when(turn >= 0)
                def _():
                    chain_step(chunk - 1, turn)

        @pl.when(turn >= 0)
        def _():
            chain_step(chunks - 1, turn)

    @pl.when(lag == 1)
    def _():
        @pl.loop(0, chunks)
        def _(chunk):
            chain_step(chunk, chips - 2)

    for chunk in range(chunks):
        finish_chunk(chunk)

    for other in others:
        mirror_copy(other).start()
    mirror_ref[me] = mirrored_ref[p, g]
    take_all()

    lane = lax.broadcasted_iota(jnp.int32, (rows, vb), 1)
    for chunk in range(chunks):
        for a in range(8):
            v = chunk * 8 + a
            alive = jnp.where(g * lanes + v < live_ref[0], live_ref[0], 0)
            both = (
                final_ref[chunk, :, a * vb:(a + 1) * vb]
                + split_ref[pl.ds(v, rows, stride=lanes), :][:, :vb]
            )
            total_ref[:, a * vb:(a + 1) * vb] = jnp.where(lane < alive, both, 0.0)
        out_ref[:, chunk * width:(chunk + 1) * width] = total_ref[...].astype(jnp.bfloat16)

    @pl.when(sends_t)
    def _():
        wait_sent(t_ref.at[pl.ds(0, chips - 1)], t_send.at[0])

    wait_sent(t_ref.at[0], t_send.at[1])

    @pl.when(relays_t)
    def _():
        for hop in range(1, grps):
            wait_sent(t_ref.at[pl.ds(0, chips - 1)], t_fwd.at[hop - 1])

    wait_sent(cross_ref, x_send)
    wait_sent(send_q, q_send)
    wait_sent(send_s, s_send)
    mirror_all().wait_send()


def fused(mesh, amplitudes, integrals, live_counts):
    occ_rows, occupied, virt_pairs = amplitudes.shape
    depth, cols = integrals.shape
    grps, pairs = mesh.shape["grp"], mesh.shape["pair"]
    rows, chips, devices = occ_rows * occupied, pairs // 2, grps * pairs
    lanes = cols // VB
    chunks = lanes // 8
    width = cols // chunks
    pieces = 3 if depth % 384 == 0 else 1
    sizes = (grps, pairs, occ_rows, occupied, depth, cols, VB)
    f32, bf16, i16 = jnp.float32, jnp.bfloat16, jnp.int16
    dma = pltpu.SemaphoreType.DMA
    out = pl.pallas_call(
        functools.partial(kernel, sizes),
        out_shape=jax.ShapeDtypeStruct((rows, cols), bf16),
        in_specs=[
            pl.BlockSpec(memory_space=pltpu.SMEM),
            pl.BlockSpec(memory_space=pltpu.HBM),
            pl.BlockSpec(memory_space=pltpu.HBM),
        ],
        out_specs=pl.BlockSpec(memory_space=pltpu.VMEM),
        scratch_shapes=[
            pltpu.VMEM((depth, cols), bf16),
            pltpu.VMEM((pairs, pieces, rows, depth // pieces), bf16),
            pltpu.VMEM((2 * rows, depth), bf16),
            pltpu.VMEM((8, depth), f32),
            pltpu.VMEM((chunks, chips, 2 * rows, width), f32),
            pltpu.VMEM((chunks, chips, rows, width), f32),
            pltpu.VMEM((chunks, chips - 1, rows, width), i16),
            pltpu.VMEM((chunks, chips - 1, 1, width), f32),
            pltpu.VMEM((chunks, 2, chips, rows, width), i16),
            pltpu.VMEM((chunks, 2, chips, 1, width), f32),
            pltpu.VMEM((rows, width), f32),
            pltpu.VMEM((chunks, rows, width + 128), f32),
            pltpu.VMEM((rows * lanes, 128), f32),
            pltpu.VMEM((rows * 8, 128), f32),
            pltpu.VMEM((pairs, grps, 16 * chunks, 128), i16),
            pltpu.VMEM((devices, 16 * chunks, 128), i16),
            dma(()), dma((2,)), dma((grps - 1,)), dma((pairs, pieces)),
            dma(()), dma((chunks, chips)), dma(()), dma(()),
            dma((chunks, 2, chips)), dma((chunks, 2, chips)), dma(()), dma(()),
        ],
        compiler_params=pltpu.CompilerParams(
            collective_id=0, has_side_effects=True, vmem_limit_bytes=VMEM_BYTES
        ),
        cost_estimate=pl.CostEstimate(
            flops=4 * pairs // 2 * rows * depth * cols,
            bytes_accessed=2 * depth * cols, transcendentals=0,
        ),
    )(live_counts, amplitudes.reshape(rows, virt_pairs), integrals)
    return out.reshape(occ_rows, occupied, cols)


def gathered(mesh, amplitudes, integrals, live_counts):
    occ_rows, occupied, virt_pairs = amplitudes.shape
    my_pairs, slab_cols = integrals.shape
    tile_size = VB
    slab_lanes = slab_cols // tile_size
    rows = occ_rows * occupied
    flat_rows = lax.all_to_all(
        amplitudes.reshape(rows, virt_pairs), "pair", split_axis=1, concat_axis=0, tiled=True
    )
    position = lax.axis_index("pair") * my_pairs + jnp.arange(my_pairs)
    keep_pairs = (
        (position // tile_size < live_counts[1]) & (position % tile_size < live_counts[1])
    ).astype(jnp.bfloat16)
    partial = jnp.dot(flat_rows * keep_pairs, integrals, preferred_element_type=jnp.float32)
    ladder = lax.psum_scatter(partial, "pair", scatter_dimension=0, tiled=True)
    blocks = ladder.reshape(occ_rows, occupied, slab_lanes, tile_size)
    mirrored = lax.all_to_all(
        lax.all_to_all(blocks, "grp", split_axis=3, concat_axis=2, tiled=True),
        "pair",
        split_axis=1,
        concat_axis=0,
        tiled=True,
    )
    summed = blocks + jnp.transpose(mirrored, (1, 0, 3, 2))
    first_virt = lax.axis_index("grp") * slab_lanes + jnp.arange(slab_lanes)
    second_virt = jnp.arange(tile_size)
    keep_out = (
        (first_virt[:, None] < live_counts[0]) & (second_virt[None, :] < live_counts[0])
    ).astype(jnp.float32)
    return (summed * keep_out).reshape(occ_rows, occupied, slab_cols).astype(jnp.bfloat16)


def on_device(mesh, amplitudes, integrals, live_counts):
    occ_rows, occupied, virt_pairs = amplitudes.shape
    depth, cols = integrals.shape
    rows, pairs = occ_rows * occupied, mesh.shape["pair"]
    held = 2 * depth * cols + rows * cols * (8 * pairs + 8) + 6 * rows * virt_pairs
    lanes = cols // VB
    packs = lanes % 8 == 0 and occ_rows * occ_rows <= 2 * (127 // lanes)
    fits = held < VMEM_BYTES and mesh.shape["grp"] == 4 and packs
    return (fused if fits else gathered)(mesh, amplitudes, integrals, live_counts)


def solution(mesh):
    return jax.shard_map(
        functools.partial(on_device, mesh),
        mesh=mesh,
        in_specs=(P("pair", None, None), P("pair", "grp"), P()),
        out_specs=P("pair", None, "grp"),
        check_vma=False,
    )
```

```python
import functools
import math

import jax
import jax.numpy as jnp
from jax import lax
from jax.experimental import pallas as pl
from jax.experimental.pallas import tpu as pltpu
from jax.sharding import PartitionSpec as P

VB = 96
STEPS = 32767.0
MESH = pl.DeviceIdType.MESH
VMEM_BYTES = 58 * 2**20


def quantize(value):
    peak = jnp.maximum(jnp.max(jnp.abs(value), axis=0, keepdims=True), 1e-33)
    whole = jnp.floor(value * (STEPS / peak) + 0.5).astype(jnp.int32)
    return whole.astype(jnp.int16), peak


def dequantize(quanta, peak):
    return quanta.astype(jnp.int32).astype(jnp.float32) * (peak * (1.0 / STEPS))


def kernel(
    sizes, live_ref, amp_ref, w_hbm, out_ref,
    w_ref, t_ref, tt_ref, mask_ref, part_ref, cross_ref, send_q, send_s,
    recv_q, recv_s, total_ref, final_ref, split_ref, piece_ref, mirrored_ref, mirror_ref,
    w_sem, t_send, t_fwd, t_recv, x_send, x_recv, q_send, s_send, q_recv, s_recv, m_send, m_recv,
):
    grps, pairs, occ_rows, occupied, depth, cols, vb = sizes
    chips = pairs // 2
    rows = occ_rows * occupied
    lanes = cols // vb
    chunks, slots = lanes // 8, 127 // lanes
    width = cols // chunks
    devices = grps * pairs
    g, p = lax.axis_index("grp"), lax.axis_index("pair")
    z, core = p // 2, p % 2
    sibling = 2 * z + 1 - core
    me = g * pairs + p

    barrier = pltpu.get_barrier_semaphore()

    to_grps = [lax.rem(g + n, grps) for n in range(grps)]
    to_pairs = [lax.rem(p + n, pairs) for n in range(pairs)]
    others = [(to_grps[n], to_pairs[m]) for m in range(pairs) for n in range(grps)][1:]
    for other in others:
        pl.semaphore_signal(barrier, inc=1, device_id=other, device_id_type=MESH)

    w_copy = pltpu.make_async_copy(w_hbm, w_ref, w_sem)
    w_copy.start()
    for c in range(depth // vb):
        alive = jnp.where(p * (depth // vb) + c < live_ref[1], live_ref[1], 0)
        lane = lax.broadcasted_iota(jnp.int32, (8, vb), 1)
        mask_ref[:, c * vb:(c + 1) * vb] = jnp.where(lane < alive, 1.0, 0.0)
    pl.semaphore_wait(barrier, devices - 1)

    pieces_t = t_ref.shape[1]
    piece_cols = depth // pieces_t

    def amp_cols(pair, piece):
        return amp_ref.at[
            :, pl.ds(pl.multiple_of(pair * depth + piece * piece_cols, 128), piece_cols)
        ]

    def t_copy(src, slot, piece, send_sem, to_grp, to_pair):
        return pltpu.make_async_remote_copy(
            src_ref=src, dst_ref=t_ref.at[slot, piece], send_sem=send_sem,
            recv_sem=t_recv.at[slot, piece],
            device_id=(to_grp, to_pair), device_id_type=MESH,
        )

    def t_wait(slot, piece):
        t_copy(t_ref.at[slot, piece], slot, piece, t_send.at[0], g, sibling).wait_recv()

    def wait_sent(ref, send_sem):
        pltpu.make_async_remote_copy(
            src_ref=ref, dst_ref=ref, send_sem=send_sem, recv_sem=t_recv.at[0, 0],
            device_id=(g, sibling), device_id_type=MESH,
        ).wait_send()

    near_low = z < chips // 2

    def group_of(step):
        low = jnp.where(step < chips - 1 - z, chips - 1 - step, step - (chips - 1 - z))
        high = jnp.where(step < z, step, chips - 1 - (step - z))
        return jnp.where(step == chips - 1, z, jnp.where(near_low, low, high))

    grp_src, grp_dst = lax.rem(g, 2), g // 2
    sends_t = core == grp_src
    relays_t = core == grp_dst

    def own_copy(piece):
        return pltpu.make_async_copy(amp_cols(p, piece), t_ref.at[p, piece], t_recv.at[p, piece])

    @pl.when(sends_t)
    def _():
        @pl.loop(0, chips - 1)
        def _(step):
            to = 2 * group_of(step) + grp_dst
            for piece in range(pieces_t):
                t_copy(amp_cols(to, piece), p, piece, t_send.at[0], g, to).start()

    for piece in range(pieces_t):
        own_copy(piece).start()
        t_copy(amp_cols(sibling, piece), p, piece, t_send.at[1], g, sibling).start()

    def relay(step):
        @pl.when(relays_t)
        def _():
            slot = 2 * group_of(step) + grp_src
            for piece in range(pieces_t):
                t_wait(slot, piece)
                for hop in range(1, grps):
                    t_copy(
                        t_ref.at[slot, piece], slot, piece, t_fwd.at[hop - 1], to_grps[hop], p
                    ).start()

    def cross_copy(chunk, group):
        return pltpu.make_async_remote_copy(
            src_ref=part_ref.at[
                chunk, group, pl.ds(pl.multiple_of((1 - core) * rows, 8), rows)
            ],
            dst_ref=cross_ref.at[chunk, group], send_sem=x_send,
            recv_sem=x_recv.at[chunk, group], device_id=(g, sibling), device_id_type=MESH,
        )

    def chain_copies(chunk, step, group, side):
        to = 2 * (z + 1 - 2 * side) + core
        quanta = pltpu.make_async_remote_copy(
            src_ref=send_q.at[chunk, step], dst_ref=recv_q.at[chunk, side, group],
            send_sem=q_send, recv_sem=q_recv.at[chunk, side, group],
            device_id=(g, to), device_id_type=MESH,
        )
        scales = pltpu.make_async_remote_copy(
            src_ref=send_s.at[chunk, step], dst_ref=recv_s.at[chunk, side, group],
            send_sem=s_send, recv_sem=s_recv.at[chunk, side, group],
            device_id=(g, to), device_id_type=MESH,
        )
        return quanta, scales

    def arrived(chunk, group, side, acc):
        for copy in chain_copies(chunk, 0, group, side):
            copy.wait_recv()
        acc[:, :width] += dequantize(recv_q[chunk, side, group], recv_s[chunk, side, group])

    def own_sum(chunk, group, acc):
        cross_copy(chunk, group).wait_recv()
        mine = part_ref[chunk, group, pl.ds(pl.multiple_of(core * rows, 8), rows), :]
        acc[:, :width] = mine + cross_ref[chunk, group]

    def chain_step(chunk, step):
        group = group_of(step)
        own_sum(chunk, group, total_ref)
        side = jnp.where(group > z, 0, 1)
        first = jnp.where(side == 0, z == 0, z == chips - 1)

        @pl.when(jnp.logical_not(first))
        def _():
            arrived(chunk, group, side, total_ref)

        quanta, peak = quantize(total_ref[...])
        send_q[chunk, step] = quanta
        send_s[chunk, step] = peak
        for copy in chain_copies(chunk, step, group, side):
            copy.start()

    lag = jnp.where(jnp.logical_or(z == 0, z == chips - 1), 0, 1)
    log_step = math.log(2.0) / 256.0
    occ_pairs = [(i, j) for i in range(occ_rows) for j in range(occ_rows)]

    def mirror_copy(other):
        to_grp, to_pair = other
        return pltpu.make_async_remote_copy(
            src_ref=mirrored_ref.at[to_pair, to_grp], dst_ref=mirror_ref.at[me],
            send_sem=m_send, recv_sem=m_recv.at[p],
            device_id=(to_grp, to_pair), device_id_type=MESH,
        )

    def mirror_part(count, recv_sem):
        part = mirror_ref.at[pl.ds(0, count)]
        return pltpu.make_async_remote_copy(
            src_ref=part, dst_ref=part, send_sem=m_send, recv_sem=recv_sem,
            device_id=(g, sibling), device_id_type=MESH,
        )

    def finish_chunk(chunk):
        acc = final_ref.at[chunk]
        own_sum(chunk, z, acc)

        @pl.when(z > 0)
        def _():
            arrived(chunk, z, 0, acc)

        @pl.when(z < chips - 1)
        def _():
            arrived(chunk, z, 1, acc)

        for a in range(8):
            piece_ref[pl.ds(a, rows, stride=8), :] = final_ref[chunk, :, a * vb:a * vb + 128]

        @pl.loop(0, pairs, unroll=4)
        def _(q):
            lane = lax.broadcasted_iota(jnp.int32, (16, 128), 1)
            pieces = [
                piece_ref[
                    pl.ds(pl.multiple_of((i * occupied + q * occ_rows + j) * 8, 8), 8), :
                ]
                for i, j in occ_pairs
            ]
            for h in range(grps):
                ends = []
                for part in (pieces[:slots], pieces[slots:]):
                    packed = jnp.zeros((8, 128), jnp.float32)
                    for at, piece in enumerate(part):
                        shift = ((at - h) * lanes) % 128
                        moved = pltpu.roll(piece, shift, 1) if shift else piece
                        inside = jnp.logical_and(
                            lane[:8] >= at * lanes, lane[:8] < (at + 1) * lanes
                        )
                        packed = jnp.where(inside, moved, packed)
                    ends.append(packed)
                block = jnp.concatenate(ends, axis=0)
                peak = jnp.maximum(jnp.max(jnp.abs(block), axis=1, keepdims=True), 1e-33)
                level = jnp.floor(jnp.log(peak) * (1.0 / log_step)) + 2.0
                whole = jnp.floor(block * (STEPS * jnp.exp(level * -log_step)) + 0.5)
                whole = jnp.where(lane == 127, level, whole).astype(jnp.int32)
                mirrored_ref[q, h, 16 * chunk:16 * chunk + 16] = whole.astype(jnp.int16)

    def take_from(q, count):
        mirror_part(count, m_recv.at[q]).wait_recv()
        blocks = []
        for h in range(grps):
            for chunk in range(chunks):
                block = mirror_ref[h * pairs + q, 16 * chunk:16 * chunk + 16].astype(jnp.int32).astype(jnp.float32)
                blocks.append(block * (jnp.exp(block[:, 127:] * log_step) * (1.0 / STEPS)))
        rest = [jnp.zeros((128 - vb, 128), jnp.float32)]
        for end in range(2):
            turned = jnp.concatenate([b[8 * end:8 * end + 8] for b in blocks] + rest, axis=0).T
            for at, (i, j) in enumerate(occ_pairs[end * slots:(end + 1) * slots]):
                row = (j * occupied + q * occ_rows + i) * lanes
                split_ref[pl.ds(pl.multiple_of(row, 8), lanes), :] = (
                    turned[at * lanes:(at + 1) * lanes]
                )

    def mask_group(group):
        for piece in range(pieces_t):
            at = slice(piece * piece_cols, (piece + 1) * piece_cols)
            both = jnp.concatenate(
                [t_ref[2 * group + c, piece].astype(jnp.float32) for c in range(2)], axis=0
            )
            tt_ref[:, at] = (both * mask_ref[:1, at]).astype(jnp.bfloat16)

    def multiply(chunk, group):
        part_ref[chunk, group] = jnp.dot(
            tt_ref[...], w_ref[:, chunk * width:(chunk + 1) * width],
            preferred_element_type=jnp.float32,
        )
        cross_copy(chunk, group).start()

    for chunk in range(chunks):
        final_ref[chunk, :, width:] = jnp.zeros((rows, 128), jnp.float32)
    w_copy.wait()
    for piece in range(pieces_t):
        own_copy(piece).wait()
        t_wait(sibling, piece)
    mask_group(z)
    multiply(0, z)
    relay(0)
    for chunk in range(1, chunks):
        multiply(chunk, z)

    @pl.loop(0, chips - 1)
    def _(step):
        group = group_of(step)

        @pl.when(step < chips - 2)
        def _():
            relay(step + 1)

        for c in range(2):
            @pl.when(jnp.logical_not(jnp.logical_and(relays_t, c == grp_src)))
            def _():
                for piece in range(pieces_t):
                    t_wait(2 * group + c, piece)

        turn = step - lag
        mask_group(group)
        for chunk in range(chunks):
            multiply(chunk, group)
            if chunk > 0:
                @pl.when(turn >= 0)
                def _():
                    chain_step(chunk - 1, turn)

        @pl.when(turn >= 0)
        def _():
            chain_step(chunks - 1, turn)

    @pl.when(lag == 1)
    def _():
        @pl.loop(0, chunks)
        def _(chunk):
            chain_step(chunk, chips - 2)

    for chunk in range(chunks):
        finish_chunk(chunk)

    for other in others:
        mirror_copy(other).start()
    mirror_ref[me] = mirrored_ref[p, g]
    take_from(p, grps - 1)

    @pl.loop(1, pairs)
    def _(step):
        take_from(lax.rem(p + pairs - step, pairs), grps)

    lane = lax.broadcasted_iota(jnp.int32, (rows, vb), 1)
    for chunk in range(chunks):
        for a in range(8):
            v = chunk * 8 + a
            alive = jnp.where(g * lanes + v < live_ref[0], live_ref[0], 0)
            both = (
                final_ref[chunk, :, a * vb:(a + 1) * vb]
                + split_ref[pl.ds(v, rows, stride=lanes), :][:, :vb]
            )
            total_ref[:, a * vb:(a + 1) * vb] = jnp.where(lane < alive, both, 0.0)
        out_ref[:, chunk * width:(chunk + 1) * width] = total_ref[...].astype(jnp.bfloat16)

    @pl.when(sends_t)
    def _():
        wait_sent(t_ref.at[pl.ds(0, chips - 1)], t_send.at[0])

    wait_sent(t_ref.at[0], t_send.at[1])

    @pl.when(relays_t)
    def _():
        for hop in range(1, grps):
            wait_sent(t_ref.at[pl.ds(0, chips - 1)], t_fwd.at[hop - 1])

    wait_sent(cross_ref, x_send)
    wait_sent(send_q, q_send)
    wait_sent(send_s, s_send)
    mirror_part(devices - 1, m_recv.at[0]).wait_send()


def fused(mesh, amplitudes, integrals, live_counts):
    occ_rows, occupied, virt_pairs = amplitudes.shape
    depth, cols = integrals.shape
    grps, pairs = mesh.shape["grp"], mesh.shape["pair"]
    rows, chips, devices = occ_rows * occupied, pairs // 2, grps * pairs
    lanes = cols // VB
    chunks = lanes // 8
    width = cols // chunks
    pieces = 3 if depth % 384 == 0 else 1
    sizes = (grps, pairs, occ_rows, occupied, depth, cols, VB)
    f32, bf16, i16 = jnp.float32, jnp.bfloat16, jnp.int16
    dma = pltpu.SemaphoreType.DMA
    out = pl.pallas_call(
        functools.partial(kernel, sizes),
        out_shape=jax.ShapeDtypeStruct((rows, cols), bf16),
        in_specs=[
            pl.BlockSpec(memory_space=pltpu.SMEM),
            pl.BlockSpec(memory_space=pltpu.HBM),
            pl.BlockSpec(memory_space=pltpu.HBM),
        ],
        out_specs=pl.BlockSpec(memory_space=pltpu.VMEM),
        scratch_shapes=[
            pltpu.VMEM((depth, cols), bf16),
            pltpu.VMEM((pairs, pieces, rows, depth // pieces), bf16),
            pltpu.VMEM((2 * rows, depth), bf16),
            pltpu.VMEM((8, depth), f32),
            pltpu.VMEM((chunks, chips, 2 * rows, width), f32),
            pltpu.VMEM((chunks, chips, rows, width), f32),
            pltpu.VMEM((chunks, chips - 1, rows, width), i16),
            pltpu.VMEM((chunks, chips - 1, 1, width), f32),
            pltpu.VMEM((chunks, 2, chips, rows, width), i16),
            pltpu.VMEM((chunks, 2, chips, 1, width), f32),
            pltpu.VMEM((rows, width), f32),
            pltpu.VMEM((chunks, rows, width + 128), f32),
            pltpu.VMEM((rows * lanes, 128), f32),
            pltpu.VMEM((rows * 8, 128), f32),
            pltpu.VMEM((pairs, grps, 16 * chunks, 128), i16),
            pltpu.VMEM((devices, 16 * chunks, 128), i16),
            dma(()), dma((2,)), dma((grps - 1,)), dma((pairs, pieces)),
            dma(()), dma((chunks, chips)), dma(()), dma(()),
            dma((chunks, 2, chips)), dma((chunks, 2, chips)), dma(()), dma((pairs,)),
        ],
        compiler_params=pltpu.CompilerParams(
            collective_id=0, has_side_effects=True, vmem_limit_bytes=VMEM_BYTES
        ),
        cost_estimate=pl.CostEstimate(
            flops=4 * pairs // 2 * rows * depth * cols,
            bytes_accessed=2 * depth * cols, transcendentals=0,
        ),
    )(live_counts, amplitudes.reshape(rows, virt_pairs), integrals)
    return out.reshape(occ_rows, occupied, cols)


def gathered(mesh, amplitudes, integrals, live_counts):
    occ_rows, occupied, virt_pairs = amplitudes.shape
    my_pairs, slab_cols = integrals.shape
    tile_size = VB
    slab_lanes = slab_cols // tile_size
    rows = occ_rows * occupied
    flat_rows = lax.all_to_all(
        amplitudes.reshape(rows, virt_pairs), "pair", split_axis=1, concat_axis=0, tiled=True
    )
    position = lax.axis_index("pair") * my_pairs + jnp.arange(my_pairs)
    keep_pairs = (
        (position // tile_size < live_counts[1]) & (position % tile_size < live_counts[1])
    ).astype(jnp.bfloat16)
    partial = jnp.dot(flat_rows * keep_pairs, integrals, preferred_element_type=jnp.float32)
    ladder = lax.psum_scatter(partial, "pair", scatter_dimension=0, tiled=True)
    blocks = ladder.reshape(occ_rows, occupied, slab_lanes, tile_size)
    mirrored = lax.all_to_all(
        lax.all_to_all(blocks, "grp", split_axis=3, concat_axis=2, tiled=True),
        "pair",
        split_axis=1,
        concat_axis=0,
        tiled=True,
    )
    summed = blocks + jnp.transpose(mirrored, (1, 0, 3, 2))
    first_virt = lax.axis_index("grp") * slab_lanes + jnp.arange(slab_lanes)
    second_virt = jnp.arange(tile_size)
    keep_out = (
        (first_virt[:, None] < live_counts[0]) & (second_virt[None, :] < live_counts[0])
    ).astype(jnp.float32)
    return (summed * keep_out).reshape(occ_rows, occupied, slab_cols).astype(jnp.bfloat16)


def on_device(mesh, amplitudes, integrals, live_counts):
    occ_rows, occupied, virt_pairs = amplitudes.shape
    depth, cols = integrals.shape
    rows, pairs = occ_rows * occupied, mesh.shape["pair"]
    held = 2 * depth * cols + rows * cols * (8 * pairs + 8) + 6 * rows * virt_pairs
    lanes = cols // VB
    packs = lanes % 8 == 0 and occ_rows * occ_rows <= 2 * (127 // lanes)
    fits = held < VMEM_BYTES and mesh.shape["grp"] == 4 and packs
    return (fused if fits else gathered)(mesh, amplitudes, integrals, live_counts)


def solution(mesh):
    return jax.shard_map(
        functools.partial(on_device, mesh),
        mesh=mesh,
        in_specs=(P("pair", None, None), P("pair", "grp"), P()),
        out_specs=P("pair", None, "grp"),
        check_vma=False,
    )
```

```python
import functools
import math

import jax
import jax.numpy as jnp
from jax import lax
from jax.experimental import pallas as pl
from jax.experimental.pallas import tpu as pltpu
from jax.sharding import PartitionSpec as P

VB = 96
STEPS = 32767.0
MESH = pl.DeviceIdType.MESH
VMEM_BYTES = 58 * 2**20


def quantize(value):
    peak = jnp.maximum(jnp.max(jnp.abs(value), axis=0, keepdims=True), 1e-33)
    whole = jnp.floor(value * (STEPS / peak) + 0.5).astype(jnp.int32)
    return whole.astype(jnp.int16), peak


def dequantize(quanta, peak):
    return quanta.astype(jnp.int32).astype(jnp.float32) * (peak * (1.0 / STEPS))


def kernel(
    sizes, live_ref, amp_ref, w_hbm, out_ref,
    w_ref, t_ref, tt_ref, mask_ref, part_ref, cross_ref, send_q, send_s,
    recv_q, recv_s, total_ref, final_ref, split_ref, piece_ref, mirrored_ref, mirror_ref,
    w_sem, t_send, t_fwd, t_recv, x_send, x_recv, q_send, s_send, q_recv, s_recv, m_send, m_recv,
):
    grps, pairs, occ_rows, occupied, depth, cols, vb = sizes
    chips = pairs // 2
    rows = occ_rows * occupied
    lanes = cols // vb
    chunks, slots = lanes // 8, 127 // lanes
    width = cols // chunks
    devices = grps * pairs
    g, p = lax.axis_index("grp"), lax.axis_index("pair")
    z, core = p // 2, p % 2
    sibling = 2 * z + 1 - core
    me = g * pairs + p

    barrier = pltpu.get_barrier_semaphore()

    to_grps = [lax.rem(g + n, grps) for n in range(grps)]
    to_pairs = [lax.rem(p + n, pairs) for n in range(pairs)]
    far_first = sorted(range(pairs), key=lambda m: (abs(m - pairs // 2), m))
    others = [(to_grps[n], to_pairs[m]) for m in far_first for n in range(grps) if n or m]
    for other in others:
        pl.semaphore_signal(barrier, inc=1, device_id=other, device_id_type=MESH)

    w_copy = pltpu.make_async_copy(w_hbm, w_ref, w_sem)
    w_copy.start()
    for c in range(depth // vb):
        alive = jnp.where(p * (depth // vb) + c < live_ref[1], live_ref[1], 0)
        lane = lax.broadcasted_iota(jnp.int32, (8, vb), 1)
        mask_ref[:, c * vb:(c + 1) * vb] = jnp.where(lane < alive, 1.0, 0.0)
    pl.semaphore_wait(barrier, devices - 1)

    pieces_t = t_ref.shape[1]
    piece_cols = depth // pieces_t

    def amp_cols(pair, piece):
        return amp_ref.at[
            :, pl.ds(pl.multiple_of(pair * depth + piece * piece_cols, 128), piece_cols)
        ]

    def t_copy(src, slot, piece, send_sem, to_grp, to_pair):
        return pltpu.make_async_remote_copy(
            src_ref=src, dst_ref=t_ref.at[slot, piece], send_sem=send_sem,
            recv_sem=t_recv.at[slot, piece],
            device_id=(to_grp, to_pair), device_id_type=MESH,
        )

    def t_wait(slot, piece):
        t_copy(t_ref.at[slot, piece], slot, piece, t_send.at[0], g, sibling).wait_recv()

    def wait_sent(ref, send_sem):
        pltpu.make_async_remote_copy(
            src_ref=ref, dst_ref=ref, send_sem=send_sem, recv_sem=t_recv.at[0, 0],
            device_id=(g, sibling), device_id_type=MESH,
        ).wait_send()

    near_low = z < chips // 2

    def group_of(step):
        low = jnp.where(step < chips - 1 - z, chips - 1 - step, step - (chips - 1 - z))
        high = jnp.where(step < z, step, chips - 1 - (step - z))
        return jnp.where(step == chips - 1, z, jnp.where(near_low, low, high))

    grp_src, grp_dst = lax.rem(g, 2), g // 2
    sends_t = core == grp_src
    relays_t = core == grp_dst

    def own_copy(piece):
        return pltpu.make_async_copy(amp_cols(p, piece), t_ref.at[p, piece], t_recv.at[p, piece])

    @pl.when(sends_t)
    def _():
        @pl.loop(0, chips - 1)
        def _(step):
            to = 2 * group_of(step) + grp_dst
            for piece in range(pieces_t):
                t_copy(amp_cols(to, piece), p, piece, t_send.at[0], g, to).start()

    for piece in range(pieces_t):
        own_copy(piece).start()
        t_copy(amp_cols(sibling, piece), p, piece, t_send.at[1], g, sibling).start()

    def relay(step):
        @pl.when(relays_t)
        def _():
            slot = 2 * group_of(step) + grp_src
            for piece in range(pieces_t):
                t_wait(slot, piece)
                for hop in range(1, grps):
                    t_copy(
                        t_ref.at[slot, piece], slot, piece, t_fwd.at[hop - 1], to_grps[hop], p
                    ).start()

    def cross_copy(chunk, group):
        return pltpu.make_async_remote_copy(
            src_ref=part_ref.at[
                chunk, group, pl.ds(pl.multiple_of((1 - core) * rows, 8), rows)
            ],
            dst_ref=cross_ref.at[chunk, group], send_sem=x_send,
            recv_sem=x_recv.at[chunk, group], device_id=(g, sibling), device_id_type=MESH,
        )

    def chain_copies(chunk, step, group, side):
        to = 2 * (z + 1 - 2 * side) + core
        quanta = pltpu.make_async_remote_copy(
            src_ref=send_q.at[chunk, step], dst_ref=recv_q.at[chunk, side, group],
            send_sem=q_send, recv_sem=q_recv.at[chunk, side, group],
            device_id=(g, to), device_id_type=MESH,
        )
        scales = pltpu.make_async_remote_copy(
            src_ref=send_s.at[chunk, step], dst_ref=recv_s.at[chunk, side, group],
            send_sem=s_send, recv_sem=s_recv.at[chunk, side, group],
            device_id=(g, to), device_id_type=MESH,
        )
        return quanta, scales

    def arrived(chunk, group, side, acc):
        for copy in chain_copies(chunk, 0, group, side):
            copy.wait_recv()
        acc[:, :width] += dequantize(recv_q[chunk, side, group], recv_s[chunk, side, group])

    def own_sum(chunk, group, acc):
        cross_copy(chunk, group).wait_recv()
        mine = part_ref[chunk, group, pl.ds(pl.multiple_of(core * rows, 8), rows), :]
        acc[:, :width] = mine + cross_ref[chunk, group]

    def chain_step(chunk, step):
        group = group_of(step)
        own_sum(chunk, group, total_ref)
        side = jnp.where(group > z, 0, 1)
        first = jnp.where(side == 0, z == 0, z == chips - 1)

        @pl.when(jnp.logical_not(first))
        def _():
            arrived(chunk, group, side, total_ref)

        quanta, peak = quantize(total_ref[...])
        send_q[chunk, step] = quanta
        send_s[chunk, step] = peak
        for copy in chain_copies(chunk, step, group, side):
            copy.start()

    lag = jnp.where(jnp.logical_or(z == 0, z == chips - 1), 0, 1)
    log_step = math.log(2.0) / 256.0
    occ_pairs = [(i, j) for i in range(occ_rows) for j in range(occ_rows)]

    def mirror_copy(other):
        to_grp, to_pair = other
        return pltpu.make_async_remote_copy(
            src_ref=mirrored_ref.at[to_pair, to_grp], dst_ref=mirror_ref.at[me],
            send_sem=m_send, recv_sem=m_recv.at[p],
            device_id=(to_grp, to_pair), device_id_type=MESH,
        )

    def mirror_part(count, recv_sem):
        part = mirror_ref.at[pl.ds(0, count)]
        return pltpu.make_async_remote_copy(
            src_ref=part, dst_ref=part, send_sem=m_send, recv_sem=recv_sem,
            device_id=(g, sibling), device_id_type=MESH,
        )

    def finish_chunk(chunk):
        acc = final_ref.at[chunk]
        own_sum(chunk, z, acc)

        @pl.when(z > 0)
        def _():
            arrived(chunk, z, 0, acc)

        @pl.when(z < chips - 1)
        def _():
            arrived(chunk, z, 1, acc)

        for a in range(8):
            piece_ref[pl.ds(a, rows, stride=8), :] = final_ref[chunk, :, a * vb:a * vb + 128]

        @pl.loop(0, pairs, unroll=4)
        def _(q):
            lane = lax.broadcasted_iota(jnp.int32, (16, 128), 1)
            pieces = [
                piece_ref[
                    pl.ds(pl.multiple_of((i * occupied + q * occ_rows + j) * 8, 8), 8), :
                ]
                for i, j in occ_pairs
            ]
            for h in range(grps):
                ends = []
                for part in (pieces[:slots], pieces[slots:]):
                    packed = jnp.zeros((8, 128), jnp.float32)
                    for at, piece in enumerate(part):
                        shift = ((at - h) * lanes) % 128
                        moved = pltpu.roll(piece, shift, 1) if shift else piece
                        inside = jnp.logical_and(
                            lane[:8] >= at * lanes, lane[:8] < (at + 1) * lanes
                        )
                        packed = jnp.where(inside, moved, packed)
                    ends.append(packed)
                block = jnp.concatenate(ends, axis=0)
                peak = jnp.maximum(jnp.max(jnp.abs(block), axis=1, keepdims=True), 1e-33)
                level = jnp.floor(jnp.log(peak) * (1.0 / log_step)) + 2.0
                whole = jnp.floor(block * (STEPS * jnp.exp(level * -log_step)) + 0.5)
                whole = jnp.where(lane == 127, level, whole).astype(jnp.int32)
                mirrored_ref[q, h, 16 * chunk:16 * chunk + 16] = whole.astype(jnp.int16)

    def take_from(q, count):
        mirror_part(count, m_recv.at[q]).wait_recv()
        blocks = []
        for h in range(grps):
            for chunk in range(chunks):
                block = mirror_ref[h * pairs + q, 16 * chunk:16 * chunk + 16]
                block = block.astype(jnp.int32).astype(jnp.float32)
                blocks.append(block * (jnp.exp(block[:, 127:] * log_step) * (1.0 / STEPS)))
        rest = [jnp.zeros((128 - vb, 128), jnp.float32)]
        for end in range(2):
            turned = jnp.concatenate([b[8 * end:8 * end + 8] for b in blocks] + rest, axis=0).T
            for at, (i, j) in enumerate(occ_pairs[end * slots:(end + 1) * slots]):
                row = (j * occupied + q * occ_rows + i) * lanes
                split_ref[pl.ds(pl.multiple_of(row, 8), lanes), :] = (
                    turned[at * lanes:(at + 1) * lanes]
                )

    def mask_group(group):
        for piece in range(pieces_t):
            at = slice(piece * piece_cols, (piece + 1) * piece_cols)
            both = jnp.concatenate(
                [t_ref[2 * group + c, piece].astype(jnp.float32) for c in range(2)], axis=0
            )
            tt_ref[:, at] = (both * mask_ref[:1, at]).astype(jnp.bfloat16)

    def multiply(chunk, group):
        part_ref[chunk, group] = jnp.dot(
            tt_ref[...], w_ref[:, chunk * width:(chunk + 1) * width],
            preferred_element_type=jnp.float32,
        )
        cross_copy(chunk, group).start()

    for chunk in range(chunks):
        final_ref[chunk, :, width:] = jnp.zeros((rows, 128), jnp.float32)
    relay(0)
    w_copy.wait()
    for piece in range(pieces_t):
        own_copy(piece).wait()
        t_wait(sibling, piece)
    mask_group(z)
    for chunk in range(chunks):
        multiply(chunk, z)

    @pl.loop(0, chips - 1)
    def _(step):
        group = group_of(step)

        @pl.when(step < chips - 2)
        def _():
            relay(step + 1)

        for c in range(2):
            @pl.when(jnp.logical_not(jnp.logical_and(relays_t, c == grp_src)))
            def _():
                for piece in range(pieces_t):
                    t_wait(2 * group + c, piece)

        turn = step - lag
        mask_group(group)
        for chunk in range(chunks):
            multiply(chunk, group)
            if chunk > 0:
                @pl.when(turn >= 0)
                def _():
                    chain_step(chunk - 1, turn)

        @pl.when(turn >= 0)
        def _():
            chain_step(chunks - 1, turn)

    @pl.when(lag == 1)
    def _():
        @pl.loop(0, chunks)
        def _(chunk):
            chain_step(chunk, chips - 2)

    for chunk in range(chunks):
        finish_chunk(chunk)

    for other in others:
        mirror_copy(other).start()
    mirror_ref[me] = mirrored_ref[p, g]
    for m in far_first:
        take_from(lax.rem(p + pairs - m, pairs), grps if m else grps - 1)

    lane = lax.broadcasted_iota(jnp.int32, (rows, vb), 1)
    for chunk in range(chunks):
        for a in range(8):
            v = chunk * 8 + a
            alive = jnp.where(g * lanes + v < live_ref[0], live_ref[0], 0)
            both = (
                final_ref[chunk, :, a * vb:(a + 1) * vb]
                + split_ref[pl.ds(v, rows, stride=lanes), :][:, :vb]
            )
            total_ref[:, a * vb:(a + 1) * vb] = jnp.where(lane < alive, both, 0.0)
        out_ref[:, chunk * width:(chunk + 1) * width] = total_ref[...].astype(jnp.bfloat16)

    @pl.when(sends_t)
    def _():
        wait_sent(t_ref.at[pl.ds(0, chips - 1)], t_send.at[0])

    wait_sent(t_ref.at[0], t_send.at[1])

    @pl.when(relays_t)
    def _():
        for hop in range(1, grps):
            wait_sent(t_ref.at[pl.ds(0, chips - 1)], t_fwd.at[hop - 1])

    wait_sent(cross_ref, x_send)
    wait_sent(send_q, q_send)
    wait_sent(send_s, s_send)
    mirror_part(devices - 1, m_recv.at[0]).wait_send()


def fused(mesh, amplitudes, integrals, live_counts):
    occ_rows, occupied, virt_pairs = amplitudes.shape
    depth, cols = integrals.shape
    grps, pairs = mesh.shape["grp"], mesh.shape["pair"]
    rows, chips, devices = occ_rows * occupied, pairs // 2, grps * pairs
    lanes = cols // VB
    chunks = lanes // 8
    width = cols // chunks
    pieces = 3 if depth % 384 == 0 else 1
    sizes = (grps, pairs, occ_rows, occupied, depth, cols, VB)
    f32, bf16, i16 = jnp.float32, jnp.bfloat16, jnp.int16
    dma = pltpu.SemaphoreType.DMA
    out = pl.pallas_call(
        functools.partial(kernel, sizes),
        out_shape=jax.ShapeDtypeStruct((rows, cols), bf16),
        in_specs=[
            pl.BlockSpec(memory_space=pltpu.SMEM),
            pl.BlockSpec(memory_space=pltpu.HBM),
            pl.BlockSpec(memory_space=pltpu.HBM),
        ],
        out_specs=pl.BlockSpec(memory_space=pltpu.VMEM),
        scratch_shapes=[
            pltpu.VMEM((depth, cols), bf16),
            pltpu.VMEM((pairs, pieces, rows, depth // pieces), bf16),
            pltpu.VMEM((2 * rows, depth), bf16),
            pltpu.VMEM((8, depth), f32),
            pltpu.VMEM((chunks, chips, 2 * rows, width), f32),
            pltpu.VMEM((chunks, chips, rows, width), f32),
            pltpu.VMEM((chunks, chips - 1, rows, width), i16),
            pltpu.VMEM((chunks, chips - 1, 1, width), f32),
            pltpu.VMEM((chunks, 2, chips, rows, width), i16),
            pltpu.VMEM((chunks, 2, chips, 1, width), f32),
            pltpu.VMEM((rows, width), f32),
            pltpu.VMEM((chunks, rows, width + 128), f32),
            pltpu.VMEM((rows * lanes, 128), f32),
            pltpu.VMEM((rows * 8, 128), f32),
            pltpu.VMEM((pairs, grps, 16 * chunks, 128), i16),
            pltpu.VMEM((devices, 16 * chunks, 128), i16),
            dma(()), dma((2,)), dma((grps - 1,)), dma((pairs, pieces)),
            dma(()), dma((chunks, chips)), dma(()), dma(()),
            dma((chunks, 2, chips)), dma((chunks, 2, chips)), dma(()), dma((pairs,)),
        ],
        compiler_params=pltpu.CompilerParams(
            collective_id=0, has_side_effects=True, vmem_limit_bytes=VMEM_BYTES
        ),
        cost_estimate=pl.CostEstimate(
            flops=4 * pairs // 2 * rows * depth * cols,
            bytes_accessed=2 * depth * cols, transcendentals=0,
        ),
    )(live_counts, amplitudes.reshape(rows, virt_pairs), integrals)
    return out.reshape(occ_rows, occupied, cols)


def gathered(mesh, amplitudes, integrals, live_counts):
    occ_rows, occupied, virt_pairs = amplitudes.shape
    my_pairs, slab_cols = integrals.shape
    tile_size = VB
    slab_lanes = slab_cols // tile_size
    rows = occ_rows * occupied
    flat_rows = lax.all_to_all(
        amplitudes.reshape(rows, virt_pairs), "pair", split_axis=1, concat_axis=0, tiled=True
    )
    position = lax.axis_index("pair") * my_pairs + jnp.arange(my_pairs)
    keep_pairs = (
        (position // tile_size < live_counts[1]) & (position % tile_size < live_counts[1])
    ).astype(jnp.bfloat16)
    partial = jnp.dot(flat_rows * keep_pairs, integrals, preferred_element_type=jnp.float32)
    ladder = lax.psum_scatter(partial, "pair", scatter_dimension=0, tiled=True)
    blocks = ladder.reshape(occ_rows, occupied, slab_lanes, tile_size)
    mirrored = lax.all_to_all(
        lax.all_to_all(blocks, "grp", split_axis=3, concat_axis=2, tiled=True),
        "pair",
        split_axis=1,
        concat_axis=0,
        tiled=True,
    )
    summed = blocks + jnp.transpose(mirrored, (1, 0, 3, 2))
    first_virt = lax.axis_index("grp") * slab_lanes + jnp.arange(slab_lanes)
    second_virt = jnp.arange(tile_size)
    keep_out = (
        (first_virt[:, None] < live_counts[0]) & (second_virt[None, :] < live_counts[0])
    ).astype(jnp.float32)
    return (summed * keep_out).reshape(occ_rows, occupied, slab_cols).astype(jnp.bfloat16)


def on_device(mesh, amplitudes, integrals, live_counts):
    occ_rows, occupied, virt_pairs = amplitudes.shape
    depth, cols = integrals.shape
    rows, pairs = occ_rows * occupied, mesh.shape["pair"]
    held = 2 * depth * cols + rows * cols * (8 * pairs + 8) + 6 * rows * virt_pairs
    lanes = cols // VB
    packs = lanes % 8 == 0 and occ_rows * occ_rows <= 2 * (127 // lanes)
    fits = held < VMEM_BYTES and mesh.shape["grp"] == 4 and packs
    return (fused if fits else gathered)(mesh, amplitudes, integrals, live_counts)


def solution(mesh):
    return jax.shard_map(
        functools.partial(on_device, mesh),
        mesh=mesh,
        in_specs=(P("pair", None, None), P("pair", "grp"), P()),
        out_specs=P("pair", None, "grp"),
        check_vma=False,
    )
```

```python
import functools
import math

import jax
import jax.numpy as jnp
from jax import lax
from jax.experimental import pallas as pl
from jax.experimental.pallas import tpu as pltpu
from jax.sharding import PartitionSpec as P

VB = 96
STEPS = 32767.0
MESH = pl.DeviceIdType.MESH
VMEM_BYTES = 58 * 2**20


def quantize(value):
    peak = jnp.maximum(jnp.max(jnp.abs(value), axis=0, keepdims=True), 1e-33)
    whole = jnp.floor(value * (STEPS / peak) + 0.5).astype(jnp.int32)
    return whole.astype(jnp.int16), peak


def dequantize(quanta, peak):
    return quanta.astype(jnp.int32).astype(jnp.float32) * (peak * (1.0 / STEPS))


def kernel(
    sizes, live_ref, amp_ref, w_hbm, out_ref,
    w_ref, t_ref, tt_ref, mask_ref, part_ref, cross_ref, send_q, send_s,
    recv_q, recv_s, total_ref, final_ref, split_ref, piece_ref, mirrored_ref, mirror_ref,
    w_sem, t_send, t_fwd, t_recv, x_send, x_recv, q_send, s_send, q_recv, s_recv, m_send, m_recv,
):
    grps, pairs, occ_rows, occupied, depth, cols, vb = sizes
    chips = pairs // 2
    rows = occ_rows * occupied
    lanes = cols // vb
    chunks, slots = lanes // 8, 127 // lanes
    width = cols // chunks
    devices = grps * pairs
    g, p = lax.axis_index("grp"), lax.axis_index("pair")
    z, core = p // 2, p % 2
    sibling = 2 * z + 1 - core
    me = g * pairs + p

    w_copy = pltpu.make_async_copy(w_hbm, w_ref, w_sem)
    w_copy.start()
    barrier = pltpu.get_barrier_semaphore()

    to_grps = [lax.rem(g + n, grps) for n in range(grps)]
    to_pairs = [lax.rem(p + n, pairs) for n in range(pairs)]
    others = [(to_grps[n], to_pairs[m]) for m in range(pairs) for n in range(grps)][1:]
    for other in others:
        pl.semaphore_signal(barrier, inc=1, device_id=other, device_id_type=MESH)

    for c in range(depth // vb):
        alive = jnp.where(p * (depth // vb) + c < live_ref[1], live_ref[1], 0)
        lane = lax.broadcasted_iota(jnp.int32, (8, vb), 1)
        mask_ref[:, c * vb:(c + 1) * vb] = jnp.where(lane < alive, 1.0, 0.0)
    for chunk in range(chunks):
        final_ref[chunk, :, width:] = jnp.zeros((rows, 128), jnp.float32)
    pl.semaphore_wait(barrier, devices - 1)

    pieces_t = t_ref.shape[1]
    piece_cols = depth // pieces_t

    def amp_cols(pair, piece):
        return amp_ref.at[
            :, pl.ds(pl.multiple_of(pair * depth + piece * piece_cols, 128), piece_cols)
        ]

    def t_copy(src, slot, piece, send_sem, to_grp, to_pair):
        return pltpu.make_async_remote_copy(
            src_ref=src, dst_ref=t_ref.at[slot, piece], send_sem=send_sem,
            recv_sem=t_recv.at[slot, piece],
            device_id=(to_grp, to_pair), device_id_type=MESH,
        )

    def t_wait(slot, piece):
        t_copy(t_ref.at[slot, piece], slot, piece, t_send.at[0], g, sibling).wait_recv()

    def wait_sent(ref, send_sem):
        pltpu.make_async_remote_copy(
            src_ref=ref, dst_ref=ref, send_sem=send_sem, recv_sem=t_recv.at[0, 0],
            device_id=(g, sibling), device_id_type=MESH,
        ).wait_send()

    near_low = z < chips // 2

    def group_of(step):
        low = jnp.where(step < chips - 1 - z, chips - 1 - step, step - (chips - 1 - z))
        high = jnp.where(step < z, step, chips - 1 - (step - z))
        return jnp.where(step == chips - 1, z, jnp.where(near_low, low, high))

    grp_src, grp_dst = lax.rem(g, 2), g // 2
    sends_t = core == grp_src
    relays_t = core == grp_dst

    def own_copy(piece):
        return pltpu.make_async_copy(amp_cols(p, piece), t_ref.at[p, piece], t_recv.at[p, piece])

    @pl.when(sends_t)
    def _():
        @pl.loop(0, chips - 1)
        def _(step):
            to = 2 * group_of(step) + grp_dst
            for piece in range(pieces_t):
                t_copy(amp_cols(to, piece), p, piece, t_send.at[0], g, to).start()

    for piece in range(pieces_t):
        own_copy(piece).start()
        t_copy(amp_cols(sibling, piece), p, piece, t_send.at[1], g, sibling).start()

    def relay(step):
        @pl.when(relays_t)
        def _():
            slot = 2 * group_of(step) + grp_src
            for piece in range(pieces_t):
                t_wait(slot, piece)
                for hop in range(1, grps):
                    t_copy(
                        t_ref.at[slot, piece], slot, piece, t_fwd.at[hop - 1], to_grps[hop], p
                    ).start()

    def cross_copy(chunk, group):
        return pltpu.make_async_remote_copy(
            src_ref=part_ref.at[
                chunk, group, pl.ds(pl.multiple_of((1 - core) * rows, 8), rows)
            ],
            dst_ref=cross_ref.at[chunk, group], send_sem=x_send,
            recv_sem=x_recv.at[chunk, group], device_id=(g, sibling), device_id_type=MESH,
        )

    def chain_copies(chunk, step, group, side):
        to = 2 * (z + 1 - 2 * side) + core
        quanta = pltpu.make_async_remote_copy(
            src_ref=send_q.at[chunk, step], dst_ref=recv_q.at[chunk, side, group],
            send_sem=q_send, recv_sem=q_recv.at[chunk, side, group],
            device_id=(g, to), device_id_type=MESH,
        )
        scales = pltpu.make_async_remote_copy(
            src_ref=send_s.at[chunk, step], dst_ref=recv_s.at[chunk, side, group],
            send_sem=s_send, recv_sem=s_recv.at[chunk, side, group],
            device_id=(g, to), device_id_type=MESH,
        )
        return quanta, scales

    def arrived(chunk, group, side, acc):
        for copy in chain_copies(chunk, 0, group, side):
            copy.wait_recv()
        acc[:, :width] += dequantize(recv_q[chunk, side, group], recv_s[chunk, side, group])

    def own_sum(chunk, group, acc):
        cross_copy(chunk, group).wait_recv()
        mine = part_ref[chunk, group, pl.ds(pl.multiple_of(core * rows, 8), rows), :]
        acc[:, :width] = mine + cross_ref[chunk, group]

    def chain_step(chunk, step):
        group = group_of(step)
        own_sum(chunk, group, total_ref)
        side = jnp.where(group > z, 0, 1)
        first = jnp.where(side == 0, z == 0, z == chips - 1)

        @pl.when(jnp.logical_not(first))
        def _():
            arrived(chunk, group, side, total_ref)

        quanta, peak = quantize(total_ref[...])
        send_q[chunk, step] = quanta
        send_s[chunk, step] = peak
        for copy in chain_copies(chunk, step, group, side):
            copy.start()

    lag = jnp.where(jnp.logical_or(z == 0, z == chips - 1), 0, 1)
    log_step = math.log(2.0) / 256.0
    occ_pairs = [(i, j) for i in range(occ_rows) for j in range(occ_rows)]

    def mirror_copy(other):
        to_grp, to_pair = other
        return pltpu.make_async_remote_copy(
            src_ref=mirrored_ref.at[to_pair, to_grp], dst_ref=mirror_ref.at[me],
            send_sem=m_send, recv_sem=m_recv.at[p],
            device_id=(to_grp, to_pair), device_id_type=MESH,
        )

    def mirror_part(count, recv_sem):
        part = mirror_ref.at[pl.ds(0, count)]
        return pltpu.make_async_remote_copy(
            src_ref=part, dst_ref=part, send_sem=m_send, recv_sem=recv_sem,
            device_id=(g, sibling), device_id_type=MESH,
        )

    def finish_chunk(chunk):
        acc = final_ref.at[chunk]
        own_sum(chunk, z, acc)

        @pl.when(z > 0)
        def _():
            arrived(chunk, z, 0, acc)

        @pl.when(z < chips - 1)
        def _():
            arrived(chunk, z, 1, acc)

        for a in range(8):
            piece_ref[pl.ds(a, rows, stride=8), :] = final_ref[chunk, :, a * vb:a * vb + 128]

        @pl.loop(0, pairs, unroll=4)
        def _(q):
            lane = lax.broadcasted_iota(jnp.int32, (16, 128), 1)
            pieces = [
                piece_ref[
                    pl.ds(pl.multiple_of((i * occupied + q * occ_rows + j) * 8, 8), 8), :
                ]
                for i, j in occ_pairs
            ]
            for h in range(grps):
                ends = []
                for part in (pieces[:slots], pieces[slots:]):
                    packed = jnp.zeros((8, 128), jnp.float32)
                    for at, piece in enumerate(part):
                        shift = ((at - h) * lanes) % 128
                        moved = pltpu.roll(piece, shift, 1) if shift else piece
                        inside = jnp.logical_and(
                            lane[:8] >= at * lanes, lane[:8] < (at + 1) * lanes
                        )
                        packed = jnp.where(inside, moved, packed)
                    ends.append(packed)
                block = jnp.concatenate(ends, axis=0)
                peak = jnp.maximum(jnp.max(jnp.abs(block), axis=1, keepdims=True), 1e-33)
                level = jnp.floor(jnp.log(peak) * (1.0 / log_step)) + 2.0
                whole = jnp.floor(block * (STEPS * jnp.exp(level * -log_step)) + 0.5)
                whole = jnp.where(lane == 127, level, whole).astype(jnp.int32)
                mirrored_ref[q, h, 16 * chunk:16 * chunk + 16] = whole.astype(jnp.int16)

    def take_from(q, count):
        mirror_part(count, m_recv.at[q]).wait_recv()
        blocks = []
        for h in range(grps):
            for chunk in range(chunks):
                block = mirror_ref[h * pairs + q, 16 * chunk:16 * chunk + 16].astype(jnp.int32).astype(jnp.float32)
                blocks.append(block * (jnp.exp(block[:, 127:] * log_step) * (1.0 / STEPS)))
        rest = [jnp.zeros((128 - vb, 128), jnp.float32)]
        for end in range(2):
            turned = jnp.concatenate([b[8 * end:8 * end + 8] for b in blocks] + rest, axis=0).T
            for at, (i, j) in enumerate(occ_pairs[end * slots:(end + 1) * slots]):
                row = (j * occupied + q * occ_rows + i) * lanes
                split_ref[pl.ds(pl.multiple_of(row, 8), lanes), :] = (
                    turned[at * lanes:(at + 1) * lanes]
                )

    def mask_group(group):
        for piece in range(pieces_t):
            at = slice(piece * piece_cols, (piece + 1) * piece_cols)
            both = jnp.concatenate(
                [t_ref[2 * group + c, piece].astype(jnp.float32) for c in range(2)], axis=0
            )
            tt_ref[:, at] = (both * mask_ref[:1, at]).astype(jnp.bfloat16)

    def multiply(chunk, group):
        part_ref[chunk, group] = jnp.dot(
            tt_ref[...], w_ref[:, chunk * width:(chunk + 1) * width],
            preferred_element_type=jnp.float32,
        )
        cross_copy(chunk, group).start()

    w_copy.wait()
    for piece in range(pieces_t):
        own_copy(piece).wait()
        t_wait(sibling, piece)
    mask_group(z)
    multiply(0, z)
    relay(0)
    for chunk in range(1, chunks):
        multiply(chunk, z)

    @pl.loop(0, chips - 1)
    def _(step):
        group = group_of(step)

        @pl.when(step < chips - 2)
        def _():
            relay(step + 1)

        for c in range(2):
            @pl.when(jnp.logical_not(jnp.logical_and(relays_t, c == grp_src)))
            def _():
                for piece in range(pieces_t):
                    t_wait(2 * group + c, piece)

        turn = step - lag
        mask_group(group)
        for chunk in range(chunks):
            multiply(chunk, group)
            if chunk > 0:
                @pl.when(turn >= 0)
                def _():
                    chain_step(chunk - 1, turn)

        @pl.when(turn >= 0)
        def _():
            chain_step(chunks - 1, turn)

    @pl.when(lag == 1)
    def _():
        @pl.loop(0, chunks)
        def _(chunk):
            chain_step(chunk, chips - 2)

    for chunk in range(chunks):
        finish_chunk(chunk)

    for other in others:
        mirror_copy(other).start()
    mirror_ref[me] = mirrored_ref[p, g]
    take_from(p, grps - 1)

    @pl.loop(1, pairs)
    def _(step):
        take_from(lax.rem(p + pairs - step, pairs), grps)

    lane = lax.broadcasted_iota(jnp.int32, (rows, vb), 1)
    for chunk in range(chunks):
        for a in range(8):
            v = chunk * 8 + a
            alive = jnp.where(g * lanes + v < live_ref[0], live_ref[0], 0)
            both = (
                final_ref[chunk, :, a * vb:(a + 1) * vb]
                + split_ref[pl.ds(v, rows, stride=lanes), :][:, :vb]
            )
            total_ref[:, a * vb:(a + 1) * vb] = jnp.where(lane < alive, both, 0.0)
        out_ref[:, chunk * width:(chunk + 1) * width] = total_ref[...].astype(jnp.bfloat16)

    @pl.when(sends_t)
    def _():
        wait_sent(t_ref.at[pl.ds(0, chips - 1)], t_send.at[0])

    wait_sent(t_ref.at[0], t_send.at[1])

    @pl.when(relays_t)
    def _():
        for hop in range(1, grps):
            wait_sent(t_ref.at[pl.ds(0, chips - 1)], t_fwd.at[hop - 1])

    wait_sent(cross_ref, x_send)
    wait_sent(send_q, q_send)
    wait_sent(send_s, s_send)
    mirror_part(devices - 1, m_recv.at[0]).wait_send()


def fused(mesh, amplitudes, integrals, live_counts):
    occ_rows, occupied, virt_pairs = amplitudes.shape
    depth, cols = integrals.shape
    grps, pairs = mesh.shape["grp"], mesh.shape["pair"]
    rows, chips, devices = occ_rows * occupied, pairs // 2, grps * pairs
    lanes = cols // VB
    chunks = lanes // 8
    width = cols // chunks
    pieces = 3 if depth % 384 == 0 else 1
    sizes = (grps, pairs, occ_rows, occupied, depth, cols, VB)
    f32, bf16, i16 = jnp.float32, jnp.bfloat16, jnp.int16
    dma = pltpu.SemaphoreType.DMA
    out = pl.pallas_call(
        functools.partial(kernel, sizes),
        out_shape=jax.ShapeDtypeStruct((rows, cols), bf16),
        in_specs=[
            pl.BlockSpec(memory_space=pltpu.SMEM),
            pl.BlockSpec(memory_space=pltpu.HBM),
            pl.BlockSpec(memory_space=pltpu.HBM),
        ],
        out_specs=pl.BlockSpec(memory_space=pltpu.VMEM),
        scratch_shapes=[
            pltpu.VMEM((depth, cols), bf16),
            pltpu.VMEM((pairs, pieces, rows, depth // pieces), bf16),
            pltpu.VMEM((2 * rows, depth), bf16),
            pltpu.VMEM((8, depth), f32),
            pltpu.VMEM((chunks, chips, 2 * rows, width), f32),
            pltpu.VMEM((chunks, chips, rows, width), f32),
            pltpu.VMEM((chunks, chips - 1, rows, width), i16),
            pltpu.VMEM((chunks, chips - 1, 1, width), f32),
            pltpu.VMEM((chunks, 2, chips, rows, width), i16),
            pltpu.VMEM((chunks, 2, chips, 1, width), f32),
            pltpu.VMEM((rows, width), f32),
            pltpu.VMEM((chunks, rows, width + 128), f32),
            pltpu.VMEM((rows * lanes, 128), f32),
            pltpu.VMEM((rows * 8, 128), f32),
            pltpu.VMEM((pairs, grps, 16 * chunks, 128), i16),
            pltpu.VMEM((devices, 16 * chunks, 128), i16),
            dma(()), dma((2,)), dma((grps - 1,)), dma((pairs, pieces)),
            dma(()), dma((chunks, chips)), dma(()), dma(()),
            dma((chunks, 2, chips)), dma((chunks, 2, chips)), dma(()), dma((pairs,)),
        ],
        compiler_params=pltpu.CompilerParams(
            collective_id=0, has_side_effects=True, vmem_limit_bytes=VMEM_BYTES
        ),
        cost_estimate=pl.CostEstimate(
            flops=4 * pairs // 2 * rows * depth * cols,
            bytes_accessed=2 * depth * cols, transcendentals=0,
        ),
    )(live_counts, amplitudes.reshape(rows, virt_pairs), integrals)
    return out.reshape(occ_rows, occupied, cols)


def gathered(mesh, amplitudes, integrals, live_counts):
    occ_rows, occupied, virt_pairs = amplitudes.shape
    my_pairs, slab_cols = integrals.shape
    tile_size = VB
    slab_lanes = slab_cols // tile_size
    rows = occ_rows * occupied
    flat_rows = lax.all_to_all(
        amplitudes.reshape(rows, virt_pairs), "pair", split_axis=1, concat_axis=0, tiled=True
    )
    position = lax.axis_index("pair") * my_pairs + jnp.arange(my_pairs)
    keep_pairs = (
        (position // tile_size < live_counts[1]) & (position % tile_size < live_counts[1])
    ).astype(jnp.bfloat16)
    partial = jnp.dot(flat_rows * keep_pairs, integrals, preferred_element_type=jnp.float32)
    ladder = lax.psum_scatter(partial, "pair", scatter_dimension=0, tiled=True)
    blocks = ladder.reshape(occ_rows, occupied, slab_lanes, tile_size)
    mirrored = lax.all_to_all(
        lax.all_to_all(blocks, "grp", split_axis=3, concat_axis=2, tiled=True),
        "pair",
        split_axis=1,
        concat_axis=0,
        tiled=True,
    )
    summed = blocks + jnp.transpose(mirrored, (1, 0, 3, 2))
    first_virt = lax.axis_index("grp") * slab_lanes + jnp.arange(slab_lanes)
    second_virt = jnp.arange(tile_size)
    keep_out = (
        (first_virt[:, None] < live_counts[0]) & (second_virt[None, :] < live_counts[0])
    ).astype(jnp.float32)
    return (summed * keep_out).reshape(occ_rows, occupied, slab_cols).astype(jnp.bfloat16)


def on_device(mesh, amplitudes, integrals, live_counts):
    occ_rows, occupied, virt_pairs = amplitudes.shape
    depth, cols = integrals.shape
    rows, pairs = occ_rows * occupied, mesh.shape["pair"]
    held = 2 * depth * cols + rows * cols * (8 * pairs + 8) + 6 * rows * virt_pairs
    lanes = cols // VB
    packs = lanes % 8 == 0 and occ_rows * occ_rows <= 2 * (127 // lanes)
    fits = held < VMEM_BYTES and mesh.shape["grp"] == 4 and packs
    return (fused if fits else gathered)(mesh, amplitudes, integrals, live_counts)


def solution(mesh):
    return jax.shard_map(
        functools.partial(on_device, mesh),
        mesh=mesh,
        in_specs=(P("pair", None, None), P("pair", "grp"), P()),
        out_specs=P("pair", None, "grp"),
        check_vma=False,
    )
```

```python
import functools
import math

import jax
import jax.numpy as jnp
from jax import lax
from jax.experimental import pallas as pl
from jax.experimental.pallas import tpu as pltpu
from jax.sharding import PartitionSpec as P

VB = 96
STEPS = 32767.0
MESH = pl.DeviceIdType.MESH
VMEM_BYTES = 58 * 2**20


def quantize(value):
    peak = jnp.maximum(jnp.max(jnp.abs(value), axis=0, keepdims=True), 1e-33)
    whole = jnp.floor(value * (STEPS / peak) + 0.5).astype(jnp.int32)
    return whole.astype(jnp.int16), peak


def dequantize(quanta, peak):
    return quanta.astype(jnp.int32).astype(jnp.float32) * (peak * (1.0 / STEPS))


def kernel(
    sizes, live_ref, amp_ref, w_hbm, out_ref,
    w_ref, t_ref, tt_ref, mask_ref, part_ref, cross_ref, send_q, send_s,
    recv_q, recv_s, total_ref, final_ref, split_ref, piece_ref, mirrored_ref, mirror_ref,
    w_sem, t_send, t_fwd, t_recv, x_send, x_recv, q_send, s_send, q_recv, s_recv, m_send, m_recv,
):
    grps, pairs, occ_rows, occupied, depth, cols, vb = sizes
    chips = pairs // 2
    rows = occ_rows * occupied
    lanes = cols // vb
    chunks, slots = lanes // 8, 127 // lanes
    width = cols // chunks
    devices = grps * pairs
    g, p = lax.axis_index("grp"), lax.axis_index("pair")
    z, core = p // 2, p % 2
    sibling = 2 * z + 1 - core
    me = g * pairs + p

    w_copy = pltpu.make_async_copy(w_hbm, w_ref, w_sem)
    w_copy.start()
    barrier = pltpu.get_barrier_semaphore()

    to_grps = [lax.rem(g + n, grps) for n in range(grps)]
    to_pairs = [lax.rem(p + n, pairs) for n in range(pairs)]
    others = [(to_grps[n], to_pairs[m]) for m in range(pairs) for n in range(grps)][1:]
    for other in others:
        pl.semaphore_signal(barrier, inc=1, device_id=other, device_id_type=MESH)

    for c in range(depth // vb):
        alive = jnp.where(p * (depth // vb) + c < live_ref[1], live_ref[1], 0)
        lane = lax.broadcasted_iota(jnp.int32, (8, vb), 1)
        mask_ref[:, c * vb:(c + 1) * vb] = jnp.where(lane < alive, 1.0, 0.0)
    for chunk in range(chunks):
        final_ref[chunk, :, width:] = jnp.zeros((rows, 128), jnp.float32)
    pl.semaphore_wait(barrier, devices - 1)

    pieces_t = t_ref.shape[1]
    piece_cols = depth // pieces_t

    def amp_cols(pair, piece):
        return amp_ref.at[
            :, pl.ds(pl.multiple_of(pair * depth + piece * piece_cols, 128), piece_cols)
        ]

    def t_copy(src, slot, piece, send_sem, to_grp, to_pair):
        return pltpu.make_async_remote_copy(
            src_ref=src, dst_ref=t_ref.at[slot, piece], send_sem=send_sem,
            recv_sem=t_recv.at[slot, piece],
            device_id=(to_grp, to_pair), device_id_type=MESH,
        )

    def t_wait(slot, piece):
        t_copy(t_ref.at[slot, piece], slot, piece, t_send.at[0], g, sibling).wait_recv()

    def wait_sent(ref, send_sem):
        pltpu.make_async_remote_copy(
            src_ref=ref, dst_ref=ref, send_sem=send_sem, recv_sem=t_recv.at[0, 0],
            device_id=(g, sibling), device_id_type=MESH,
        ).wait_send()

    near_low = z < chips // 2

    def group_of(step):
        low = jnp.where(step < chips - 1 - z, chips - 1 - step, step - (chips - 1 - z))
        high = jnp.where(step < z, step, chips - 1 - (step - z))
        return jnp.where(step == chips - 1, z, jnp.where(near_low, low, high))

    grp_src, grp_dst = lax.rem(g, 2), g // 2
    sends_t = core == grp_src
    relays_t = core == grp_dst

    def own_copy(piece):
        return pltpu.make_async_copy(amp_cols(p, piece), t_ref.at[p, piece], t_recv.at[p, piece])

    @pl.when(sends_t)
    def _():
        @pl.loop(0, chips - 1)
        def _(step):
            to = 2 * group_of(step) + grp_dst
            for piece in range(pieces_t):
                t_copy(amp_cols(to, piece), p, piece, t_send.at[0], g, to).start()

    for piece in range(pieces_t):
        own_copy(piece).start()
        t_copy(amp_cols(sibling, piece), p, piece, t_send.at[1], g, sibling).start()

    def relay(step):
        @pl.when(relays_t)
        def _():
            slot = 2 * group_of(step) + grp_src
            for piece in range(pieces_t):
                t_wait(slot, piece)
                for hop in range(1, grps):
                    t_copy(
                        t_ref.at[slot, piece], slot, piece, t_fwd.at[hop - 1], to_grps[hop], p
                    ).start()

    def cross_copy(chunk, group):
        return pltpu.make_async_remote_copy(
            src_ref=part_ref.at[
                chunk, group, pl.ds(pl.multiple_of((1 - core) * rows, 8), rows)
            ],
            dst_ref=cross_ref.at[chunk, group], send_sem=x_send,
            recv_sem=x_recv.at[chunk, group], device_id=(g, sibling), device_id_type=MESH,
        )

    def chain_copies(chunk, step, group, side):
        to = 2 * (z + 1 - 2 * side) + core
        quanta = pltpu.make_async_remote_copy(
            src_ref=send_q.at[chunk, step], dst_ref=recv_q.at[chunk, side, group],
            send_sem=q_send, recv_sem=q_recv.at[chunk, side, group],
            device_id=(g, to), device_id_type=MESH,
        )
        scales = pltpu.make_async_remote_copy(
            src_ref=send_s.at[chunk, step], dst_ref=recv_s.at[chunk, side, group],
            send_sem=s_send, recv_sem=s_recv.at[chunk, side, group],
            device_id=(g, to), device_id_type=MESH,
        )
        return quanta, scales

    def arrived(chunk, group, side, acc):
        for copy in chain_copies(chunk, 0, group, side):
            copy.wait_recv()
        acc[:, :width] += dequantize(recv_q[chunk, side, group], recv_s[chunk, side, group])

    def own_sum(chunk, group, acc):
        cross_copy(chunk, group).wait_recv()
        mine = part_ref[chunk, group, pl.ds(pl.multiple_of(core * rows, 8), rows), :]
        acc[:, :width] = mine + cross_ref[chunk, group]

    def chain_step(chunk, step):
        group = group_of(step)
        own_sum(chunk, group, total_ref)
        side = jnp.where(group > z, 0, 1)
        first = jnp.where(side == 0, z == 0, z == chips - 1)

        @pl.when(jnp.logical_not(first))
        def _():
            arrived(chunk, group, side, total_ref)

        quanta, peak = quantize(total_ref[...])
        send_q[chunk, step] = quanta
        send_s[chunk, step] = peak
        for copy in chain_copies(chunk, step, group, side):
            copy.start()

    lag = jnp.where(jnp.logical_or(z == 0, z == chips - 1), 0, 1)
    log_step = math.log(2.0) / 256.0
    occ_pairs = [(i, j) for i in range(occ_rows) for j in range(occ_rows)]

    def mirror_copy(other):
        to_grp, to_pair = other
        return pltpu.make_async_remote_copy(
            src_ref=mirrored_ref.at[to_pair, to_grp], dst_ref=mirror_ref.at[me],
            send_sem=m_send, recv_sem=m_recv.at[p],
            device_id=(to_grp, to_pair), device_id_type=MESH,
        )

    def mirror_part(count, recv_sem):
        part = mirror_ref.at[pl.ds(0, count)]
        return pltpu.make_async_remote_copy(
            src_ref=part, dst_ref=part, send_sem=m_send, recv_sem=recv_sem,
            device_id=(g, sibling), device_id_type=MESH,
        )

    def finish_chunk(chunk):
        acc = final_ref.at[chunk]
        own_sum(chunk, z, acc)

        @pl.when(z > 0)
        def _():
            arrived(chunk, z, 0, acc)

        @pl.when(z < chips - 1)
        def _():
            arrived(chunk, z, 1, acc)

        for a in range(8):
            piece_ref[pl.ds(a, rows, stride=8), :] = final_ref[chunk, :, a * vb:a * vb + 128]

        @pl.loop(0, pairs, unroll=4)
        def _(q):
            lane = lax.broadcasted_iota(jnp.int32, (16, 128), 1)
            pieces = [
                piece_ref[
                    pl.ds(pl.multiple_of((i * occupied + q * occ_rows + j) * 8, 8), 8), :
                ]
                for i, j in occ_pairs
            ]
            for h in range(grps):
                ends = []
                for part in (pieces[:slots], pieces[slots:]):
                    packed = jnp.zeros((8, 128), jnp.float32)
                    for at, piece in enumerate(part):
                        shift = ((at - h) * lanes) % 128
                        moved = pltpu.roll(piece, shift, 1) if shift else piece
                        inside = jnp.logical_and(
                            lane[:8] >= at * lanes, lane[:8] < (at + 1) * lanes
                        )
                        packed = jnp.where(inside, moved, packed)
                    ends.append(packed)
                block = jnp.concatenate(ends, axis=0)
                peak = jnp.maximum(jnp.max(jnp.abs(block), axis=1, keepdims=True), 1e-33)
                level = jnp.floor(jnp.log(peak) * (1.0 / log_step)) + 2.0
                whole = jnp.floor(block * (STEPS * jnp.exp(level * -log_step)) + 0.5)
                whole = jnp.where(lane == 127, level, whole).astype(jnp.int32)
                mirrored_ref[q, h, 16 * chunk:16 * chunk + 16] = whole.astype(jnp.int16)

    def take_from(q, count):
        mirror_part(count, m_recv.at[q]).wait_recv()
        blocks = []
        for h in range(grps):
            for chunk in range(chunks):
                block = mirror_ref[h * pairs + q, 16 * chunk:16 * chunk + 16].astype(jnp.int32).astype(jnp.float32)
                blocks.append(block * (jnp.exp(block[:, 127:] * log_step) * (1.0 / STEPS)))
        rest = [jnp.zeros((128 - vb, 128), jnp.float32)]
        for end in range(2):
            turned = jnp.concatenate([b[8 * end:8 * end + 8] for b in blocks] + rest, axis=0).T
            for at, (i, j) in enumerate(occ_pairs[end * slots:(end + 1) * slots]):
                row = (j * occupied + q * occ_rows + i) * lanes
                split_ref[pl.ds(pl.multiple_of(row, 8), lanes), :] = (
                    turned[at * lanes:(at + 1) * lanes]
                )

    def mask_group(group):
        for piece in range(pieces_t):
            at = slice(piece * piece_cols, (piece + 1) * piece_cols)
            both = jnp.concatenate(
                [t_ref[2 * group + c, piece].astype(jnp.float32) for c in range(2)], axis=0
            )
            tt_ref[:, at] = (both * mask_ref[:1, at]).astype(jnp.bfloat16)

    def multiply(chunk, group):
        part_ref[chunk, group] = jnp.dot(
            tt_ref[...], w_ref[:, chunk * width:(chunk + 1) * width],
            preferred_element_type=jnp.float32,
        )
        cross_copy(chunk, group).start()

    w_copy.wait()
    for piece in range(pieces_t):
        own_copy(piece).wait()
        t_wait(sibling, piece)
    mask_group(z)
    multiply(0, z)
    relay(0)
    for chunk in range(1, chunks):
        multiply(chunk, z)

    @pl.loop(0, chips - 1)
    def _(step):
        group = group_of(step)

        @pl.when(step < chips - 2)
        def _():
            relay(step + 1)

        for c in range(2):
            @pl.when(jnp.logical_not(jnp.logical_and(relays_t, c == grp_src)))
            def _():
                for piece in range(pieces_t):
                    t_wait(2 * group + c, piece)

        turn = step - lag
        mask_group(group)
        for chunk in range(chunks):
            multiply(chunk, group)
            if chunk > 0:
                @pl.when(turn >= 0)
                def _():
                    chain_step(chunk - 1, turn)

        @pl.when(turn >= 0)
        def _():
            chain_step(chunks - 1, turn)

    @pl.when(lag == 1)
    def _():
        @pl.loop(0, chunks)
        def _(chunk):
            chain_step(chunk, chips - 2)

    for chunk in range(chunks):
        finish_chunk(chunk)

    for other in others:
        mirror_copy(other).start()
    mirror_ref[me] = mirrored_ref[p, g]
    take_from(p, grps - 1)

    @pl.loop(1, pairs)
    def _(step):
        take_from(lax.rem(p + pairs - step, pairs), grps)

    lane = lax.broadcasted_iota(jnp.int32, (rows, vb), 1)
    for chunk in range(chunks):
        for a in range(8):
            v = chunk * 8 + a
            alive = jnp.where(g * lanes + v < live_ref[0], live_ref[0], 0)
            both = (
                final_ref[chunk, :, a * vb:(a + 1) * vb]
                + split_ref[pl.ds(v, rows, stride=lanes), :][:, :vb]
            )
            total_ref[:, a * vb:(a + 1) * vb] = jnp.where(lane < alive, both, 0.0)
        out_ref[:, chunk * width:(chunk + 1) * width] = total_ref[...].astype(jnp.bfloat16)

    @pl.when(sends_t)
    def _():
        wait_sent(t_ref.at[pl.ds(0, chips - 1)], t_send.at[0])

    wait_sent(t_ref.at[0], t_send.at[1])

    @pl.when(relays_t)
    def _():
        for hop in range(1, grps):
            wait_sent(t_ref.at[pl.ds(0, chips - 1)], t_fwd.at[hop - 1])

    wait_sent(cross_ref, x_send)
    wait_sent(send_q, q_send)
    wait_sent(send_s, s_send)
    mirror_part(devices - 1, m_recv.at[0]).wait_send()


def fused(mesh, amplitudes, integrals, live_counts):
    occ_rows, occupied, virt_pairs = amplitudes.shape
    depth, cols = integrals.shape
    grps, pairs = mesh.shape["grp"], mesh.shape["pair"]
    rows, chips, devices = occ_rows * occupied, pairs // 2, grps * pairs
    lanes = cols // VB
    chunks = lanes // 8
    width = cols // chunks
    pieces = 1
    sizes = (grps, pairs, occ_rows, occupied, depth, cols, VB)
    f32, bf16, i16 = jnp.float32, jnp.bfloat16, jnp.int16
    dma = pltpu.SemaphoreType.DMA
    out = pl.pallas_call(
        functools.partial(kernel, sizes),
        out_shape=jax.ShapeDtypeStruct((rows, cols), bf16),
        in_specs=[
            pl.BlockSpec(memory_space=pltpu.SMEM),
            pl.BlockSpec(memory_space=pltpu.HBM),
            pl.BlockSpec(memory_space=pltpu.HBM),
        ],
        out_specs=pl.BlockSpec(memory_space=pltpu.VMEM),
        scratch_shapes=[
            pltpu.VMEM((depth, cols), bf16),
            pltpu.VMEM((pairs, pieces, rows, depth // pieces), bf16),
            pltpu.VMEM((2 * rows, depth), bf16),
            pltpu.VMEM((8, depth), f32),
            pltpu.VMEM((chunks, chips, 2 * rows, width), f32),
            pltpu.VMEM((chunks, chips, rows, width), f32),
            pltpu.VMEM((chunks, chips - 1, rows, width), i16),
            pltpu.VMEM((chunks, chips - 1, 1, width), f32),
            pltpu.VMEM((chunks, 2, chips, rows, width), i16),
            pltpu.VMEM((chunks, 2, chips, 1, width), f32),
            pltpu.VMEM((rows, width), f32),
            pltpu.VMEM((chunks, rows, width + 128), f32),
            pltpu.VMEM((rows * lanes, 128), f32),
            pltpu.VMEM((rows * 8, 128), f32),
            pltpu.VMEM((pairs, grps, 16 * chunks, 128), i16),
            pltpu.VMEM((devices, 16 * chunks, 128), i16),
            dma(()), dma((2,)), dma((grps - 1,)), dma((pairs, pieces)),
            dma(()), dma((chunks, chips)), dma(()), dma(()),
            dma((chunks, 2, chips)), dma((chunks, 2, chips)), dma(()), dma((pairs,)),
        ],
        compiler_params=pltpu.CompilerParams(
            collective_id=0, has_side_effects=True, vmem_limit_bytes=VMEM_BYTES
        ),
        cost_estimate=pl.CostEstimate(
            flops=4 * pairs // 2 * rows * depth * cols,
            bytes_accessed=2 * depth * cols, transcendentals=0,
        ),
    )(live_counts, amplitudes.reshape(rows, virt_pairs), integrals)
    return out.reshape(occ_rows, occupied, cols)


def gathered(mesh, amplitudes, integrals, live_counts):
    occ_rows, occupied, virt_pairs = amplitudes.shape
    my_pairs, slab_cols = integrals.shape
    tile_size = VB
    slab_lanes = slab_cols // tile_size
    rows = occ_rows * occupied
    flat_rows = lax.all_to_all(
        amplitudes.reshape(rows, virt_pairs), "pair", split_axis=1, concat_axis=0, tiled=True
    )
    position = lax.axis_index("pair") * my_pairs + jnp.arange(my_pairs)
    keep_pairs = (
        (position // tile_size < live_counts[1]) & (position % tile_size < live_counts[1])
    ).astype(jnp.bfloat16)
    partial = jnp.dot(flat_rows * keep_pairs, integrals, preferred_element_type=jnp.float32)
    ladder = lax.psum_scatter(partial, "pair", scatter_dimension=0, tiled=True)
    blocks = ladder.reshape(occ_rows, occupied, slab_lanes, tile_size)
    mirrored = lax.all_to_all(
        lax.all_to_all(blocks, "grp", split_axis=3, concat_axis=2, tiled=True),
        "pair",
        split_axis=1,
        concat_axis=0,
        tiled=True,
    )
    summed = blocks + jnp.transpose(mirrored, (1, 0, 3, 2))
    first_virt = lax.axis_index("grp") * slab_lanes + jnp.arange(slab_lanes)
    second_virt = jnp.arange(tile_size)
    keep_out = (
        (first_virt[:, None] < live_counts[0]) & (second_virt[None, :] < live_counts[0])
    ).astype(jnp.float32)
    return (summed * keep_out).reshape(occ_rows, occupied, slab_cols).astype(jnp.bfloat16)


def on_device(mesh, amplitudes, integrals, live_counts):
    occ_rows, occupied, virt_pairs = amplitudes.shape
    depth, cols = integrals.shape
    rows, pairs = occ_rows * occupied, mesh.shape["pair"]
    held = 2 * depth * cols + rows * cols * (8 * pairs + 8) + 6 * rows * virt_pairs
    lanes = cols // VB
    packs = lanes % 8 == 0 and occ_rows * occ_rows <= 2 * (127 // lanes)
    fits = held < VMEM_BYTES and mesh.shape["grp"] == 4 and packs
    return (fused if fits else gathered)(mesh, amplitudes, integrals, live_counts)


def solution(mesh):
    return jax.shard_map(
        functools.partial(on_device, mesh),
        mesh=mesh,
        in_specs=(P("pair", None, None), P("pair", "grp"), P()),
        out_specs=P("pair", None, "grp"),
        check_vma=False,
    )
```
